32 devices in a mesh: dp: 16 (over z, x, core), tensor: 2 (over y).
Axes of the slice: x: 2, y: 2, z: 4, core: 2. Of those that a mesh axis runs over, the one named last changes fastest.
Arguments:
- frames: float32 [32768, 1024], P(('dp', 'tensor')), may hold values from -6 to 6
- logit_grad: float32 [32768, 32], P(('dp', 'tensor')), may hold values from -6 to 6
- lengths: int32 [16, 10], P('dp'), may hold values from 0 to 1000, as said below
- ln_gain: bfloat16 [2, 2, 1024], replicated, may hold values from 0.5 to 1.5
- ln_bias: bfloat16 [2, 2, 1024], replicated, may hold values from -2 to 2
- w_qkv: bfloat16 [2, 3, 1024, 1024], P(None, None, None, 'tensor'), may hold values from -0.1875 to 0.1875
- b_qv: bfloat16 [2, 2, 1024], P(None, None, 'tensor'), may hold values from -3 to 3
- w_out: bfloat16 [2, 1024, 1024], P(None, 'tensor'), may hold values from -1.5 to 1.5
- b_out: bfloat16 [2, 1024], replicated, may hold values from -2 to 2
- w_up: bfloat16 [2, 1024, 4096], P(None, None, 'tensor'), may hold values from -0.1875 to 0.1875
- b_up: bfloat16 [2, 4096], P(None, 'tensor'), may hold values from -3 to 3
- w_down: bfloat16 [2, 4096, 1024], P(None, 'tensor'), may hold values from -0.125 to 0.125
- b_down: bfloat16 [2, 1024], replicated, may hold values from -2 to 2
- w_head: bfloat16 [1024, 32], P('tensor'), may hold values from -0.1875 to 0.1875
- b_head: bfloat16 [32], replicated, may hold values from -4 to 4
Outputs:
- logits: float32 [32768, 32], P(('dp', 'tensor'))
- input_grad: float32 [32768, 1024], P(('dp', 'tensor'))
- grad_ln_gain: float32 [2, 2, 1024], P(None, None, 'tensor')
- grad_ln_bias: float32 [2, 2, 1024], P(None, None, 'tensor')
- grad_w_qkv: float32 [2, 3, 1024, 1024], P(None, None, None, 'tensor')
- grad_b_qv: float32 [2, 2, 1024], P(None, None, 'tensor')
- grad_w_out: float32 [2, 1024, 1024], P(None, 'tensor')
- grad_b_out: float32 [2, 1024], P(None, 'tensor')
- grad_w_up: float32 [2, 1024, 4096], P(None, None, 'tensor')
- grad_b_up: float32 [2, 4096], P(None, 'tensor')
- grad_w_down: float32 [2, 4096, 1024], P(None, 'tensor')
- grad_b_down: float32 [2, 1024], P(None, 'tensor')
- grad_w_head: float32 [1024, 32], P('tensor')
- grad_b_head: float32 [32], P('tensor')
The draws below stay inside these ranges and needn't reach their ends.
Inputs may be any that keep to these rules, and one draw needn't show every extreme that they name: Row r lists the utterances of data index r in order, packed from slot 0; all lengths of a row lie in one of the buckets (up to 200, 400, 700 or 1000 of 2048 parts of 2048); unused slots are 0 and come last; a row sums to at most 2048, slots past the sum are padding.
All inputs are finite; a program needn't handle non-finite values.
Results may differ from the reference program's by a relative error of at most 0.02.
Values may be sent and summed in bfloat16 or wider, within the bound.
No kernel may reach another device: no remote copies, remote signals or barrier semaphores. Data moves between devices by JAX's collectives and lax.ppermute only.
A program may use at most 768 MiB of HBM per device.

```python
import jax
import jax.numpy as jnp
from jax import lax

D = 1024
HEADS = 16
HEAD_DIM = 64
FF = 4096
VOCAB = 32
LAYERS = 2
UTT = 10
TOK_DEV = 2048
TOKENS = 32768
N_DP = 16


def draw_lengths(key, part):
    key = jax.random.fold_in(key, 11)
    bucket_key, pick_key, length_key = jax.random.split(key, 3)
    tops = jnp.array([TOK_DEV * 200 // 2048, TOK_DEV * 400 // 2048, TOK_DEV * 700 // 2048, TOK_DEV * 1000 // 2048], jnp.int32)
    floors = jnp.array([TOK_DEV * 100 // 2048, TOK_DEV * 200 // 2048, TOK_DEV * 400 // 2048, TOK_DEV * 700 // 2048], jnp.int32) + 1
    bucket = jax.random.randint(bucket_key, (N_DP,), 0, 4)
    chosen = jax.random.randint(pick_key, (), 0, N_DP)
    bucket = jnp.where(jnp.arange(N_DP) == chosen, 3, bucket)
    upper = tops[bucket]
    lower = floors[bucket]
    number = jnp.minimum(UTT, TOK_DEV // upper)
    random_draw = jax.random.randint(length_key, (N_DP, UTT), 0, 1 << 20)
    length = lower[:, None] + random_draw % (upper - lower + 1)[:, None]
    slots = jnp.arange(UTT)[None, :]
    length = jnp.where(slots == 0, upper[:, None], length)
    return jnp.where(slots < number[:, None], length, 0).astype(jnp.int32)


def block_levels(own_key, extent, cuts, low, high):
    loudness = 1.0
    for position, blocks in cuts:
        steps = jax.random.uniform(jax.random.fold_in(jax.random.fold_in(own_key, 6), position), (blocks,), jnp.float32, low / len(cuts), high / len(cuts))
        loudness = loudness * jnp.repeat(jnp.exp(steps), extent[position] // blocks).reshape((-1,) + (1,) * (len(extent) - 1 - position))
    return loudness


def noise(own_key, dims, scale, reach, shards=(), kind=jnp.bfloat16):
    values = jax.random.normal(own_key, dims, jnp.float32) * scale
    if len(shards) > 0:
        values = block_levels(own_key, dims, shards, -0.22, 0.18) * values
    return jnp.clip(values, min=-reach, max=reach).astype(kind)


def setup_inputs(seed: int = 0) -> dict:
    key_list = jax.random.split(jax.random.key(seed), 16)
    frames = noise(key_list[0], (TOKENS, D), 1.0, 6.0, ((0, 32),), jnp.float32)
    logit_grad = noise(key_list[1], (TOKENS, VOCAB), 1.0, 6.0, ((0, 32),), jnp.float32)
    lengths = draw_lengths(jax.random.fold_in(key_list[15], 71), 0)
    ln_gain = jnp.clip(1.0 + 0.1 * jax.random.normal(key_list[3], (LAYERS, 2, D), jnp.float32), 0.5, 1.5).astype(jnp.bfloat16)
    ln_bias = noise(key_list[4], (LAYERS, 2, D), 0.3, 2.0)
    w_qkv = noise(key_list[5], (LAYERS, 3, D, D), D ** -0.5, 0.1875, ((3, 2),))
    b_qv = noise(key_list[6], (LAYERS, 2, D), 0.5, 3.0, ((2, 2),))
    w_out = noise(key_list[7], (LAYERS, D, D), (D // 64) ** -0.5, 1.5, ((1, 2),))
    b_out = noise(key_list[8], (LAYERS, D), 0.3, 2.0)
    w_up = noise(key_list[9], (LAYERS, D, FF), D ** -0.5, 0.1875, ((2, 2),))
    b_up = noise(key_list[10], (LAYERS, FF), 0.5, 3.0, ((1, 2),))
    w_down = noise(key_list[11], (LAYERS, FF, D), (FF // 2) ** -0.5, 0.125, ((1, 2),))
    b_down = noise(key_list[12], (LAYERS, D), 0.3, 2.0)
    w_head = noise(key_list[13], (D, VOCAB), D ** -0.5, 0.1875, ((0, 2),))
    b_head = noise(key_list[14], (VOCAB,), 1.0, 4.0)
    return {"frames": frames, "logit_grad": logit_grad, "lengths": lengths, "ln_gain": ln_gain, "ln_bias": ln_bias, "w_qkv": w_qkv, "b_qv": b_qv, "w_out": w_out, "b_out": b_out, "w_up": w_up, "b_up": b_up, "w_down": w_down, "b_down": b_down, "w_head": w_head, "b_head": b_head}


EPSILON = 1e-05
HIGHEST = lax.Precision.HIGHEST

@jax.custom_vjp
def low(v):
    return lax.optimization_barrier(v.astype(jnp.bfloat16)).astype(jnp.float32)

@jax.custom_vjp
def low_back(v):
    return v

def low_keep(v):
    return (low(v), None)

def low_pass(kept, grad):
    return (grad,)

def back_keep(v):
    return (v, None)

def back_low(kept, grad):
    return (low(grad),)
low.defvjp(low_keep, low_pass)
low_back.defvjp(back_keep, back_low)

def both_ways(values):
    return low_back(low(values))

def layer_norm(values, gain, shift):
    mean = lax.optimization_barrier(jnp.mean(values, axis=-1, keepdims=True))
    centred = values - mean
    spread = lax.optimization_barrier(jnp.mean(centred * centred, axis=-1, keepdims=True))
    return centred * lax.rsqrt(spread + EPSILON) * gain + shift

def product(left, right):
    return jnp.dot(left, right, precision=HIGHEST)

def attend_group(inputs):
    query, keys, values, segment = inputs
    query_heads = query.reshape(TOK_DEV, HEADS, HEAD_DIM)
    key_heads = keys.reshape(TOK_DEV, HEADS, HEAD_DIM)
    value_heads = values.reshape(TOK_DEV, HEADS, HEAD_DIM)
    scores = jnp.einsum('qhd,khd->hqk', query_heads, key_heads, precision=HIGHEST) * HEAD_DIM ** (-0.5)
    scores = low_back(scores)
    same = segment[:, None] == segment[None, :]
    scores = jnp.where(same[None], scores, -1e+30)
    maximum = lax.optimization_barrier(jnp.max(scores, axis=-1, keepdims=True))
    weights = jnp.exp(scores - maximum)
    shares = low(weights / lax.optimization_barrier(jnp.sum(weights, axis=-1, keepdims=True)))
    context = jnp.einsum('hqk,khd->qhd', shares, value_heads, precision=HIGHEST)
    return context.reshape(TOK_DEV, D)

def network(frames, ln_gain, ln_bias, w_qkv, b_qv, w_out, b_out, w_up, b_up, w_down, b_down, w_head, b_head, segment):
    stream = frames
    for layer in range(LAYERS):
        normed = low(layer_norm(stream, ln_gain[layer, 0], ln_bias[layer, 0]))
        query = both_ways(product(normed, w_qkv[layer, 0]) + b_qv[layer, 0])
        keys = both_ways(product(normed, w_qkv[layer, 1]))
        values = both_ways(product(normed, w_qkv[layer, 2]) + b_qv[layer, 1])
        context = lax.map(jax.checkpoint(attend_group), (query.reshape(N_DP, TOK_DEV, D), keys.reshape(N_DP, TOK_DEV, D), values.reshape(N_DP, TOK_DEV, D), segment))
        context = both_ways(context.reshape(TOKENS, D))
        middle = stream + low_back(product(context, w_out[layer]) + b_out[layer])
        normed = low(layer_norm(middle, ln_gain[layer, 1], ln_bias[layer, 1]))
        inner = low_back(product(normed, w_up[layer]) + b_up[layer])
        hidden = low(jax.nn.gelu(inner, approximate=False))
        stream = middle + low_back(product(hidden, w_down[layer]) + b_down[layer])
    return low_back(product(low(stream), w_head) + b_head)

def reference(frames, logit_grad, lengths, ln_gain, ln_bias, w_qkv, b_qv, w_out, b_out, w_up, b_up, w_down, b_down, w_head, b_head):
    params = tuple((item.astype(jnp.float32) for item in (ln_gain, ln_bias, w_qkv, b_qv, w_out, b_out, w_up, b_up, w_down, b_down, w_head, b_head)))
    positions = jnp.arange(TOK_DEV, dtype=jnp.int32)
    ends = jnp.cumsum(lengths, axis=1).astype(jnp.int32)
    segment = lax.optimization_barrier(jnp.sum((positions[None, :, None] >= ends[:, None, :]).astype(jnp.int32), axis=2)).astype(jnp.int32)
    valid = (positions[None, :] < ends[:, -1:]).reshape(TOKENS, 1)

    def closed(*values):
        return network(*values, segment)
    logits, back = jax.vjp(closed, frames.astype(jnp.float32), *params)
    grads = back(jnp.where(valid, logit_grad.astype(jnp.float32), jnp.zeros_like(logits)))
    return (logits, grads[0], grads[1], grads[2], grads[3], grads[4], grads[5], grads[6], grads[7], grads[8], grads[9], grads[10], grads[11], grads[12])
```

```python
import functools

import jax
import jax.numpy as jnp
from jax import lax
from jax.experimental import pallas as pl
from jax.experimental.pallas import tpu as pltpu
from jax.sharding import PartitionSpec as P

HEAD_DIM = 64
LAYERS = 2
EPSILON = 1e-05
PAIR = 2 * HEAD_DIM
NEGATIVE = -1e30
LOG2_E = 1.4426950408889634
LN_2 = 0.6931471805599453
MIB = 1 << 20
NT = (((1,), (1,)), ((), ()))
TN = (((0,), (0,)), ((), ()))


def layer_norm(values, gain, shift):
    mean = jnp.mean(values, axis=-1, keepdims=True)
    centred = values - mean
    spread = jnp.mean(centred * centred, axis=-1, keepdims=True)
    return centred * lax.rsqrt(spread + EPSILON) * gain + shift


def norm_backward(values, gain, shift, grad):
    unused, back = jax.vjp(layer_norm, values, gain, shift)
    return back(grad)


def matmul(left, right):
    return jnp.dot(left, right, preferred_element_type=jnp.float32)


def outer_cols(left, right):
    return lax.dot_general(left, right, NT, preferred_element_type=jnp.float32)


def inner_rows(left, right):
    return lax.dot_general(left, right, TN, preferred_element_type=jnp.float32)


def column_sums(values):
    return jnp.sum(values, axis=0, dtype=jnp.float32)


def tile(size, limit):
    return size if size <= limit else limit


def params(mib):
    return pltpu.CompilerParams(vmem_limit_bytes=mib * MIB)


def project_kernel(x_ref, w_ref, b_ref, *rest):
    out_ref = rest[-1]
    gain = jnp.where(pl.program_id(0) == 0, HEAD_DIM ** (-0.5) * LOG2_E, 1.0)
    value = jnp.dot(x_ref[...], w_ref[...], preferred_element_type=jnp.float32)
    out_ref[...] = ((value + b_ref[...]) * gain).astype(jnp.bfloat16)


def project(x, weight, bias, chunk, ways, joined):
    rows, depth = x.shape
    kinds, unused, width = weight.shape
    wide = tile(width, 512)
    in_specs = [
        pl.BlockSpec((rows, depth), lambda k, n: (0, 0)),
        pl.BlockSpec((None, depth, wide), lambda k, n: (k, 0, n)),
        pl.BlockSpec((None, 1, wide), lambda k, n: (k, 0, n)),
    ]
    args = [x, weight, bias]
    aliases = {}
    if joined is not None:
        in_specs.append(pl.BlockSpec(memory_space=pl.ANY))
        args.append(joined)
        aliases = {3: 0}
    return pl.pallas_call(
        project_kernel,
        grid=(kinds, width // wide),
        in_specs=in_specs,
        out_specs=pl.BlockSpec((None, rows, wide), lambda k, n: (k, chunk, n)),
        out_shape=jax.ShapeDtypeStruct((kinds, rows * ways, width), jnp.bfloat16),
        input_output_aliases=aliases,
        compiler_params=params(32),
        cost_estimate=pl.CostEstimate(
            flops=2 * rows * depth * kinds * width,
            bytes_accessed=2 * (rows * depth + kinds * width * (depth + rows)),
            transcendentals=0,
        ),
    )(*args)


ERF_STEP = 0.3275911
ERF_TERMS = (0.254829592, -0.284496736, 1.421413741, -1.453152027, 1.061405429)


def gelu_kernel(sub, x_ref, w_ref, b_ref, hidden_ref, slope_ref):
    for start in range(0, x_ref.shape[0], sub):
        rows = pl.ds(start, sub)
        u = (
            jnp.dot(x_ref[rows, :], w_ref[...], preferred_element_type=jnp.float32)
            + b_ref[...]
        )
        density = jnp.exp(u * u * -0.5)
        t = 1.0 / (1.0 + (ERF_STEP * 0.5**0.5) * jnp.abs(u))
        poly = ERF_TERMS[4]
        for term in ERF_TERMS[3::-1]:
            poly = poly * t + term
        tail = (0.5 * poly) * t * density
        phi = jnp.where(u < 0.0, tail, 1.0 - tail)
        hidden_ref[rows, :] = (u * phi).astype(jnp.bfloat16)
        slope_ref[rows, :] = (phi + u * density * 0.3989422804014327).astype(jnp.bfloat16)


def gelu_up(x, weight, bias):
    rows, depth = x.shape
    width = weight.shape[1]
    wide = tile(width, 512)
    out = jax.ShapeDtypeStruct((rows, width), jnp.bfloat16)
    return pl.pallas_call(
        functools.partial(gelu_kernel, tile(rows, 256)),
        grid=(width // wide,),
        in_specs=[
            pl.BlockSpec((rows, depth), lambda n: (0, 0)),
            pl.BlockSpec((depth, wide), lambda n: (0, n)),
            pl.BlockSpec((1, wide), lambda n: (0, n)),
        ],
        out_specs=[pl.BlockSpec((rows, wide), lambda n: (0, n))] * 2,
        out_shape=[out, out],
        compiler_params=params(32),
        cost_estimate=pl.CostEstimate(
            flops=2 * rows * depth * width + 40 * rows * width,
            bytes_accessed=2 * (rows * depth + depth * width + 2 * rows * width),
            transcendentals=2 * rows * width,
        ),
    )(x, weight, bias)


def weight_kernel(chunks, *refs):
    x_refs, d_refs = refs[:chunks], refs[chunks : 2 * chunks]
    out_ref, turned = refs[2 * chunks :]

    @pl.when((pl.program_id(1) == 0) & (pl.program_id(2) == 0))
    def _():
        for k in range(chunks):
            turned[k] = x_refs[k][...].T

    total = jnp.dot(turned[0], d_refs[0][...], preferred_element_type=jnp.float32)
    for k in range(1, chunks):
        total += jnp.dot(turned[k], d_refs[k][...], preferred_element_type=jnp.float32)
    out_ref[...] = total.astype(jnp.bfloat16)


def weight_grad(xs, ds):
    chunks = len(xs)
    rows, tall = xs[0][0].shape[-2:]
    width = ds[0][0].shape[-1]
    kinds = 1
    if None in ds[0][1]:
        kinds = ds[0][0].shape[ds[0][1].index(None)]
    high, wide = tile(tall, 512), tile(width, 512)

    def x_spec(lead):
        return pl.BlockSpec(
            (None,) * len(lead) + (rows, high), lambda m, g, n: lead + (0, m)
        )

    def d_spec(lead):
        return pl.BlockSpec(
            (None,) * len(lead) + (rows, wide),
            lambda m, g, n: tuple(g if at is None else at for at in lead) + (0, n),
        )

    out = pl.pallas_call(
        functools.partial(weight_kernel, chunks),
        grid=(tall // high, kinds, width // wide),
        in_specs=[x_spec(lead) for unused, lead in xs]
        + [d_spec(lead) for unused, lead in ds],
        out_specs=pl.BlockSpec((None, high, wide), lambda m, g, n: (g, m, n)),
        out_shape=jax.ShapeDtypeStruct((kinds, tall, width), jnp.bfloat16),
        scratch_shapes=[pltpu.VMEM((chunks, high, rows), jnp.bfloat16)],
        compiler_params=params(40),
        cost_estimate=pl.CostEstimate(
            flops=2 * rows * chunks * tall * kinds * width,
            bytes_accessed=2
            * (rows * chunks * (tall + kinds * width) + kinds * tall * width),
            transcendentals=0,
        ),
    )(*[array for array, unused in xs], *[array for array, unused in ds])
    return out


def head_lanes(shape):
    return lax.broadcasted_iota(jnp.int32, shape, 1) < HEAD_DIM


def split_heads(values):
    first = head_lanes(values.shape)
    zero = jnp.zeros_like(values)
    return jnp.where(first, values, zero), jnp.where(first, zero, values)


def attend_kernel(blocks, ranges, q_ref, k_ref, v_ref, col_ref, row_ref, ctx_ref, lse_ref):
    i = pl.program_id(1)
    size = q_ref.shape[0]
    shift = ranges[0]
    queries = split_heads(q_ref[...])
    own = col_ref[...]
    ones = jnp.ones((size, PAIR), jnp.bfloat16)

    def step(j, carry):
        place = lax.rem(j + blocks - shift, blocks)
        rows = pl.ds(pl.multiple_of(place * size, size), size)
        keys = k_ref[rows, :]
        values = jnp.concatenate([v_ref[rows, :], ones], axis=1)
        same = own == row_ref[place]
        out = []
        for h in range(2):
            top, total = carry[h]
            s = lax.dot_general(queries[h], keys, NT, preferred_element_type=jnp.float32)
            s = jnp.where(same, s, NEGATIVE)
            new = jnp.maximum(top, jnp.max(s, axis=1, keepdims=True))
            p = jnp.exp2(s - new)
            total = total * jnp.exp2(top - new) + jnp.dot(
                p.astype(jnp.bfloat16), values, preferred_element_type=jnp.float32
            )
            out.append((new, total))
        return tuple(out)

    start = (
        jnp.full((size, 1), NEGATIVE, jnp.float32),
        jnp.zeros((size, 2 * PAIR), jnp.float32),
    )
    done = lax.fori_loop(ranges[1 + 2 * i], ranges[2 + 2 * i], step, (start, start))
    parts = []
    for h in range(2):
        top, total = done[h]
        sums = total[:, PAIR:]
        parts.append(total[:, :PAIR] / sums)
        logs = top + jnp.log(sums) * LOG2_E
        lse_ref[h : h + 1, :] = logs.T[0:1, :]
    ctx_ref[...] = jnp.where(head_lanes(parts[0].shape), parts[0], parts[1]).astype(
        jnp.bfloat16
    )


def attend(joined, ranges, columns, rows_of, blocks):
    unused, total, width = joined.shape
    size = total // blocks
    pairs = width // PAIR
    grid_spec = pltpu.PrefetchScalarGridSpec(
        num_scalar_prefetch=1,
        grid=(pairs, blocks),
        in_specs=[
            pl.BlockSpec((None, size, PAIR), lambda p, i, r: (0, i, p)),
            pl.BlockSpec((None, total, PAIR), lambda p, i, r: (1, 0, p)),
            pl.BlockSpec((None, total, PAIR), lambda p, i, r: (2, 0, p)),
            pl.BlockSpec((size, 1), lambda p, i, r: (i, 0)),
            pl.BlockSpec((blocks, 1, size), lambda p, i, r: (0, 0, 0)),
        ],
        out_specs=[
            pl.BlockSpec((size, PAIR), lambda p, i, r: (i, p)),
            pl.BlockSpec((None, None, 2, size), lambda p, i, r: (p, i, 0, 0)),
        ],
    )
    return pl.pallas_call(
        functools.partial(attend_kernel, blocks),
        grid_spec=grid_spec,
        out_shape=[
            jax.ShapeDtypeStruct((total, width), jnp.bfloat16),
            jax.ShapeDtypeStruct((pairs, blocks, 2, size), jnp.float32),
        ],
        compiler_params=params(32),
        cost_estimate=pl.CostEstimate(
            flops=8 * total * total * width,
            bytes_accessed=8 * total * width,
            transcendentals=total * total * pairs,
        ),
    )(ranges, joined, joined, joined, columns, rows_of)


def attend_back_kernel(
    blocks,
    ranges,
    q_ref,
    k_ref,
    v_ref,
    g_ref,
    ctx_ref,
    lse_ref,
    col_ref,
    row_ref,
    out_ref,
    q_heads,
    g_heads,
    dq_ref,
    delta_ref,
):
    total = q_ref.shape[0]
    size = total // blocks
    chunks, unused, own_rows, unused = out_ref.shape
    shift = ranges[0]
    picks = (
        lax.broadcasted_iota(jnp.int32, (8, PAIR), 1) // HEAD_DIM
        == lax.broadcasted_iota(jnp.int32, (8, PAIR), 0)
    ).astype(jnp.float32)

    def prepare(i, unused):
        rows = pl.ds(pl.multiple_of(i * size, size), size)
        grad = g_ref[rows, :]
        product = grad.astype(jnp.float32) * ctx_ref[rows, :].astype(jnp.float32)
        delta_ref[i] = lax.dot_general(
            picks,
            product,
            NT,
            preferred_element_type=jnp.float32,
            precision=lax.Precision.HIGHEST,
        )
        for h, value in enumerate(split_heads(q_ref[rows, :])):
            q_heads[h, rows, :] = value
        for h, value in enumerate(split_heads(grad)):
            g_heads[h, rows, :] = value
        dq_ref[rows, :] = jnp.zeros((size, PAIR), jnp.float32)
        return unused

    lax.fori_loop(0, blocks, prepare, 0)

    def key_block(i, unused):
        rows = pl.ds(pl.multiple_of(i * size, size), size)
        keys = split_heads(k_ref[rows, :])
        values = split_heads(v_ref[rows, :])
        own = col_ref[rows, :]

        def step(j, carry):
            dk, dv = carry
            place = lax.rem(j + blocks - shift, blocks)
            there = pl.ds(pl.multiple_of(place * size, size), size)
            query = q_ref[there, :]
            grad = g_ref[there, :]
            same = own == row_ref[place]
            logs = lse_ref[place]
            delta = delta_ref[place]
            dq = dq_ref[there, :]
            for h in range(2):
                s = lax.dot_general(keys[h], query, NT, preferred_element_type=jnp.float32)
                s = jnp.where(same, s, NEGATIVE)
                p = jnp.exp2(s - logs[h : h + 1, :])
                dp = lax.dot_general(values[h], grad, NT, preferred_element_type=jnp.float32)
                ds = (p * (dp - delta[h : h + 1, :])).astype(jnp.bfloat16)
                dv += jnp.dot(
                    p.astype(jnp.bfloat16),
                    g_heads[h, there, :],
                    preferred_element_type=jnp.float32,
                )
                dk += jnp.dot(ds, q_heads[h, there, :], preferred_element_type=jnp.float32)
                dq += lax.dot_general(ds, keys[h], TN, preferred_element_type=jnp.float32)
            dq_ref[there, :] = dq
            return dk, dv

        zero = jnp.zeros((size, PAIR), jnp.float32)
        dk, dv = lax.fori_loop(ranges[1 + 2 * i], ranges[2 + 2 * i], step, (zero, zero))
        per_chunk = own_rows // size
        chunk = lax.div(i, per_chunk)
        spot = pl.ds(pl.multiple_of(lax.rem(i, per_chunk) * size, size), size)
        out_ref[chunk, 1, spot, :] = (dk * LN_2).astype(jnp.bfloat16)
        out_ref[chunk, 2, spot, :] = dv.astype(jnp.bfloat16)
        return unused

    lax.fori_loop(0, blocks, key_block, 0)
    for chunk in range(chunks):
        out_ref[chunk, 0] = (
            dq_ref[pl.ds(chunk * own_rows, own_rows), :] * HEAD_DIM ** (-0.5)
        ).astype(jnp.bfloat16)


def attend_back(joined, grad, context, lse, ranges, columns, rows_of, blocks, ways):
    unused, total, width = joined.shape
    size = total // blocks
    pairs = width // PAIR
    rows = total // ways
    whole = pl.BlockSpec((total, PAIR), lambda p, r: (0, p))
    grid_spec = pltpu.PrefetchScalarGridSpec(
        num_scalar_prefetch=1,
        grid=(pairs,),
        in_specs=[
            pl.BlockSpec((None, total, PAIR), lambda p, r: (0, 0, p)),
            pl.BlockSpec((None, total, PAIR), lambda p, r: (1, 0, p)),
            pl.BlockSpec((None, total, PAIR), lambda p, r: (2, 0, p)),
            whole,
            whole,
            pl.BlockSpec((None, blocks, 2, size), lambda p, r: (p, 0, 0, 0)),
            pl.BlockSpec((total, 1), lambda p, r: (0, 0)),
            pl.BlockSpec((blocks, 1, size), lambda p, r: (0, 0, 0)),
        ],
        out_specs=pl.BlockSpec((ways, 3, rows, PAIR), lambda p, r: (0, 0, 0, p)),
        scratch_shapes=[
            pltpu.VMEM((2, total, PAIR), jnp.bfloat16),
            pltpu.VMEM((2, total, PAIR), jnp.bfloat16),
            pltpu.VMEM((total, PAIR), jnp.float32),
            pltpu.VMEM((blocks, 8, size), jnp.float32),
        ],
    )
    return pl.pallas_call(
        functools.partial(attend_back_kernel, blocks),
        grid_spec=grid_spec,
        out_shape=jax.ShapeDtypeStruct((ways, 3, rows, width), jnp.bfloat16),
        compiler_params=params(48),
        cost_estimate=pl.CostEstimate(
            flops=20 * total * total * width,
            bytes_accessed=16 * total * width,
            transcendentals=total * total * pairs,
        ),
    )(ranges, joined, joined, joined, grad, context, lse, columns, rows_of)


class Layout:
    def __init__(self, dp, tensor):
        self.dp, self.tensor = dp, tensor
        self.paired = tensor == 2 and dp % 2 == 0
        self.ways = tensor

    def index(self):
        if self.paired:
            return lax.rem(lax.axis_index("dp"), 2)
        return lax.axis_index("tensor")

    def permute(self, values, target):
        pairs = []
        for place in range(self.dp * self.tensor):
            dp, tensor = divmod(place, self.tensor)
            pairs.append((place, target(dp, tensor)))
        return lax.ppermute(values, ("dp", "tensor"), pairs)

    def swap(self, values):
        if not self.paired:
            return values
        return self.permute(values, lambda dp, tensor: (dp // 2 * 2 + tensor) * 2 + dp % 2)

    def shift(self, values, step):
        if self.paired:
            return self.permute(values, lambda dp, tensor: (dp // 2 * 2 + (dp + step) % 2) * 2 + tensor)
        return self.permute(
            values, lambda dp, tensor: dp * self.tensor + (tensor + step) % self.tensor
        )

    def gather(self, values):
        return [values] + [self.shift(values, -step) for step in range(1, self.ways)]

    def scatter_sum(self, part):
        received = [
            self.shift(part(k).astype(jnp.bfloat16), k) for k in range(1, self.ways)
        ]
        total = part(0)
        for values in received:
            total = total + values.astype(jnp.float32)
        return total


def per_device(
    layout,
    frames,
    logit_grad,
    lengths,
    ln_gain,
    ln_bias,
    w_qkv,
    b_qv,
    w_out,
    b_out,
    w_up,
    b_up,
    w_down,
    b_down,
    w_head,
    b_head,
):
    ways = layout.ways
    rows, features = frames.shape
    total = rows * ways
    size = min(256, rows)
    blocks = total // size
    chunk_blocks = rows // size
    part = layout.index()
    swap = layout.swap

    stream = swap(frames.astype(jnp.bfloat16)).astype(jnp.float32)
    small = swap(jnp.concatenate([b_qv.reshape(-1), b_up.reshape(-1)]).reshape(-1, 128))
    lengths = swap(lengths)
    qkv_weights, out_weights, up_weights, down_weights = [], [], [], []
    for layer in range(LAYERS):
        qkv_weights.append(swap(w_qkv[layer]))
        out_weights.append(swap(w_out[layer]))
        up_weights.append(swap(w_up[layer]))
        down_weights.append(swap(w_down[layer]))
    logit_grad = swap(logit_grad.astype(jnp.bfloat16))
    small = small.reshape(-1).astype(jnp.float32)
    qv_biases = small[: b_qv.size].reshape(b_qv.shape)
    up_biases = small[b_qv.size :].reshape(b_up.shape)

    positions = lax.rem(jnp.arange(total, dtype=jnp.int32) + part * rows, total)
    ends = jnp.cumsum(lengths[0])
    segment = jnp.sum((positions[:, None] >= ends[None, :]).astype(jnp.int32), axis=1)
    own_valid = positions[:rows] < ends[-1]
    columns = segment[:, None]
    rows_of = segment.reshape(blocks, 1, size)
    firsts = positions.reshape(blocks, size)[:, :1]
    lows = jnp.max(jnp.where(ends[None, :] <= firsts, ends[None, :], 0), axis=1) // size
    lasts = firsts + (size - 1)
    highs = jnp.min(jnp.where(ends[None, :] > lasts, ends[None, :], total), axis=1)
    highs = (highs + size - 1) // size
    ranges = jnp.concatenate(
        [(part * chunk_blocks).reshape(1), jnp.stack([lows, highs], axis=1).reshape(-1)]
    ).astype(jnp.int32)
    gains = ln_gain.astype(jnp.float32)
    shifts = ln_bias.astype(jnp.float32)

    def chunk(values, k):
        return values[k * rows : (k + 1) * rows]

    saved = []
    for layer in range(LAYERS):
        normed = layer_norm(stream, gains[layer, 0], shifts[layer, 0]).astype(jnp.bfloat16)
        normed_all = layout.gather(normed)
        bias = jnp.stack(
            [qv_biases[layer, 0], jnp.zeros_like(qv_biases[layer, 0]), qv_biases[layer, 1]]
        )[:, None, :]
        joined = None
        for k in range(ways):
            joined = project(normed_all[k], qkv_weights[layer], bias, k, ways, joined)
        context, lse = attend(joined, ranges, columns, rows_of, blocks)
        attn_rows = layout.scatter_sum(
            lambda k: matmul(chunk(context, k), out_weights[layer])
        )
        middle = stream + attn_rows + b_out[layer].astype(jnp.float32)
        normed_ffn = layer_norm(middle, gains[layer, 1], shifts[layer, 1]).astype(jnp.bfloat16)
        ffn_all = layout.gather(normed_ffn)
        hidden, slopes = [], []
        for k in range(ways):
            one, other = gelu_up(ffn_all[k], up_weights[layer], up_biases[layer][None, :])
            hidden.append(one)
            slopes.append(other)
        ffn_rows = layout.scatter_sum(lambda k: matmul(hidden[k], down_weights[layer]))
        saved.append(
            (stream, middle, normed_all, joined, context, lse, ffn_all, hidden, slopes)
        )
        stream = middle + ffn_rows + b_down[layer].astype(jnp.float32)

    head_all = lax.all_gather(w_head, "tensor", axis=0, tiled=True)
    final_low = stream.astype(jnp.bfloat16)
    logits = swap((matmul(final_low, head_all) + b_head.astype(jnp.float32)))
    grad_logits = jnp.where(own_valid[:, None], logit_grad, 0.0).astype(jnp.bfloat16)
    head_grad = inner_rows(final_low, grad_logits)
    head_bias_grad = column_sums(grad_logits)
    grad_stream = outer_cols(grad_logits, head_all)

    def reduce(values):
        return lax.psum(swap(values), "dp")

    sums = {}
    weights = [None] * LAYERS
    for layer in reversed(range(LAYERS)):
        stream_in, middle, normed_all, joined, context, lse, ffn_all, hidden, slopes = saved[
            layer
        ]
        low = grad_stream.astype(jnp.bfloat16)
        sums["b_down", layer] = column_sums(low)
        low_all = layout.gather(low)
        inner = [
            (outer_cols(low_all[k], down_weights[layer]) * slopes[k].astype(jnp.float32)).astype(
                jnp.bfloat16
            )
            for k in range(ways)
        ]
        grad_normed = layout.scatter_sum(lambda k: outer_cols(inner[k], up_weights[layer]))
        grad_down = weight_grad(
            [(hidden[k], ()) for k in range(ways)], [(low_all[k], ()) for k in range(ways)]
        )[0]
        grad_up = weight_grad(
            [(ffn_all[k], ()) for k in range(ways)], [(inner[k], ()) for k in range(ways)]
        )[0]
        sums["b_up", layer] = sum(column_sums(values) for values in inner)
        grad_in, sums["gain", layer, 1], sums["shift", layer, 1] = norm_backward(
            middle, gains[layer, 1], shifts[layer, 1], grad_normed
        )
        grad_middle = grad_stream + grad_in
        low = grad_middle.astype(jnp.bfloat16)
        sums["b_out", layer] = column_sums(low)
        low_all = layout.gather(low)
        grad_context = jnp.concatenate(
            [outer_cols(low_all[k], out_weights[layer]).astype(jnp.bfloat16) for k in range(ways)]
        )
        grad_out = weight_grad(
            [(context.reshape(ways, rows, -1), (k,)) for k in range(ways)],
            [(low_all[k], ()) for k in range(ways)],
        )[0]
        grads = attend_back(
            joined, grad_context, context, lse, ranges, columns, rows_of, blocks, ways
        )
        grad_qkv = weight_grad(
            [(normed_all[k], ()) for k in range(ways)], [(grads, (k, None)) for k in range(ways)]
        )
        sums["b_qv", layer] = jnp.sum(grads, axis=(0, 2), dtype=jnp.float32)[::2]
        grad_normed = layout.scatter_sum(
            lambda k: jnp.einsum(
                "ktc,kdc->td", grads[k], qkv_weights[layer], preferred_element_type=jnp.float32
            )
        )
        grad_in, sums["gain", layer, 0], sums["shift", layer, 0] = norm_backward(
            stream_in, gains[layer, 0], shifts[layer, 0], grad_normed
        )
        grad_stream = grad_middle + grad_in
        weights[layer] = [reduce(values) for values in (grad_qkv, grad_out, grad_up, grad_down)]

    input_grad = swap(grad_stream.astype(jnp.bfloat16)).astype(jnp.float32)

    width = b_qv.shape[2] * ways
    inner_width = b_up.shape[1] * ways

    def spread(values):
        return lax.dynamic_update_slice_in_dim(
            jnp.zeros(values.shape[:-1] + (values.shape[-1] * ways,), jnp.float32),
            values,
            part * values.shape[-1],
            values.ndim - 1,
        )

    pieces = [
        jnp.stack([jnp.stack([sums[name, layer, n] for n in range(2)]) for layer in range(LAYERS)])
        for name in ("gain", "shift")
    ]
    pieces += [
        jnp.stack([sums[name, layer] for layer in range(LAYERS)]) for name in ("b_out", "b_down")
    ]
    pieces.append(spread(jnp.stack([sums["b_qv", layer] for layer in range(LAYERS)])))
    pieces.append(spread(jnp.stack([sums["b_up", layer] for layer in range(LAYERS)])))
    pieces.append(head_grad)
    pieces.append(head_bias_grad)
    packed = lax.psum(
        jnp.concatenate([piece.reshape(-1) for piece in pieces]), ("dp", "tensor")
    )
    mine = lax.axis_index("tensor")
    spots, at = [], 0
    for piece in pieces:
        spots.append(packed[at : at + piece.size].reshape(piece.shape))
        at += piece.size

    def share(values, axis):
        extent = values.shape[axis] // ways
        return lax.dynamic_slice_in_dim(values, mine * extent, extent, axis)

    gain, shift, bias_out, bias_down, bias_qv, bias_up = [
        share(values, values.ndim - 1) for values in spots[:6]
    ]
    head_weight, head_bias = share(spots[6], 0), share(spots[7], 0)
    grad_qkv, grad_out, grad_up, grad_down = [
        jnp.stack([weights[layer][n].astype(jnp.float32) for layer in range(LAYERS)])
        for n in range(4)
    ]
    return (
        logits,
        input_grad,
        gain,
        shift,
        grad_qkv,
        bias_qv,
        grad_out,
        bias_out,
        grad_up,
        bias_up,
        grad_down,
        bias_down,
        head_weight,
        head_bias,
    )


def solution(mesh):
    layout = Layout(mesh.shape["dp"], mesh.shape["tensor"])
    by_rows = P(("dp", "tensor"), None)
    placed = (
        by_rows,
        by_rows,
        P("dp", None),
        P(),
        P(),
        P(None, None, None, "tensor"),
        P(None, None, "tensor"),
        P(None, "tensor", None),
        P(),
        P(None, None, "tensor"),
        P(None, "tensor"),
        P(None, "tensor", None),
        P(),
        P("tensor", None),
        P(),
    )
    return jax.shard_map(
        functools.partial(per_device, layout),
        mesh=mesh,
        in_specs=placed,
        out_specs=(
            by_rows,
            by_rows,
            P(None, None, "tensor"),
            P(None, None, "tensor"),
            P(None, None, None, "tensor"),
            P(None, None, "tensor"),
            P(None, "tensor", None),
            P(None, "tensor"),
            P(None, None, "tensor"),
            P(None, "tensor"),
            P(None, "tensor", None),
            P(None, "tensor"),
            P("tensor", None),
            P("tensor"),
        ),
        check_vma=False,
    )
```

```python
import functools

import jax
import jax.numpy as jnp
from jax import lax
from jax.experimental import pallas as pl
from jax.experimental.pallas import tpu as pltpu
from jax.sharding import PartitionSpec as P

HEAD_DIM = 64
LAYERS = 2
EPSILON = 1e-05
PAIR = 2 * HEAD_DIM
NEGATIVE = -1e30
SUM_ROWS = 16
SMALL_ROWS = 128
LOG2_E = 1.4426950408889634
LN_2 = 0.6931471805599453
MIB = 1 << 20
NN = (((1,), (0,)), ((), ()))
NT = (((1,), (1,)), ((), ()))
TN = (((0,), (0,)), ((), ()))


def layer_norm(values, gain, shift):
    mean = jnp.mean(values, axis=-1, keepdims=True)
    centred = values - mean
    spread = jnp.mean(centred * centred, axis=-1, keepdims=True)
    return centred * lax.rsqrt(spread + EPSILON) * gain + shift


def matmul(left, right):
    return jnp.dot(left, right, preferred_element_type=jnp.float32)


def outer_cols(left, right):
    return lax.dot_general(left, right, NT, preferred_element_type=jnp.float32)


def inner_rows(left, right):
    return lax.dot_general(left, right, TN, preferred_element_type=jnp.float32)


def column_sums(values):
    return jnp.sum(values, axis=0, dtype=jnp.float32)


def tile(size, limit):
    return size if size <= limit else limit


LIGHT = pl.CostEstimate(flops=0, bytes_accessed=0, transcendentals=0)


def after(kernel, first, tokens):
    return lambda *refs: kernel(*refs[:first], *refs[first + len(tokens) :])


def params(mib):
    return pltpu.CompilerParams(vmem_limit_bytes=mib * MIB)


def project_kernel(x_ref, w_ref, b_ref, *rest):
    out_ref = rest[-1]
    gain = jnp.where(pl.program_id(0) == 0, HEAD_DIM ** (-0.5) * LOG2_E, 1.0)
    value = jnp.dot(x_ref[...], w_ref[...], preferred_element_type=jnp.float32)
    out_ref[...] = ((value + b_ref[...]) * gain).astype(jnp.bfloat16)


def project(x, weight, bias, chunk, ways, joined):
    rows, depth = x.shape
    kinds, unused, width = weight.shape
    wide = tile(width, 512)
    in_specs = [
        pl.BlockSpec((rows, depth), lambda k, n: (0, 0)),
        pl.BlockSpec((None, depth, wide), lambda k, n: (k, 0, n)),
        pl.BlockSpec((None, 1, wide), lambda k, n: (k, 0, n)),
    ]
    args = [x, weight, bias]
    aliases = {}
    if joined is not None:
        in_specs.append(pl.BlockSpec(memory_space=pl.ANY))
        args.append(joined)
        aliases = {3: 0}
    return pl.pallas_call(
        project_kernel,
        grid=(kinds, width // wide),
        in_specs=in_specs,
        out_specs=pl.BlockSpec((None, rows, wide), lambda k, n: (k, chunk, n)),
        out_shape=jax.ShapeDtypeStruct((kinds, rows * ways, width), jnp.bfloat16),
        input_output_aliases=aliases,
        compiler_params=params(32),
        cost_estimate=LIGHT,
    )(*args)


ERF_STEP = 0.3275911
ERF_TERMS = (0.254829592, -0.284496736, 1.421413741, -1.453152027, 1.061405429)


def gelu_kernel(sub, x_ref, w_ref, b_ref, hidden_ref, slope_ref):
    for start in range(0, x_ref.shape[0], sub):
        rows = pl.ds(start, sub)
        u = (
            jnp.dot(x_ref[rows, :], w_ref[...], preferred_element_type=jnp.float32)
            + b_ref[...]
        )
        density = jnp.exp(u * u * -0.5)
        t = 1.0 / (1.0 + (ERF_STEP * 0.5**0.5) * jnp.abs(u))
        poly = ERF_TERMS[4]
        for term in ERF_TERMS[3::-1]:
            poly = poly * t + term
        tail = (0.5 * poly) * t * density
        phi = jnp.where(u < 0.0, tail, 1.0 - tail)
        hidden_ref[rows, :] = (u * phi).astype(jnp.bfloat16)
        slope_ref[rows, :] = (phi + u * density * 0.3989422804014327).astype(jnp.bfloat16)


def gelu_up(x, weight, bias):
    rows, depth = x.shape
    width = weight.shape[1]
    wide = tile(width, 512)
    out = jax.ShapeDtypeStruct((rows, width), jnp.bfloat16)
    return pl.pallas_call(
        functools.partial(gelu_kernel, tile(rows, 256)),
        grid=(width // wide,),
        in_specs=[
            pl.BlockSpec((rows, depth), lambda n: (0, 0)),
            pl.BlockSpec((depth, wide), lambda n: (0, n)),
            pl.BlockSpec((1, wide), lambda n: (0, n)),
        ],
        out_specs=[pl.BlockSpec((rows, wide), lambda n: (0, n))] * 2,
        out_shape=[out, out],
        compiler_params=params(32),
        cost_estimate=LIGHT,
    )(x, weight, bias)


def times_kernel(dims, x_ref, w_ref, *rest):
    rest[-1][...] = lax.dot_general(
        x_ref[...], w_ref[...], dims, preferred_element_type=jnp.float32
    ).astype(jnp.bfloat16)


def row_spec(array, lead, high):
    return pl.BlockSpec(
        (None,) * len(lead) + (high, array.shape[-1]), lambda m: lead + (m, 0)
    )


def whole_spec(array):
    return pl.BlockSpec(array.shape, lambda m: (0,) * array.ndim)


def times(x, lead, weight, dims, chunk=0, chunks=1, buffer=None, tokens=()):
    rows = x.shape[-2]
    width = weight.shape[0] if dims == NT else weight.shape[1]
    high = tile(rows, 256)
    in_specs = [row_spec(x, lead, high), whole_spec(weight)]
    args = [x, weight]
    aliases = {}
    if buffer is not None:
        aliases = {2: 0}
        in_specs.append(pl.BlockSpec(memory_space=pl.ANY))
        args.append(buffer)
    in_specs += [pl.BlockSpec(memory_space=pl.ANY)] * len(tokens)
    args += tokens
    return pl.pallas_call(
        functools.partial(times_kernel, dims),
        grid=(rows // high,),
        in_specs=in_specs,
        out_specs=pl.BlockSpec((high, width), lambda m: (chunk * (rows // high) + m, 0)),
        out_shape=jax.ShapeDtypeStruct((rows * chunks, width), jnp.bfloat16),
        input_output_aliases=aliases,
        compiler_params=params(40),
        cost_estimate=LIGHT,
    )(*args)


def join_kernel(count, last, x_ref, w_ref, res_ref, bias_ref, gain_ref, shift_ref, *rest):
    received, outs = rest[:count], rest[count:]
    value = jnp.dot(x_ref[...], w_ref[...], preferred_element_type=jnp.float32)
    for ref in received:
        value += ref[...].astype(jnp.float32)
    value += res_ref[...] + bias_ref[...]
    if last:
        outs[0][...] = value.astype(jnp.bfloat16)
    else:
        outs[0][...] = value
        outs[1][...] = layer_norm(value, gain_ref[...], shift_ref[...]).astype(jnp.bfloat16)


def join(x, lead, weight, residual, bias, gain, shift, received, last=False):
    rows, features = residual.shape
    high = tile(rows, 256)
    block = pl.BlockSpec((high, features), lambda m: (m, 0))
    vector = pl.BlockSpec((1, features), lambda m: (0, 0))
    low = jax.ShapeDtypeStruct(residual.shape, jnp.bfloat16)
    full = jax.ShapeDtypeStruct(residual.shape, jnp.float32)
    return pl.pallas_call(
        functools.partial(join_kernel, len(received), last),
        grid=(rows // high,),
        in_specs=[row_spec(x, lead, high), whole_spec(weight), block, vector, vector, vector]
        + [block] * len(received),
        out_specs=[block] if last else [block, block],
        out_shape=[low] if last else [full, low],
        compiler_params=params(40),
        cost_estimate=LIGHT,
    )(x, weight, residual, bias[None], gain[None], shift[None], *received)


def inner_kernel(sub, d_ref, w_ref, slope_ref, out_ref, sums_ref):
    sums = jnp.zeros(sums_ref.shape, jnp.float32)
    for start in range(0, d_ref.shape[0], sub):
        rows = pl.ds(start, sub)
        value = lax.dot_general(
            d_ref[rows, :], w_ref[...], NT, preferred_element_type=jnp.float32
        )
        value = (value * slope_ref[rows, :].astype(jnp.float32)).astype(jnp.bfloat16)
        out_ref[rows, :] = value
        sums += jnp.sum(value.astype(jnp.float32), axis=0, keepdims=True)
    sums_ref[...] = sums


def inner_grad(d, weight, slope):
    rows, features = d.shape
    width = weight.shape[0]
    wide = tile(width, 512)
    column = pl.BlockSpec((rows, wide), lambda n: (0, n))
    return pl.pallas_call(
        functools.partial(inner_kernel, tile(rows, 256)),
        grid=(width // wide,),
        in_specs=[
            pl.BlockSpec((rows, features), lambda n: (0, 0)),
            pl.BlockSpec((wide, features), lambda n: (n, 0)),
            column,
        ],
        out_specs=[column, pl.BlockSpec((1, wide), lambda n: (0, n))],
        out_shape=[
            jax.ShapeDtypeStruct((rows, width), jnp.bfloat16),
            jax.ShapeDtypeStruct((1, width), jnp.float32),
        ],
        compiler_params=params(40),
        cost_estimate=LIGHT,
    )(d, weight, slope)


def back_kernel(kinds, count, *refs):
    xs, ws = refs[:kinds], refs[kinds]
    value_ref, grad_ref, gain_ref = refs[kinds + 1 : kinds + 4]
    received = refs[kinds + 4 : kinds + 4 + count]
    full_ref, low_ref, sums_ref = refs[kinds + 4 + count :]
    if kinds == 1:
        weights = [ws[...]]
    else:
        weights = [ws[k] for k in range(kinds)]
    given = lax.dot_general(xs[0][...], weights[0], NT, preferred_element_type=jnp.float32)
    for k in range(1, kinds):
        given += lax.dot_general(xs[k][...], weights[k], NT, preferred_element_type=jnp.float32)
    for ref in received:
        given += ref[...].astype(jnp.float32)
    values = value_ref[...]
    centred = values - jnp.mean(values, axis=-1, keepdims=True)
    scale = lax.rsqrt(jnp.mean(centred * centred, axis=-1, keepdims=True) + EPSILON)
    unit = centred * scale
    inward = given * gain_ref[...]
    mean = jnp.mean(inward, axis=-1, keepdims=True)
    along = jnp.mean(inward * unit, axis=-1, keepdims=True)
    full = grad_ref[...] + scale * (inward - mean - unit * along)
    low = full.astype(jnp.bfloat16)
    full_ref[...] = full
    low_ref[...] = low

    @pl.when(pl.program_id(0) == 0)
    def _():
        sums_ref[...] = jnp.zeros(sums_ref.shape, jnp.float32)

    sums_ref[0:1, :] += jnp.sum(given * unit, axis=0, keepdims=True)
    sums_ref[1:2, :] += jnp.sum(given, axis=0, keepdims=True)
    sums_ref[2:3, :] += jnp.sum(low.astype(jnp.float32), axis=0, keepdims=True)


def norm_back(xs, weight, values, grad, gain, received):
    rows, features = values.shape
    high = tile(rows, 256)
    block = pl.BlockSpec((high, features), lambda m: (m, 0))
    return pl.pallas_call(
        functools.partial(back_kernel, len(xs), len(received)),
        grid=(rows // high,),
        in_specs=[row_spec(x, lead, high) for x, lead in xs]
        + [whole_spec(weight), block, block, pl.BlockSpec((1, features), lambda m: (0, 0))]
        + [block] * len(received),
        out_specs=[block, block, pl.BlockSpec((8, features), lambda m: (0, 0))],
        out_shape=[
            jax.ShapeDtypeStruct(values.shape, jnp.float32),
            jax.ShapeDtypeStruct(values.shape, jnp.bfloat16),
            jax.ShapeDtypeStruct((8, features), jnp.float32),
        ],
        compiler_params=params(48),
        cost_estimate=LIGHT,
    )(*[x for x, unused in xs], weight, values, grad, gain[None], *received)


def weight_kernel(chunks, *refs):
    x_refs, d_refs = refs[:chunks], refs[chunks : 2 * chunks]
    out_ref, turned = refs[-2:]

    @pl.when((pl.program_id(1) == 0) & (pl.program_id(2) == 0))
    def _():
        for k in range(chunks):
            turned[k] = x_refs[k][...].T

    total = jnp.dot(turned[0], d_refs[0][...], preferred_element_type=jnp.float32)
    for k in range(1, chunks):
        total += jnp.dot(turned[k], d_refs[k][...], preferred_element_type=jnp.float32)
    out_ref[...] = total.astype(jnp.bfloat16)


def weight_grad(xs, ds, buffer, shape, place, tokens=()):
    chunks = len(xs)
    rows, tall = xs[0][0].shape[-2:]
    width = ds[0][0].shape[-1]
    kinds = 1
    if None in ds[0][1]:
        kinds = ds[0][0].shape[ds[0][1].index(None)]
    high, wide = tile(tall, 512), shape[2]

    def x_spec(lead):
        return pl.BlockSpec(
            (None,) * len(lead) + (rows, high), lambda m, g, n: lead + (0, m)
        )

    def d_spec(lead):
        return pl.BlockSpec(
            (None,) * len(lead) + (rows, wide),
            lambda m, g, n: tuple(g if at is None else at for at in lead) + (0, n),
        )

    def out_index(m, g, n):
        half, row = place(g, n)
        return half, row // high + m, 0

    in_specs = [x_spec(lead) for unused, lead in xs] + [d_spec(lead) for unused, lead in ds]
    args = [array for array, unused in xs] + [array for array, unused in ds]
    aliases = {}
    if buffer is not None:
        aliases = {len(args): 0}
        in_specs.append(pl.BlockSpec(memory_space=pl.ANY))
        args.append(buffer)
    in_specs += [pl.BlockSpec(memory_space=pl.ANY)] * len(tokens)
    args += tokens
    return pl.pallas_call(
        functools.partial(weight_kernel, chunks),
        grid=(tall // high, kinds, width // wide),
        in_specs=in_specs,
        out_specs=pl.BlockSpec((None, high, wide), out_index),
        out_shape=jax.ShapeDtypeStruct(shape, jnp.bfloat16),
        scratch_shapes=[pltpu.VMEM((chunks, high, rows), jnp.bfloat16)],
        input_output_aliases=aliases,
        compiler_params=params(40),
        cost_estimate=LIGHT,
    )(*args)


def choose_kernel(flag, own_ref, other_ref, out_ref):
    out_ref[...] = jnp.where(flag[0] == 0, own_ref[...], other_ref[...])


def choose(own, first, other, flag, tokens=()):
    tall, width = other.shape
    high = tile(tall, 512)

    def spec(which, skip):
        return pl.BlockSpec(
            (high, width), lambda m, f: (jnp.where(f[0] == which, skip + m, 0), 0)
        )

    return pl.pallas_call(
        after(choose_kernel, 3, tokens),
        grid_spec=pltpu.PrefetchScalarGridSpec(
            num_scalar_prefetch=1,
            grid=(tall // high,),
            in_specs=[spec(0, first // high), spec(1, 0)]
            + [pl.BlockSpec(memory_space=pl.ANY)] * len(tokens),
            out_specs=pl.BlockSpec((high, width), lambda m, f: (m, 0)),
        ),
        out_shape=jax.ShapeDtypeStruct(other.shape, other.dtype),
        compiler_params=params(32),
        cost_estimate=LIGHT,
    )(flag, own, other, *tokens)


def unpack_kernel(flag, one_ref, two_ref, *rest):
    rest[-1][...] = jnp.where(flag[0] == 0, one_ref[...], two_ref[...]).astype(jnp.float32)


def unpack(one, two, flag, first, tall, tiles, layer, output, out_rows, out_first):
    wide = one.shape[1]
    high = tile(tall, 1024)
    skip = first // high

    def spec(which):
        def index(m, n, f):
            here = jnp.where(f[0] == which, 1, 0)
            return here * (skip + n * (tall // high) + m), 0

        return pl.BlockSpec((high, wide), index)

    args = [flag, one, two]
    in_specs = [spec(0), spec(1)]
    aliases = {}
    if output is not None:
        aliases = {3: 0}
        in_specs.append(pl.BlockSpec(memory_space=pl.ANY))
        args.append(output)
    return pl.pallas_call(
        unpack_kernel,
        grid_spec=pltpu.PrefetchScalarGridSpec(
            num_scalar_prefetch=1,
            grid=(tall // high, tiles),
            in_specs=in_specs,
            out_specs=pl.BlockSpec(
                (None, high, wide), lambda m, n, f: (layer, out_first // high + m, n)
            ),
        ),
        out_shape=jax.ShapeDtypeStruct((LAYERS, out_rows, tiles * wide), jnp.float32),
        input_output_aliases=aliases,
        compiler_params=params(32),
        cost_estimate=LIGHT,
    )(*args)


def head_lanes(shape):
    return lax.broadcasted_iota(jnp.int32, shape, 1) < HEAD_DIM


def split_heads(values):
    first = head_lanes(values.shape)
    zero = jnp.zeros_like(values)
    return jnp.where(first, values, zero), jnp.where(first, zero, values)


def attend_kernel(
    blocks, ranges, q_ref, k_ref, v_ref, col_ref, row_ref, ctx_ref, lse_ref, turned, tops, totals
):
    i = pl.program_id(0)
    size, width = q_ref.shape
    heads = width // HEAD_DIM
    pairs = width // PAIR
    groups, group_heads, unused = lse_ref.shape
    shift = ranges[0]

    @pl.when(i == 0)
    def _():
        def turn(place, unused):
            rows = pl.ds(pl.multiple_of(place * size, size), size)
            for p in range(pairs):
                flipped = v_ref[rows, p * PAIR : (p + 1) * PAIR].T
                for h in range(2):
                    turned[place, 2 * p + h, :HEAD_DIM, :] = flipped[
                        h * HEAD_DIM : (h + 1) * HEAD_DIM
                    ]
                    turned[place, 2 * p + h, HEAD_DIM:, :] = jnp.ones(
                        (SUM_ROWS, size), jnp.bfloat16
                    )
            return unused

        lax.fori_loop(0, blocks, turn, 0)

    own = row_ref[i]
    for h in range(heads):
        tops[h] = jnp.full((1, size), NEGATIVE, jnp.float32)
        totals[h] = jnp.zeros((HEAD_DIM + SUM_ROWS, size), jnp.float32)

    def step(j, unused):
        place = lax.rem(j + blocks - shift, blocks)
        rows = pl.ds(pl.multiple_of(place * size, size), size)
        same = col_ref[rows, :] == own
        for p in range(pairs):
            lanes = slice(p * PAIR, (p + 1) * PAIR)
            keys = k_ref[rows, lanes]
            queries = split_heads(q_ref[:, lanes])
            for h in range(2):
                at = 2 * p + h
                s = lax.dot_general(keys, queries[h], NT, preferred_element_type=jnp.float32)
                s = jnp.where(same, s, NEGATIVE)
                top = tops[at]
                new = jnp.maximum(top, jnp.max(s, axis=0, keepdims=True))
                weights = jnp.exp2(s - new)
                tops[at] = new
                totals[at] = totals[at] * jnp.exp2(top - new) + jnp.dot(
                    turned[place, at],
                    weights.astype(jnp.bfloat16),
                    preferred_element_type=jnp.float32,
                )
        return unused

    lax.fori_loop(ranges[1 + 2 * i], ranges[2 + 2 * i], step, 0)
    for p in range(pairs):
        parts = []
        for h in (2 * p, 2 * p + 1):
            total = totals[h]
            sums = total[HEAD_DIM : HEAD_DIM + 1, :]
            parts.append(total[:HEAD_DIM, :] / sums)
            group, row = divmod(h, group_heads)
            lse_ref[group, row : row + 1, :] = tops[h] + jnp.log(sums) * LOG2_E
        ctx_ref[:, p * PAIR : (p + 1) * PAIR] = (
            jnp.concatenate(parts, axis=0).T.astype(jnp.bfloat16)
        )


def group_width(width):
    return tile(width, 2 * PAIR)


def attend(joined, ranges, columns, rows_of, blocks, tokens=()):
    unused, total, width = joined.shape
    size = total // blocks
    heads = width // HEAD_DIM
    group_heads = group_width(width) // HEAD_DIM
    groups = heads // group_heads
    grid_spec = pltpu.PrefetchScalarGridSpec(
        num_scalar_prefetch=1,
        grid=(blocks,),
        in_specs=[
            pl.BlockSpec((None, size, width), lambda i, r: (0, i, 0)),
            pl.BlockSpec((None, total, width), lambda i, r: (1, 0, 0)),
            pl.BlockSpec((None, total, width), lambda i, r: (2, 0, 0)),
            pl.BlockSpec((total, 1), lambda i, r: (0, 0)),
            pl.BlockSpec((blocks, 1, size), lambda i, r: (0, 0, 0)),
        ]
        + [pl.BlockSpec(memory_space=pl.ANY)] * len(tokens),
        out_specs=[
            pl.BlockSpec((size, width), lambda i, r: (i, 0)),
            pl.BlockSpec((groups, None, group_heads, size), lambda i, r: (0, i, 0, 0)),
        ],
        scratch_shapes=[
            pltpu.VMEM((blocks, heads, HEAD_DIM + SUM_ROWS, size), jnp.bfloat16),
            pltpu.VMEM((heads, 1, size), jnp.float32),
            pltpu.VMEM((heads, HEAD_DIM + SUM_ROWS, size), jnp.float32),
        ],
    )
    return pl.pallas_call(
        after(functools.partial(attend_kernel, blocks), 6, tokens),
        grid_spec=grid_spec,
        out_shape=[
            jax.ShapeDtypeStruct((total, width), jnp.bfloat16),
            jax.ShapeDtypeStruct((groups, blocks, group_heads, size), jnp.float32),
        ],
        compiler_params=params(40),
        cost_estimate=LIGHT,
    )(ranges, joined, joined, joined, columns, rows_of, *tokens)


def attend_back_kernel(
    blocks,
    ranges,
    q_ref,
    k_ref,
    v_ref,
    g_ref,
    ctx_ref,
    lse_ref,
    col_ref,
    row_ref,
    out_ref,
    dq_ref,
    dk_ref,
    dv_ref,
    delta_ref,
):
    total, width = q_ref.shape
    size = total // blocks
    pairs = width // PAIR
    chunks, unused, own_rows, unused = out_ref.shape
    shift = ranges[0]
    picks = (
        lax.broadcasted_iota(jnp.int32, (8, width), 1) // HEAD_DIM
        == lax.broadcasted_iota(jnp.int32, (8, width), 0)
    ).astype(jnp.float32)

    def prepare(i, unused):
        rows = pl.ds(pl.multiple_of(i * size, size), size)
        product = g_ref[rows, :].astype(jnp.float32) * ctx_ref[rows, :].astype(jnp.float32)
        delta_ref[i] = lax.dot_general(
            picks,
            product,
            NT,
            preferred_element_type=jnp.float32,
            precision=lax.Precision.HIGHEST,
        )
        dq_ref[rows, :] = jnp.zeros((size, width), jnp.float32)
        return unused

    lax.fori_loop(0, blocks, prepare, 0)

    def key_block(i, unused):
        rows = pl.ds(pl.multiple_of(i * size, size), size)
        own = col_ref[rows, :]
        dk_ref[...] = jnp.zeros((size, width), jnp.float32)
        dv_ref[...] = jnp.zeros((size, width), jnp.float32)

        def step(j, unused):
            place = lax.rem(j + blocks - shift, blocks)
            there = pl.ds(pl.multiple_of(place * size, size), size)
            same = own == row_ref[place]
            for pair in range(pairs):
                lanes = slice(pair * PAIR, (pair + 1) * PAIR)
                query = q_ref[there, lanes]
                grad = g_ref[there, lanes]
                keys = split_heads(k_ref[rows, lanes])
                values = split_heads(v_ref[rows, lanes])
                shares, slopes = [], []
                for h in range(2):
                    at = 2 * pair + h
                    s = lax.dot_general(
                        keys[h], query, NT, preferred_element_type=jnp.float32
                    )
                    s = jnp.where(same, s, NEGATIVE)
                    p = jnp.exp2(s - lse_ref[place, at : at + 1, :])
                    dp = lax.dot_general(
                        values[h], grad, NT, preferred_element_type=jnp.float32
                    )
                    shares.append(p.astype(jnp.bfloat16))
                    slopes.append(
                        (p * (dp - delta_ref[place, at : at + 1, :])).astype(jnp.bfloat16)
                    )
                dv_ref[:, lanes] += jnp.dot(
                    jnp.concatenate(shares, axis=1),
                    jnp.concatenate(split_heads(grad), axis=0),
                    preferred_element_type=jnp.float32,
                )
                dk_ref[:, lanes] += jnp.dot(
                    jnp.concatenate(slopes, axis=1),
                    jnp.concatenate(split_heads(query), axis=0),
                    preferred_element_type=jnp.float32,
                )
                dq_ref[there, lanes] += lax.dot_general(
                    jnp.concatenate(slopes, axis=0),
                    jnp.concatenate(keys, axis=0),
                    TN,
                    preferred_element_type=jnp.float32,
                )
            return unused

        lax.fori_loop(ranges[1 + 2 * i], ranges[2 + 2 * i], step, 0)
        per_chunk = own_rows // size
        chunk = lax.div(i, per_chunk)
        spot = pl.ds(pl.multiple_of(lax.rem(i, per_chunk) * size, size), size)
        out_ref[chunk, 1, spot, :] = (dk_ref[...] * LN_2).astype(jnp.bfloat16)
        out_ref[chunk, 2, spot, :] = dv_ref[...].astype(jnp.bfloat16)
        return unused

    lax.fori_loop(0, blocks, key_block, 0)
    for chunk in range(chunks):
        out_ref[chunk, 0] = (
            dq_ref[pl.ds(chunk * own_rows, own_rows), :] * HEAD_DIM ** (-0.5)
        ).astype(jnp.bfloat16)


def attend_back(
    joined, grad, context, lse, ranges, columns, rows_of, blocks, ways, tokens=()
):
    unused, total, width = joined.shape
    size = total // blocks
    wide = group_width(width)
    rows = total // ways
    whole = pl.BlockSpec((total, wide), lambda p, r: (0, p))
    grid_spec = pltpu.PrefetchScalarGridSpec(
        num_scalar_prefetch=1,
        grid=(width // wide,),
        in_specs=[
            pl.BlockSpec((None, total, wide), lambda p, r: (0, 0, p)),
            pl.BlockSpec((None, total, wide), lambda p, r: (1, 0, p)),
            pl.BlockSpec((None, total, wide), lambda p, r: (2, 0, p)),
            whole,
            whole,
            pl.BlockSpec((None,) + lse.shape[1:], lambda p, r: (p, 0, 0, 0)),
            pl.BlockSpec((total, 1), lambda p, r: (0, 0)),
            pl.BlockSpec((blocks, 1, size), lambda p, r: (0, 0, 0)),
        ]
        + [pl.BlockSpec(memory_space=pl.ANY)] * len(tokens),
        out_specs=pl.BlockSpec((ways, 3, rows, wide), lambda p, r: (0, 0, 0, p)),
        scratch_shapes=[
            pltpu.VMEM((total, wide), jnp.float32),
            pltpu.VMEM((size, wide), jnp.float32),
            pltpu.VMEM((size, wide), jnp.float32),
            pltpu.VMEM((blocks, 8, size), jnp.float32),
        ],
    )
    return pl.pallas_call(
        after(functools.partial(attend_back_kernel, blocks), 9, tokens),
        grid_spec=grid_spec,
        out_shape=jax.ShapeDtypeStruct((ways, 3, rows, width), jnp.bfloat16),
        compiler_params=params(48),
        cost_estimate=LIGHT,
    )(ranges, joined, joined, joined, grad, context, lse, columns, rows_of, *tokens)


class Layout:
    def __init__(self, dp, tensor):
        self.dp, self.tensor = dp, tensor
        self.paired = tensor == 2 and dp % 2 == 0
        self.ways = tensor

    def index(self):
        if self.paired:
            return lax.rem(lax.axis_index("dp"), 2)
        return lax.axis_index("tensor")

    def permute(self, values, target):
        pairs = []
        for place in range(self.dp * self.tensor):
            there = target(*divmod(place, self.tensor))
            if there != place:
                pairs.append((place, there))
        return lax.ppermute(values, ("dp", "tensor"), pairs)

    def stays(self):
        return lax.rem(lax.axis_index("dp"), 2) == lax.axis_index("tensor")

    def exchanged(self, values):
        return self.permute(values, lambda dp, tensor: (dp // 2 * 2 + tensor) * 2 + dp % 2)

    def swap(self, values):
        if not self.paired:
            return values
        return jnp.where(self.stays(), values, self.exchanged(values))

    def weight(self, weights, layer, tokens=()):
        if not self.paired:
            return weights[layer]
        width = weights.shape[-1]
        own = weights.reshape(-1, width)
        other = self.exchanged(weights[layer])
        first = layer * (own.shape[0] // weights.shape[0])
        moved = jnp.where(self.stays(), 0, 1).astype(jnp.int32).reshape(1)
        return choose(own, first, other.reshape(-1, width), moved, tokens).reshape(other.shape)

    def across(self, values, bit):
        return self.permute(values, lambda dp, tensor: (dp ^ 2 * bit) * 2 + tensor)

    def chip_sum(self, mine):
        chips = self.dp // 2
        bits = [1 << n for n in range(chips.bit_length() - 1)]
        if 1 << len(bits) != chips:
            groups = [[2 * chip + at for chip in range(chips)] for at in range(2)]
            return lax.psum(mine, "dp", axis_index_groups=groups)
        chip = lax.axis_index("dp") // 2
        for bit in bits:
            place = chip // bit % 2
            half = mine.shape[0] // 2
            given = self.across(
                lax.dynamic_slice_in_dim(mine, (1 - place) * half, half, 0), bit
            )
            kept = lax.dynamic_slice_in_dim(mine, place * half, half, 0)
            mine = (kept.astype(jnp.float32) + given.astype(jnp.float32)).astype(jnp.bfloat16)
        for bit in reversed(bits):
            given = self.across(mine, bit)
            mine = jnp.where(
                chip // bit % 2 == 0,
                jnp.concatenate([mine, given]),
                jnp.concatenate([given, mine]),
            )
        return mine

    def reduce(self, buffer, ahead, stepwise=False):
        if not self.paired:
            total = lax.psum(buffer, "dp")
            return total[0], total[1], jnp.zeros((1,), jnp.int32), (total, total, total)
        core = self.index()
        other = self.exchanged(buffer)
        stays = self.stays()

        def half(which):
            return jnp.where(
                stays,
                lax.dynamic_index_in_dim(buffer, which, 0, keepdims=False),
                lax.dynamic_index_in_dim(other, which, 0, keepdims=False),
            )

        given = self.shift(half(1 - core), 1)
        mine = (half(core).astype(jnp.float32) + given.astype(jnp.float32)).astype(jnp.bfloat16)
        sent = mine
        if stepwise:
            mine = self.chip_sum(mine)
            return mine, self.shift(mine, 1), core.reshape(1), (other, sent, mine)
        if ahead is not None:
            mine, unused = lax.optimization_barrier((mine, ahead))
        groups = [[2 * chip + at for chip in range(self.dp // 2)] for at in range(2)]
        mine = lax.psum(mine, "dp", axis_index_groups=groups)
        return mine, self.shift(mine, 1), core.reshape(1), (other, sent, mine)

    def shift(self, values, step):
        if self.paired:
            return self.permute(values, lambda dp, tensor: (dp // 2 * 2 + (dp + step) % 2) * 2 + tensor)
        return self.permute(
            values, lambda dp, tensor: dp * self.tensor + (tensor + step) % self.tensor
        )

    def gather(self, values):
        return [values] + [self.shift(values, -step) for step in range(1, self.ways)]

    def scatter(self, part):
        return [self.shift(part(k), k) for k in range(1, self.ways)]


def per_device(
    layout,
    frames,
    logit_grad,
    lengths,
    ln_gain,
    ln_bias,
    w_qkv,
    b_qv,
    w_out,
    b_out,
    w_up,
    b_up,
    w_down,
    b_down,
    w_head,
    b_head,
):
    ways = layout.ways
    rows, features = frames.shape
    total = rows * ways
    size = min(256, rows)
    blocks = total // size
    chunk_blocks = rows // size
    part = layout.index()
    swap = layout.swap

    stream = swap(frames.astype(jnp.bfloat16)).astype(jnp.float32)
    small = swap(
        jnp.concatenate([b_qv.reshape(-1), b_up.reshape(-1), w_head.reshape(-1)]).reshape(-1, 128)
    )
    lengths = swap(lengths)
    qkv_weights, out_weights, up_weights, down_weights = [], [], [], []
    for layer in range(LAYERS):
        qkv_weights.append(layout.weight(w_qkv, layer))
        out_weights.append(layout.weight(w_out, layer))
        down_weights.append(layout.weight(w_down, layer))
    logit_grad = swap(logit_grad.astype(jnp.bfloat16))
    small = small.reshape(-1)
    head_part = small[b_qv.size + b_up.size :].reshape(w_head.shape)
    small = small.astype(jnp.float32)
    qv_biases = small[: b_qv.size].reshape(b_qv.shape)
    up_biases = small[b_qv.size : b_qv.size + b_up.size].reshape(b_up.shape)
    head_parts = layout.gather(head_part)
    head_all = jnp.roll(jnp.concatenate(head_parts), part * w_head.shape[0], axis=0)

    positions = lax.rem(jnp.arange(total, dtype=jnp.int32) + part * rows, total)
    ends = jnp.cumsum(lengths[0])
    segment = jnp.sum((positions[:, None] >= ends[None, :]).astype(jnp.int32), axis=1)
    own_valid = positions[:rows] < ends[-1]
    columns = segment[:, None]
    rows_of = segment.reshape(blocks, 1, size)
    firsts = positions.reshape(blocks, size)[:, :1]
    lows = jnp.max(jnp.where(ends[None, :] <= firsts, ends[None, :], 0), axis=1) // size
    lasts = firsts + (size - 1)
    highs = jnp.min(jnp.where(ends[None, :] > lasts, ends[None, :], total), axis=1)
    highs = (highs + size - 1) // size
    ranges = jnp.concatenate(
        [(part * chunk_blocks).reshape(1), jnp.stack([lows, highs], axis=1).reshape(-1)]
    ).astype(jnp.int32)
    gains = ln_gain.astype(jnp.float32)
    shifts = ln_bias.astype(jnp.float32)

    def chunk(values, k):
        return values[k * rows : (k + 1) * rows]

    saved = []
    normed = layer_norm(stream, gains[0, 0], shifts[0, 0]).astype(jnp.bfloat16)
    for layer in range(LAYERS):
        last = layer + 1 == LAYERS
        normed_all = layout.gather(normed)
        bias = jnp.stack(
            [qv_biases[layer, 0], jnp.zeros_like(qv_biases[layer, 0]), qv_biases[layer, 1]]
        )[:, None, :]
        joined = None
        for k in range(ways):
            joined = project(normed_all[k], qkv_weights[layer], bias, k, ways, joined)
        context, lse = attend(
            joined, ranges, columns, rows_of, blocks, (logit_grad,) if last else ()
        )
        chunks = context.reshape(ways, rows, -1)
        up_weights.append(layout.weight(w_up, layer, (context,)))
        weight = out_weights[layer]
        received = layout.scatter(
            lambda k: times(chunks, (k,), weight, NN, tokens=(up_weights[layer],))
        )
        middle, normed_ffn = join(
            chunks,
            (0,),
            weight,
            stream,
            b_out[layer].astype(jnp.float32),
            gains[layer, 1],
            shifts[layer, 1],
            received,
        )
        ffn_all = layout.gather(normed_ffn)
        hidden, slopes = [], []
        for k in range(ways):
            one, other = gelu_up(ffn_all[k], up_weights[layer], up_biases[layer][None, :])
            hidden.append(one)
            slopes.append(other)
        weight = down_weights[layer]
        received = layout.scatter(lambda k: times(hidden[k], (), weight, NN))
        saved.append(
            (stream, middle, normed_all, joined, context, lse, ffn_all, hidden, slopes)
        )
        following = (layer + 1) % LAYERS
        ended = join(
            hidden[0],
            (),
            weight,
            middle,
            b_down[layer].astype(jnp.float32),
            gains[following, 0],
            shifts[following, 0],
            received,
            last,
        )
        if last:
            final_low = ended[0]
        else:
            stream, normed = ended

    logits = swap((matmul(final_low, head_all) + b_head.astype(jnp.float32)))
    grad_logits = jnp.where(own_valid[:, None], logit_grad, 0.0).astype(jnp.bfloat16)
    head_grad = inner_rows(final_low, grad_logits)
    head_bias_grad = column_sums(grad_logits)
    grad_stream = outer_cols(grad_logits, head_all)

    wide = w_qkv.shape[3]
    inner_width = w_up.shape[2]
    tiles = features // wide
    inner_tiles = inner_width // wide
    ffn_shape = (2, features * inner_tiles + SMALL_ROWS, wide)
    attn_shape = (2, 2 * features + SMALL_ROWS, wide)

    def shares(vectors):
        matrix = jnp.stack(vectors)

        def share(k):
            return lax.dynamic_slice_in_dim(matrix, lax.rem(part + k, ways) * wide, wide, 1)

        received = layout.scatter(lambda k: share(k).astype(jnp.bfloat16))
        return share(0) + sum(values.astype(jnp.float32) for values in received)

    def with_small(buffer, lines):
        count, width = lines.shape
        lines = jnp.pad(lines, ((0, 2 * SMALL_ROWS - count), (0, 0))).astype(jnp.bfloat16)
        return lax.dynamic_update_slice(
            buffer, lines.reshape(2, SMALL_ROWS, width), (0, buffer.shape[1] - SMALL_ROWS, 0)
        )

    head_lines = [
        head_grad.T,
        jnp.pad(head_bias_grad.reshape(ways, -1), ((0, 0), (0, wide - b_head.shape[0] // ways))).reshape(
            1, features
        ),
    ]
    low = grad_stream.astype(jnp.bfloat16)
    bias_down = column_sums(low)
    ahead = None
    stages = {}
    outputs = [None] * 4
    smalls = {}

    for layer in reversed(range(LAYERS)):
        stream_in, middle, normed_all, joined, context, lse, ffn_all, hidden, slopes = saved[
            layer
        ]
        low_all = layout.gather(low)
        inner, inner_sums = [], []
        for k in range(ways):
            one, other = inner_grad(low_all[k], down_weights[layer], slopes[k])
            inner.append(one)
            inner_sums.append(other)
        weight = up_weights[layer]
        received = layout.scatter(lambda k: times(inner[k], (), weight, NT))
        grad_middle, middle_low, norm_sums = norm_back(
            [(inner[0], ())], weight, middle, grad_stream, gains[layer, 1], received
        )
        tokens = ()
        if layer + 1 < LAYERS:
            tokens = (stages["ffn", layer + 1][1], stages["attn", layer + 1][0])
        buffer = weight_grad(
            [(hidden[k], ()) for k in range(ways)],
            [(low_all[k], ()) for k in range(ways)],
            None,
            ffn_shape,
            lambda g, n: (1, n * inner_width),
            tokens,
        )
        buffer = weight_grad(
            [(ffn_all[k], ()) for k in range(ways)],
            [(inner[k], ()) for k in range(ways)],
            buffer,
            ffn_shape,
            lambda g, n: (0, n * features),
        )
        bias_up = sum(inner_sums)
        bias_out = norm_sums[2]
        lines = [bias_down, norm_sums[0], norm_sums[1]]
        if layer == LAYERS - 1:
            lines += list(head_lines[0]) + list(head_lines[1])
        lines = jnp.concatenate([bias_up.reshape(inner_tiles, wide), shares(lines)])
        buffer = with_small(buffer, lines)
        one, two, flag, stages["ffn", layer] = layout.reduce(buffer, ahead)
        ahead = one
        follow = (buffer,)
        outputs[0] = unpack(
            one, two, flag, 0, features, inner_tiles, layer, outputs[0], features, 0
        )
        outputs[1] = unpack(
            two, one, flag, 0, inner_width, tiles, layer, outputs[1], inner_width, 0
        )
        smalls["ffn", layer] = (one, two, flag)

        low_all = layout.gather(middle_low)
        grad_context = None
        for k in range(ways):
            grad_context = times(
                low_all[k], (), out_weights[layer], NT, k, ways, grad_context
            )
        buffer = weight_grad(
            [(context.reshape(ways, rows, -1), (k,)) for k in range(ways)],
            [(low_all[k], ()) for k in range(ways)],
            None,
            attn_shape,
            lambda g, n: (1, features + n * wide),
        )
        grads = attend_back(
            joined, grad_context, context, lse, ranges, columns, rows_of, blocks, ways, follow
        )
        tokens = (stages["ffn", layer][0],)
        if layer + 1 < LAYERS:
            tokens += (stages["ffn", layer + 1][2],)
        buffer = weight_grad(
            [(normed_all[k], ()) for k in range(ways)],
            [(grads, (k, None)) for k in range(ways)],
            buffer,
            attn_shape,
            lambda g, n: (g // 2, g % 2 * features),
            tokens,
        )
        bias_qv = jnp.sum(grads, axis=(0, 2), dtype=jnp.float32)[::2]
        weight = qkv_weights[layer]
        received = layout.scatter(
            lambda k: jnp.einsum(
                "ktc,kdc->td", grads[k], weight, preferred_element_type=jnp.float32
            ).astype(jnp.bfloat16)
        )
        grad_stream, low, norm_sums = norm_back(
            [(grads, (0, kind)) for kind in range(3)],
            weight,
            stream_in,
            grad_middle,
            gains[layer, 0],
            received,
        )
        lines = jnp.concatenate([bias_qv, shares([bias_out, norm_sums[0], norm_sums[1]])])
        bias_down = norm_sums[2]
        one, two, flag, stages["attn", layer] = layout.reduce(
            with_small(buffer, lines), ahead, layer == 0
        )
        ahead = one
        joined_rows = 3 * features
        outputs[2] = unpack(
            one, two, flag, 0, 2 * features, 1, layer, outputs[2], joined_rows, 0
        )
        outputs[2] = unpack(
            two, one, flag, 0, features, 1, layer, outputs[2], joined_rows, 2 * features
        )
        outputs[3] = unpack(
            two, one, flag, features, wide, tiles, layer, outputs[3], wide, 0
        )
        smalls["attn", layer] = (one, two, flag)

    input_grad = swap(low).astype(jnp.float32)

    grad_qkv = outputs[2].reshape(LAYERS, 3, features, wide)

    def lines_of(kind, layer):
        one, two, flag = smalls[kind, layer]
        one, two = one[-SMALL_ROWS:], two[-SMALL_ROWS:]
        return jnp.where(
            flag[0] == 0, jnp.concatenate([one, two]), jnp.concatenate([two, one])
        ).astype(jnp.float32)

    ffn_lines = [lines_of("ffn", layer) for layer in range(LAYERS)]
    attn_lines = [lines_of("attn", layer) for layer in range(LAYERS)]
    t = inner_tiles
    bias_up = jnp.stack([lines[:t].reshape(-1) for lines in ffn_lines])
    bias_down = jnp.stack([lines[t] for lines in ffn_lines])
    bias_qv = jnp.stack([lines[:2] for lines in attn_lines])
    bias_out = jnp.stack([lines[2] for lines in attn_lines])
    gain = jnp.stack(
        [jnp.stack([attn_lines[layer][3], ffn_lines[layer][t + 1]]) for layer in range(LAYERS)]
    )
    shift = jnp.stack(
        [jnp.stack([attn_lines[layer][4], ffn_lines[layer][t + 2]]) for layer in range(LAYERS)]
    )
    vocab = b_head.shape[0]
    head_weight = ffn_lines[-1][t + 3 : t + 3 + vocab].T
    head_bias = ffn_lines[-1][t + 3 + vocab, : vocab // ways]
    return (
        logits,
        input_grad,
        gain,
        shift,
        grad_qkv,
        bias_qv,
        outputs[3],
        bias_out,
        outputs[0],
        bias_up,
        outputs[1],
        bias_down,
        head_weight,
        head_bias,
    )


def solution(mesh):
    layout = Layout(mesh.shape["dp"], mesh.shape["tensor"])
    by_rows = P(("dp", "tensor"), None)
    placed = (
        by_rows,
        by_rows,
        P("dp", None),
        P(),
        P(),
        P(None, None, None, "tensor"),
        P(None, None, "tensor"),
        P(None, "tensor", None),
        P(),
        P(None, None, "tensor"),
        P(None, "tensor"),
        P(None, "tensor", None),
        P(),
        P("tensor", None),
        P(),
    )
    return jax.shard_map(
        functools.partial(per_device, layout),
        mesh=mesh,
        in_specs=placed,
        out_specs=(
            by_rows,
            by_rows,
            P(None, None, "tensor"),
            P(None, None, "tensor"),
            P(None, None, None, "tensor"),
            P(None, None, "tensor"),
            P(None, "tensor", None),
            P(None, "tensor"),
            P(None, None, "tensor"),
            P(None, "tensor"),
            P(None, "tensor", None),
            P(None, "tensor"),
            P("tensor", None),
            P("tensor"),
        ),
        check_vma=False,
    )
```

```python
import functools

import jax
import jax.numpy as jnp
from jax import lax
from jax.experimental import pallas as pl
from jax.experimental.pallas import tpu as pltpu
from jax.sharding import PartitionSpec as P

HEAD_DIM = 64
LAYERS = 2
EPSILON = 1e-05
PAIR = 2 * HEAD_DIM
NEGATIVE = -1e30
SUM_ROWS = 16
FFN_SMALL = 256
ATTN_SMALL = 128
LOG2_E = 1.4426950408889634
LN_2 = 0.6931471805599453
MIB = 1 << 20
NN = (((1,), (0,)), ((), ()))
NT = (((1,), (1,)), ((), ()))
TN = (((0,), (0,)), ((), ()))


def layer_norm(values, gain, shift):
    mean = jnp.mean(values, axis=-1, keepdims=True)
    centred = values - mean
    spread = jnp.mean(centred * centred, axis=-1, keepdims=True)
    return centred * lax.rsqrt(spread + EPSILON) * gain + shift


def matmul(left, right):
    return jnp.dot(left, right, preferred_element_type=jnp.float32)


def outer_cols(left, right):
    return lax.dot_general(left, right, NT, preferred_element_type=jnp.float32)


def inner_rows(left, right):
    return lax.dot_general(left, right, TN, preferred_element_type=jnp.float32)


def column_sums(values):
    return jnp.sum(values, axis=0, dtype=jnp.float32)


def tile(size, limit):
    return size if size <= limit else limit


LIGHT = pl.CostEstimate(flops=0, bytes_accessed=0, transcendentals=0)


def after(kernel, first, tokens):
    return lambda *refs: kernel(*refs[:first], *refs[first + len(tokens) :])


def params(mib):
    return pltpu.CompilerParams(vmem_limit_bytes=mib * MIB)


def project_kernel(x_ref, w_ref, b_ref, *rest):
    out_ref = rest[-1]
    gain = jnp.where(pl.program_id(0) == 0, HEAD_DIM ** (-0.5) * LOG2_E, 1.0)
    value = jnp.dot(x_ref[...], w_ref[...], preferred_element_type=jnp.float32)
    out_ref[...] = ((value + b_ref[...]) * gain).astype(jnp.bfloat16)


def project(x, weight, bias, chunk, ways, joined):
    rows, depth = x.shape
    kinds, unused, width = weight.shape
    wide = tile(width, 512)
    in_specs = [
        pl.BlockSpec((rows, depth), lambda k, n: (0, 0)),
        pl.BlockSpec((None, depth, wide), lambda k, n: (k, 0, n)),
        pl.BlockSpec((None, 1, wide), lambda k, n: (k, 0, n)),
    ]
    args = [x, weight, bias]
    aliases = {}
    if joined is not None:
        in_specs.append(pl.BlockSpec(memory_space=pl.ANY))
        args.append(joined)
        aliases = {3: 0}
    return pl.pallas_call(
        project_kernel,
        grid=(kinds, width // wide),
        in_specs=in_specs,
        out_specs=pl.BlockSpec((None, rows, wide), lambda k, n: (k, chunk, n)),
        out_shape=jax.ShapeDtypeStruct((kinds, rows * ways, width), jnp.bfloat16),
        input_output_aliases=aliases,
        compiler_params=params(32),
        cost_estimate=LIGHT,
    )(*args)


ERF_STEP = 0.3275911
ERF_TERMS = (0.254829592, -0.284496736, 1.421413741, -1.453152027, 1.061405429)


def gelu_kernel(sub, x_ref, w_ref, b_ref, hidden_ref, slope_ref):
    for start in range(0, x_ref.shape[0], sub):
        rows = pl.ds(start, sub)
        u = (
            jnp.dot(x_ref[rows, :], w_ref[...], preferred_element_type=jnp.float32)
            + b_ref[...]
        )
        density = jnp.exp(u * u * -0.5)
        t = 1.0 / (1.0 + (ERF_STEP * 0.5**0.5) * jnp.abs(u))
        poly = ERF_TERMS[4]
        for term in ERF_TERMS[3::-1]:
            poly = poly * t + term
        tail = (0.5 * poly) * t * density
        phi = jnp.where(u < 0.0, tail, 1.0 - tail)
        hidden_ref[rows, :] = (u * phi).astype(jnp.bfloat16)
        slope_ref[rows, :] = (phi + u * density * 0.3989422804014327).astype(jnp.bfloat16)


def gelu_up(x, weight, bias):
    rows, depth = x.shape
    width = weight.shape[1]
    wide = tile(width, 512)
    out = jax.ShapeDtypeStruct((rows, width), jnp.bfloat16)
    return pl.pallas_call(
        functools.partial(gelu_kernel, tile(rows, 256)),
        grid=(width // wide,),
        in_specs=[
            pl.BlockSpec((rows, depth), lambda n: (0, 0)),
            pl.BlockSpec((depth, wide), lambda n: (0, n)),
            pl.BlockSpec((1, wide), lambda n: (0, n)),
        ],
        out_specs=[pl.BlockSpec((rows, wide), lambda n: (0, n))] * 2,
        out_shape=[out, out],
        compiler_params=params(32),
        cost_estimate=LIGHT,
    )(x, weight, bias)


def times_kernel(dims, x_ref, w_ref, *rest):
    rest[-1][...] = lax.dot_general(
        x_ref[...], w_ref[...], dims, preferred_element_type=jnp.float32
    ).astype(jnp.bfloat16)


def row_spec(array, lead, high):
    return pl.BlockSpec(
        (None,) * len(lead) + (high, array.shape[-1]), lambda m: lead + (m, 0)
    )


def whole_spec(array):
    return pl.BlockSpec(array.shape, lambda m: (0,) * array.ndim)


def times(x, lead, weight, dims, chunk=0, chunks=1, buffer=None, tokens=()):
    rows = x.shape[-2]
    width = weight.shape[0] if dims == NT else weight.shape[1]
    high = tile(rows, 256)
    in_specs = [row_spec(x, lead, high), whole_spec(weight)]
    args = [x, weight]
    aliases = {}
    if buffer is not None:
        aliases = {2: 0}
        in_specs.append(pl.BlockSpec(memory_space=pl.ANY))
        args.append(buffer)
    in_specs += [pl.BlockSpec(memory_space=pl.ANY)] * len(tokens)
    args += tokens
    return pl.pallas_call(
        functools.partial(times_kernel, dims),
        grid=(rows // high,),
        in_specs=in_specs,
        out_specs=pl.BlockSpec((high, width), lambda m: (chunk * (rows // high) + m, 0)),
        out_shape=jax.ShapeDtypeStruct((rows * chunks, width), jnp.bfloat16),
        input_output_aliases=aliases,
        compiler_params=params(40),
        cost_estimate=LIGHT,
    )(*args)


def kinds_kernel(x_ref, w_ref, out_ref):
    total = lax.dot_general(x_ref[0], w_ref[0], NT, preferred_element_type=jnp.float32)
    for kind in range(1, w_ref.shape[0]):
        total += lax.dot_general(
            x_ref[kind], w_ref[kind], NT, preferred_element_type=jnp.float32
        )
    out_ref[...] = total.astype(jnp.bfloat16)


def times_kinds(x, chunk, weight):
    kinds, rows, width = x.shape[1:]
    features = weight.shape[1]
    high = tile(rows, 256)
    return pl.pallas_call(
        kinds_kernel,
        grid=(rows // high,),
        in_specs=[
            pl.BlockSpec((None, kinds, high, width), lambda m: (chunk, 0, m, 0)),
            whole_spec(weight),
        ],
        out_specs=pl.BlockSpec((high, features), lambda m: (m, 0)),
        out_shape=jax.ShapeDtypeStruct((rows, features), jnp.bfloat16),
        compiler_params=params(40),
        cost_estimate=LIGHT,
    )(x, weight)


def join_kernel(count, last, x_ref, w_ref, res_ref, bias_ref, gain_ref, shift_ref, *rest):
    received, outs = rest[:count], rest[count:]
    value = jnp.dot(x_ref[...], w_ref[...], preferred_element_type=jnp.float32)
    for ref in received:
        value += ref[...].astype(jnp.float32)
    value += res_ref[...] + bias_ref[...]
    if last:
        outs[0][...] = value.astype(jnp.bfloat16)
    else:
        outs[0][...] = value
        outs[1][...] = layer_norm(value, gain_ref[...], shift_ref[...]).astype(jnp.bfloat16)


def join(x, lead, weight, residual, bias, gain, shift, received, last=False):
    rows, features = residual.shape
    high = tile(rows, 256)
    block = pl.BlockSpec((high, features), lambda m: (m, 0))
    vector = pl.BlockSpec((1, features), lambda m: (0, 0))
    low = jax.ShapeDtypeStruct(residual.shape, jnp.bfloat16)
    full = jax.ShapeDtypeStruct(residual.shape, jnp.float32)
    return pl.pallas_call(
        functools.partial(join_kernel, len(received), last),
        grid=(rows // high,),
        in_specs=[row_spec(x, lead, high), whole_spec(weight), block, vector, vector, vector]
        + [block] * len(received),
        out_specs=[block] if last else [block, block],
        out_shape=[low] if last else [full, low],
        compiler_params=params(40),
        cost_estimate=LIGHT,
    )(x, weight, residual, bias[None], gain[None], shift[None], *received)


def inner_kernel(sub, d_ref, w_ref, slope_ref, out_ref, sums_ref):
    sums = jnp.zeros(sums_ref.shape, jnp.float32)
    for start in range(0, d_ref.shape[0], sub):
        rows = pl.ds(start, sub)
        value = lax.dot_general(
            d_ref[rows, :], w_ref[...], NT, preferred_element_type=jnp.float32
        )
        value = (value * slope_ref[rows, :].astype(jnp.float32)).astype(jnp.bfloat16)
        out_ref[rows, :] = value
        sums += jnp.sum(value.astype(jnp.float32), axis=0, keepdims=True)
    sums_ref[...] = sums


def inner_grad(d, weight, slope, tokens=()):
    rows, features = d.shape
    width = weight.shape[0]
    wide = tile(width, 512)
    column = pl.BlockSpec((rows, wide), lambda n: (0, n))
    return pl.pallas_call(
        after(functools.partial(inner_kernel, tile(rows, 256)), 3, tokens),
        grid=(width // wide,),
        in_specs=[
            pl.BlockSpec((rows, features), lambda n: (0, 0)),
            pl.BlockSpec((wide, features), lambda n: (n, 0)),
            column,
        ]
        + [pl.BlockSpec(memory_space=pl.ANY)] * len(tokens),
        out_specs=[column, pl.BlockSpec((1, wide), lambda n: (0, n))],
        out_shape=[
            jax.ShapeDtypeStruct((rows, width), jnp.bfloat16),
            jax.ShapeDtypeStruct((1, width), jnp.float32),
        ],
        compiler_params=params(40),
        cost_estimate=LIGHT,
    )(d, weight, slope, *tokens)


def back_kernel(kinds, count, *refs):
    xs, ws = refs[:kinds], refs[kinds]
    value_ref, grad_ref, gain_ref = refs[kinds + 1 : kinds + 4]
    received = refs[kinds + 4 : kinds + 4 + count]
    full_ref, low_ref, sums_ref = refs[kinds + 4 + count :]
    if kinds == 1:
        weights = [ws[...]]
    else:
        weights = [ws[k] for k in range(kinds)]
    given = lax.dot_general(xs[0][...], weights[0], NT, preferred_element_type=jnp.float32)
    for k in range(1, kinds):
        given += lax.dot_general(xs[k][...], weights[k], NT, preferred_element_type=jnp.float32)
    for ref in received:
        given += ref[...].astype(jnp.float32)
    values = value_ref[...]
    centred = values - jnp.mean(values, axis=-1, keepdims=True)
    scale = lax.rsqrt(jnp.mean(centred * centred, axis=-1, keepdims=True) + EPSILON)
    unit = centred * scale
    inward = given * gain_ref[...]
    mean = jnp.mean(inward, axis=-1, keepdims=True)
    along = jnp.mean(inward * unit, axis=-1, keepdims=True)
    full = grad_ref[...] + scale * (inward - mean - unit * along)
    low = full.astype(jnp.bfloat16)
    full_ref[...] = full
    low_ref[...] = low

    @pl.when(pl.program_id(0) == 0)
    def _():
        sums_ref[...] = jnp.zeros(sums_ref.shape, jnp.float32)

    sums_ref[0:1, :] += jnp.sum(given * unit, axis=0, keepdims=True)
    sums_ref[1:2, :] += jnp.sum(given, axis=0, keepdims=True)
    sums_ref[2:3, :] += jnp.sum(low.astype(jnp.float32), axis=0, keepdims=True)


def norm_back(xs, weight, values, grad, gain, received):
    rows, features = values.shape
    high = tile(rows, 256)
    block = pl.BlockSpec((high, features), lambda m: (m, 0))
    return pl.pallas_call(
        functools.partial(back_kernel, len(xs), len(received)),
        grid=(rows // high,),
        in_specs=[row_spec(x, lead, high) for x, lead in xs]
        + [whole_spec(weight), block, block, pl.BlockSpec((1, features), lambda m: (0, 0))]
        + [block] * len(received),
        out_specs=[block, block, pl.BlockSpec((8, features), lambda m: (0, 0))],
        out_shape=[
            jax.ShapeDtypeStruct(values.shape, jnp.float32),
            jax.ShapeDtypeStruct(values.shape, jnp.bfloat16),
            jax.ShapeDtypeStruct((8, features), jnp.float32),
        ],
        compiler_params=params(48),
        cost_estimate=LIGHT,
    )(*[x for x, unused in xs], weight, values, grad, gain[None], *received)


def weight_kernel(chunks, *refs):
    x_refs, d_refs = refs[:chunks], refs[chunks : 2 * chunks]
    out_ref, turned = refs[-2:]

    @pl.when((pl.program_id(1) == 0) & (pl.program_id(2) == 0))
    def _():
        for k in range(chunks):
            turned[k] = x_refs[k][...].T

    total = jnp.dot(turned[0], d_refs[0][...], preferred_element_type=jnp.float32)
    for k in range(1, chunks):
        total += jnp.dot(turned[k], d_refs[k][...], preferred_element_type=jnp.float32)
    out_ref[...] = total.astype(jnp.bfloat16)


def weight_grad(xs, ds, buffer, shape, place, tokens=()):
    chunks = len(xs)
    rows, tall = xs[0][0].shape[-2:]
    width = ds[0][0].shape[-1]
    kinds = 1
    if None in ds[0][1]:
        kinds = ds[0][0].shape[ds[0][1].index(None)]
    high, wide = tile(tall, 512), shape[2]

    def x_spec(lead):
        return pl.BlockSpec(
            (None,) * len(lead) + (rows, high), lambda m, g, n: lead + (0, m)
        )

    def d_spec(lead):
        return pl.BlockSpec(
            (None,) * len(lead) + (rows, wide),
            lambda m, g, n: tuple(g if at is None else at for at in lead) + (0, n),
        )

    def out_index(m, g, n):
        half, row = place(g, n)
        return half, row // high + m, 0

    in_specs = [x_spec(lead) for unused, lead in xs] + [d_spec(lead) for unused, lead in ds]
    args = [array for array, unused in xs] + [array for array, unused in ds]
    aliases = {}
    if buffer is not None:
        aliases = {len(args): 0}
        in_specs.append(pl.BlockSpec(memory_space=pl.ANY))
        args.append(buffer)
    in_specs += [pl.BlockSpec(memory_space=pl.ANY)] * len(tokens)
    args += tokens
    return pl.pallas_call(
        functools.partial(weight_kernel, chunks),
        grid=(tall // high, kinds, width // wide),
        in_specs=in_specs,
        out_specs=pl.BlockSpec((None, high, wide), out_index),
        out_shape=jax.ShapeDtypeStruct(shape, jnp.bfloat16),
        scratch_shapes=[pltpu.VMEM((chunks, high, rows), jnp.bfloat16)],
        input_output_aliases=aliases,
        compiler_params=params(40),
        cost_estimate=LIGHT,
    )(*args)


def choose_kernel(flag, own_ref, other_ref, out_ref):
    out_ref[...] = jnp.where(flag[0] == 0, own_ref[...], other_ref[...])


def choose(flag, own, own_place, other, other_place, shape, block, tokens=()):
    def spec(which, place):
        def index(m, n, f):
            here = jnp.where(f[0] == which, 1, 0)
            row, column = place(m, n, f)
            return here * row, here * column

        return pl.BlockSpec(block, index)

    return pl.pallas_call(
        after(choose_kernel, 3, tokens),
        grid_spec=pltpu.PrefetchScalarGridSpec(
            num_scalar_prefetch=1,
            grid=(shape[0] // block[0], shape[1] // block[1]),
            in_specs=[spec(0, own_place), spec(1, other_place)]
            + [pl.BlockSpec(memory_space=pl.ANY)] * len(tokens),
            out_specs=pl.BlockSpec(block, lambda m, n, f: (m, n)),
        ),
        out_shape=jax.ShapeDtypeStruct(shape, jnp.bfloat16),
        compiler_params=params(32),
        cost_estimate=LIGHT,
    )(flag, own, other, *tokens)


def copy_kernel(in_ref, out_ref):
    out_ref[...] = in_ref[...]


def pick(values, first, rows, tokens):
    width = values.shape[1]
    high = tile(rows, 512)
    return pl.pallas_call(
        after(copy_kernel, 1, tokens),
        grid=(rows // high,),
        in_specs=[pl.BlockSpec((high, width), lambda m: (first // high + m, 0))]
        + [pl.BlockSpec(memory_space=pl.ANY)] * len(tokens),
        out_specs=pl.BlockSpec((high, width), lambda m: (m, 0)),
        out_shape=jax.ShapeDtypeStruct((rows, width), values.dtype),
        compiler_params=params(16),
        cost_estimate=LIGHT,
    )(values, *tokens)


def take_kernel(count, up_ref, down_ref, out_ref):
    out_ref[...] = jnp.where(pl.program_id(0) < count, up_ref[...], down_ref[...])


def take(w_up, w_down, layer, tokens=()):
    features, inner = w_up.shape[1:]
    high = tile(features, 512)
    rows, down = features // high, inner // high
    ups = rows * (inner // features)

    def up_index(m):
        here = jnp.minimum(m, ups - 1)
        return layer, here % rows, here // rows

    return pl.pallas_call(
        after(functools.partial(take_kernel, ups), 2, tokens),
        grid=(ups + down,),
        in_specs=[
            pl.BlockSpec((None, high, features), up_index),
            pl.BlockSpec((None, high, features), lambda m: (layer, jnp.maximum(m - ups, 0), 0)),
        ]
        + [pl.BlockSpec(memory_space=pl.ANY)] * len(tokens),
        out_specs=pl.BlockSpec((high, features), lambda m: (m, 0)),
        out_shape=jax.ShapeDtypeStruct((2 * inner, features), jnp.bfloat16),
        compiler_params=params(32),
        cost_estimate=LIGHT,
    )(w_up, w_down, *tokens)


def fold_kernel(place, mine_ref, given_ref, out_ref):
    out_ref[...] = (
        mine_ref[...].astype(jnp.float32) + given_ref[...].astype(jnp.float32)
    ).astype(jnp.bfloat16)


def fold(mine, given, place, tokens=()):
    rows, width = given.shape
    block = (rows, width)
    return pl.pallas_call(
        after(fold_kernel, 3, tokens),
        grid_spec=pltpu.PrefetchScalarGridSpec(
            num_scalar_prefetch=1,
            grid=(1,),
            in_specs=[
                pl.BlockSpec(block, lambda m, p: (p[0], 0)),
                pl.BlockSpec(block, lambda m, p: (0, 0)),
            ]
            + [pl.BlockSpec(memory_space=pl.ANY)] * len(tokens),
            out_specs=pl.BlockSpec(block, lambda m, p: (0, 0)),
        ),
        out_shape=jax.ShapeDtypeStruct(block, jnp.bfloat16),
        compiler_params=params(32),
        cost_estimate=LIGHT,
    )(place.astype(jnp.int32).reshape(1), mine, given, *tokens)


def unpack_kernel(flag, one_ref, two_ref, *rest):
    rest[-1][...] = jnp.where(flag[0] == 0, one_ref[...], two_ref[...]).astype(jnp.float32)


def unpack(one, two, flag, first, tall, tiles, layer, output, out_rows, out_first):
    wide = one.shape[1]
    high = tile(tall, 1024)
    skip = first // high

    def spec(which):
        def index(m, n, f):
            here = jnp.where(f[0] == which, 1, 0)
            return here * (skip + n * (tall // high) + m), 0

        return pl.BlockSpec((high, wide), index)

    args = [flag, one, two]
    in_specs = [spec(0), spec(1)]
    aliases = {}
    if output is not None:
        aliases = {3: 0}
        in_specs.append(pl.BlockSpec(memory_space=pl.ANY))
        args.append(output)
    return pl.pallas_call(
        unpack_kernel,
        grid_spec=pltpu.PrefetchScalarGridSpec(
            num_scalar_prefetch=1,
            grid=(tall // high, tiles),
            in_specs=in_specs,
            out_specs=pl.BlockSpec(
                (None, high, wide), lambda m, n, f: (layer, out_first // high + m, n)
            ),
        ),
        out_shape=jax.ShapeDtypeStruct((LAYERS, out_rows, tiles * wide), jnp.float32),
        input_output_aliases=aliases,
        compiler_params=params(32),
        cost_estimate=LIGHT,
    )(*args)


def head_lanes(shape):
    return lax.broadcasted_iota(jnp.int32, shape, 1) < HEAD_DIM


def split_heads(values):
    first = head_lanes(values.shape)
    zero = jnp.zeros_like(values)
    return jnp.where(first, values, zero), jnp.where(first, zero, values)


def attend_kernel(
    blocks, ranges, q_ref, k_ref, v_ref, col_ref, row_ref, ctx_ref, lse_ref, turned, tops, totals
):
    i = pl.program_id(0)
    size, width = q_ref.shape
    heads = width // HEAD_DIM
    pairs = width // PAIR
    groups, group_heads, unused = lse_ref.shape
    shift = ranges[0]

    @pl.when(i == 0)
    def _():
        def turn(place, unused):
            rows = pl.ds(pl.multiple_of(place * size, size), size)
            for p in range(pairs):
                flipped = v_ref[rows, p * PAIR : (p + 1) * PAIR].T
                for h in range(2):
                    turned[place, 2 * p + h, :HEAD_DIM, :] = flipped[
                        h * HEAD_DIM : (h + 1) * HEAD_DIM
                    ]
                    turned[place, 2 * p + h, HEAD_DIM:, :] = jnp.ones(
                        (SUM_ROWS, size), jnp.bfloat16
                    )
            return unused

        lax.fori_loop(0, blocks, turn, 0)

    own = row_ref[i]
    for h in range(heads):
        tops[h] = jnp.full((1, size), NEGATIVE, jnp.float32)
        totals[h] = jnp.zeros((HEAD_DIM + SUM_ROWS, size), jnp.float32)

    def step(j, unused):
        place = lax.rem(j + blocks - shift, blocks)
        rows = pl.ds(pl.multiple_of(place * size, size), size)
        same = col_ref[rows, :] == own
        for p in range(pairs):
            lanes = slice(p * PAIR, (p + 1) * PAIR)
            keys = k_ref[rows, lanes]
            queries = split_heads(q_ref[:, lanes])
            for h in range(2):
                at = 2 * p + h
                s = lax.dot_general(keys, queries[h], NT, preferred_element_type=jnp.float32)
                s = jnp.where(same, s, NEGATIVE)
                top = tops[at]
                new = jnp.maximum(top, jnp.max(s, axis=0, keepdims=True))
                weights = jnp.exp2(s - new)
                tops[at] = new
                totals[at] = totals[at] * jnp.exp2(top - new) + jnp.dot(
                    turned[place, at],
                    weights.astype(jnp.bfloat16),
                    preferred_element_type=jnp.float32,
                )
        return unused

    lax.fori_loop(ranges[1 + 2 * i], ranges[2 + 2 * i], step, 0)
    for p in range(pairs):
        parts = []
        for h in (2 * p, 2 * p + 1):
            total = totals[h]
            sums = total[HEAD_DIM : HEAD_DIM + 1, :]
            parts.append(total[:HEAD_DIM, :] / sums)
            group, row = divmod(h, group_heads)
            lse_ref[group, row : row + 1, :] = tops[h] + jnp.log(sums) * LOG2_E
        ctx_ref[:, p * PAIR : (p + 1) * PAIR] = (
            jnp.concatenate(parts, axis=0).T.astype(jnp.bfloat16)
        )


def group_width(width):
    return tile(width, 2 * PAIR)


def attend(joined, ranges, columns, rows_of, blocks, tokens=()):
    unused, total, width = joined.shape
    size = total // blocks
    heads = width // HEAD_DIM
    group_heads = group_width(width) // HEAD_DIM
    groups = heads // group_heads
    grid_spec = pltpu.PrefetchScalarGridSpec(
        num_scalar_prefetch=1,
        grid=(blocks,),
        in_specs=[
            pl.BlockSpec((None, size, width), lambda i, r: (0, i, 0)),
            pl.BlockSpec((None, total, width), lambda i, r: (1, 0, 0)),
            pl.BlockSpec((None, total, width), lambda i, r: (2, 0, 0)),
            pl.BlockSpec((total, 1), lambda i, r: (0, 0)),
            pl.BlockSpec((blocks, 1, size), lambda i, r: (0, 0, 0)),
        ]
        + [pl.BlockSpec(memory_space=pl.ANY)] * len(tokens),
        out_specs=[
            pl.BlockSpec((size, width), lambda i, r: (i, 0)),
            pl.BlockSpec((groups, None, group_heads, size), lambda i, r: (0, i, 0, 0)),
        ],
        scratch_shapes=[
            pltpu.VMEM((blocks, heads, HEAD_DIM + SUM_ROWS, size), jnp.bfloat16),
            pltpu.VMEM((heads, 1, size), jnp.float32),
            pltpu.VMEM((heads, HEAD_DIM + SUM_ROWS, size), jnp.float32),
        ],
    )
    return pl.pallas_call(
        after(functools.partial(attend_kernel, blocks), 6, tokens),
        grid_spec=grid_spec,
        out_shape=[
            jax.ShapeDtypeStruct((total, width), jnp.bfloat16),
            jax.ShapeDtypeStruct((groups, blocks, group_heads, size), jnp.float32),
        ],
        compiler_params=params(40),
        cost_estimate=LIGHT,
    )(ranges, joined, joined, joined, columns, rows_of, *tokens)


def attend_back_kernel(
    blocks,
    ranges,
    q_ref,
    k_ref,
    v_ref,
    g_ref,
    ctx_ref,
    lse_ref,
    col_ref,
    row_ref,
    out_ref,
    sums_ref,
    dq_ref,
    dk_ref,
    dv_ref,
    delta_ref,
):
    total, width = q_ref.shape
    size = total // blocks
    pairs = width // PAIR
    chunks, unused, own_rows, unused = out_ref.shape
    shift = ranges[0]
    picks = (
        lax.broadcasted_iota(jnp.int32, (8, width), 1) // HEAD_DIM
        == lax.broadcasted_iota(jnp.int32, (8, width), 0)
    ).astype(jnp.float32)

    def prepare(i, unused):
        rows = pl.ds(pl.multiple_of(i * size, size), size)
        product = g_ref[rows, :].astype(jnp.float32) * ctx_ref[rows, :].astype(jnp.float32)
        delta_ref[i] = lax.dot_general(
            picks,
            product,
            NT,
            preferred_element_type=jnp.float32,
            precision=lax.Precision.HIGHEST,
        )
        dq_ref[rows, :] = jnp.zeros((size, width), jnp.float32)
        return unused

    sums_ref[...] = jnp.zeros(sums_ref.shape, jnp.float32)
    lax.fori_loop(0, blocks, prepare, 0)

    def key_block(i, unused):
        rows = pl.ds(pl.multiple_of(i * size, size), size)
        own = col_ref[rows, :]
        dk_ref[...] = jnp.zeros((size, width), jnp.float32)
        dv_ref[...] = jnp.zeros((size, width), jnp.float32)

        def step(j, unused):
            place = lax.rem(j + blocks - shift, blocks)
            there = pl.ds(pl.multiple_of(place * size, size), size)
            same = own == row_ref[place]
            for pair in range(pairs):
                lanes = slice(pair * PAIR, (pair + 1) * PAIR)
                query = q_ref[there, lanes]
                grad = g_ref[there, lanes]
                keys = split_heads(k_ref[rows, lanes])
                values = split_heads(v_ref[rows, lanes])
                shares, slopes = [], []
                for h in range(2):
                    at = 2 * pair + h
                    s = lax.dot_general(
                        keys[h], query, NT, preferred_element_type=jnp.float32
                    )
                    s = jnp.where(same, s, NEGATIVE)
                    p = jnp.exp2(s - lse_ref[place, at : at + 1, :])
                    dp = lax.dot_general(
                        values[h], grad, NT, preferred_element_type=jnp.float32
                    )
                    shares.append(p.astype(jnp.bfloat16))
                    slopes.append(
                        (p * (dp - delta_ref[place, at : at + 1, :])).astype(jnp.bfloat16)
                    )
                dv_ref[:, lanes] += jnp.dot(
                    jnp.concatenate(shares, axis=1),
                    jnp.concatenate(split_heads(grad), axis=0),
                    preferred_element_type=jnp.float32,
                )
                dk_ref[:, lanes] += jnp.dot(
                    jnp.concatenate(slopes, axis=1),
                    jnp.concatenate(split_heads(query), axis=0),
                    preferred_element_type=jnp.float32,
                )
                dq_ref[there, lanes] += lax.dot_general(
                    jnp.concatenate(slopes, axis=0),
                    jnp.concatenate(keys, axis=0),
                    TN,
                    preferred_element_type=jnp.float32,
                )
            return unused

        lax.fori_loop(ranges[1 + 2 * i], ranges[2 + 2 * i], step, 0)
        per_chunk = own_rows // size
        chunk = lax.div(i, per_chunk)
        spot = pl.ds(pl.multiple_of(lax.rem(i, per_chunk) * size, size), size)
        out_ref[chunk, 1, spot, :] = (dk_ref[...] * LN_2).astype(jnp.bfloat16)
        out_ref[chunk, 2, spot, :] = dv_ref[...].astype(jnp.bfloat16)
        sums_ref[1:2, :] += jnp.sum(dv_ref[...], axis=0, keepdims=True)
        return unused

    lax.fori_loop(0, blocks, key_block, 0)
    for chunk in range(chunks):
        dq = dq_ref[pl.ds(chunk * own_rows, own_rows), :] * HEAD_DIM ** (-0.5)
        sums_ref[0:1, :] += jnp.sum(dq, axis=0, keepdims=True)
        out_ref[chunk, 0] = dq.astype(jnp.bfloat16)


def attend_back(
    joined, grad, context, lse, ranges, columns, rows_of, blocks, ways, tokens=()
):
    unused, total, width = joined.shape
    size = total // blocks
    wide = group_width(width)
    rows = total // ways
    whole = pl.BlockSpec((total, wide), lambda p, r: (0, p))
    grid_spec = pltpu.PrefetchScalarGridSpec(
        num_scalar_prefetch=1,
        grid=(width // wide,),
        in_specs=[
            pl.BlockSpec((None, total, wide), lambda p, r: (0, 0, p)),
            pl.BlockSpec((None, total, wide), lambda p, r: (1, 0, p)),
            pl.BlockSpec((None, total, wide), lambda p, r: (2, 0, p)),
            whole,
            whole,
            pl.BlockSpec((None,) + lse.shape[1:], lambda p, r: (p, 0, 0, 0)),
            pl.BlockSpec((total, 1), lambda p, r: (0, 0)),
            pl.BlockSpec((blocks, 1, size), lambda p, r: (0, 0, 0)),
        ]
        + [pl.BlockSpec(memory_space=pl.ANY)] * len(tokens),
        out_specs=[
            pl.BlockSpec((ways, 3, rows, wide), lambda p, r: (0, 0, 0, p)),
            pl.BlockSpec((8, wide), lambda p, r: (0, p)),
        ],
        scratch_shapes=[
            pltpu.VMEM((total, wide), jnp.float32),
            pltpu.VMEM((size, wide), jnp.float32),
            pltpu.VMEM((size, wide), jnp.float32),
            pltpu.VMEM((blocks, 8, size), jnp.float32),
        ],
    )
    return pl.pallas_call(
        after(functools.partial(attend_back_kernel, blocks), 9, tokens),
        grid_spec=grid_spec,
        out_shape=[
            jax.ShapeDtypeStruct((ways, 3, rows, width), jnp.bfloat16),
            jax.ShapeDtypeStruct((8, width), jnp.float32),
        ],
        compiler_params=params(48),
        cost_estimate=LIGHT,
    )(ranges, joined, joined, joined, grad, context, lse, columns, rows_of, *tokens)


class Layout:
    def __init__(self, dp, tensor):
        self.dp, self.tensor = dp, tensor
        self.paired = tensor == 2 and dp % 2 == 0
        self.ways = tensor

    def index(self):
        if self.paired:
            return lax.rem(lax.axis_index("dp"), 2)
        return lax.axis_index("tensor")

    def permute(self, values, target):
        pairs = []
        for place in range(self.dp * self.tensor):
            there = target(*divmod(place, self.tensor))
            if there != place:
                pairs.append((place, there))
        return lax.ppermute(values, ("dp", "tensor"), pairs)

    def stays(self):
        return lax.rem(lax.axis_index("dp"), 2) == lax.axis_index("tensor")

    def exchanged(self, values):
        return self.permute(values, lambda dp, tensor: (dp // 2 * 2 + tensor) * 2 + dp % 2)

    def swap(self, values):
        if not self.paired:
            return values
        return jnp.where(self.stays(), values, self.exchanged(values))

    def moved(self):
        return jnp.where(self.stays(), 0, 1).astype(jnp.int32).reshape(1)

    def across(self, values, bit):
        return self.permute(values, lambda dp, tensor: (dp ^ 2 * bit) * 2 + tensor)

    def chip_sum(self, mine, turn, tokens=()):
        chips = self.dp // 2
        bits = [1 << n for n in range(chips.bit_length() - 1)]
        if 1 << len(bits) != chips:
            return lax.psum(mine, "dp", axis_index_groups=self.groups())
        bits = bits[turn:] + bits[:turn]
        chip = lax.axis_index("dp") // 2
        for bit in bits:
            place = chip // bit % 2
            half = mine.shape[0] // 2
            given = self.across(
                lax.dynamic_slice_in_dim(mine, (1 - place) * half, half, 0), bit
            )
            mine = fold(mine, given, place, tokens)
            tokens = ()
        for bit in reversed(bits):
            given = self.across(mine, bit)
            mine = jnp.where(
                chip // bit % 2 == 0,
                jnp.concatenate([mine, given]),
                jnp.concatenate([given, mine]),
            )
        return mine

    def shift(self, values, step):
        if self.paired:
            return self.permute(values, lambda dp, tensor: (dp // 2 * 2 + (dp + step) % 2) * 2 + tensor)
        return self.permute(
            values, lambda dp, tensor: dp * self.tensor + (tensor + step) % self.tensor
        )

    def gather(self, values):
        return [values] + [self.shift(values, -step) for step in range(1, self.ways)]

    def send_home(self, buffer):
        return self.exchanged(buffer) if self.paired else None

    def combine(self, buffer, other, tokens=()):
        core = self.index()
        halves, rows, width = buffer.shape
        high = rows // 8
        moved = self.moved()

        def half(which, tokens):
            def place(m, n, f):
                return f[1] * 8 + m, n

            return choose(
                jnp.concatenate([moved, which.reshape(1)]),
                buffer.reshape(-1, width),
                place,
                other.reshape(-1, width),
                place,
                (rows, width),
                (high, width),
                tokens,
            )

        given = self.shift(half(1 - core, tokens), 1)
        return fold(half(core, tokens), given, core * 0)

    def groups(self):
        return [[2 * chip + at for chip in range(self.dp // 2)] for at in range(2)]

    def finish(self, mine):
        return mine, self.shift(mine, 1), self.index().reshape(1)

    def scatter(self, part):
        return [self.shift(part(k), k) for k in range(1, self.ways)]


def per_device(
    layout,
    frames,
    logit_grad,
    lengths,
    ln_gain,
    ln_bias,
    w_qkv,
    b_qv,
    w_out,
    b_out,
    w_up,
    b_up,
    w_down,
    b_down,
    w_head,
    b_head,
):
    ways = layout.ways
    rows, features = frames.shape
    total = rows * ways
    size = min(256, rows)
    blocks = total // size
    chunk_blocks = rows // size
    part = layout.index()
    swap = layout.swap

    low = frames.astype(jnp.bfloat16)
    came_frames = layout.exchanged(low) if layout.paired else low
    if layout.paired:
        low = jnp.where(layout.stays(), low, came_frames)
    stream = low.astype(jnp.float32)
    small = jnp.concatenate(
        [
            b_qv.reshape(-1),
            b_up.reshape(-1),
            w_head.reshape(-1),
            logit_grad.astype(jnp.bfloat16).reshape(-1),
        ]
    ).reshape(-1, 128)
    if layout.paired:
        came_small = layout.exchanged(small)
        small = jnp.where(layout.stays(), small, came_small)
    small = small.reshape(-1)
    lengths = swap(lengths)
    at = [b_qv.size, b_up.size, w_head.size, logit_grad.size]
    at = [sum(at[:n]) for n in range(5)]
    qv_biases = small[at[0] : at[1]].reshape(b_qv.shape).astype(jnp.float32)
    up_biases = small[at[1] : at[2]].reshape(b_up.shape).astype(jnp.float32)
    head_part = small[at[2] : at[3]].reshape(w_head.shape)
    logit_grad = small[at[3] : at[4]].reshape(logit_grad.shape)
    head_parts = layout.gather(head_part)
    head_all = jnp.roll(jnp.concatenate(head_parts), part * w_head.shape[0], axis=0)

    wide = w_qkv.shape[3]
    inner_width = w_up.shape[2]
    paired = layout.paired
    moved = layout.moved() if paired else None
    came_ffn = []
    if paired:
        own_qkv, own_out = w_qkv.reshape(-1, wide), w_out.reshape(-1, features)
        qkv_rows = 3 * features
        came_qkv = [layout.exchanged(w_qkv[0]).reshape(-1, wide)]
        came_out = [layout.exchanged(pick(own_out, 0, wide, (came_frames,)))]
        packs = [take(w_up, w_down, 0, (came_qkv[0], came_frames, came_small))]
        picked = packs[0]
        for layer in range(1, LAYERS):
            picked = pick(own_qkv, layer * qkv_rows, qkv_rows, (picked,))
            came_qkv.append(layout.exchanged(picked))
            picked = pick(own_out, layer * wide, wide, (picked,))
            came_out.append(layout.exchanged(picked))
    high = tile(wide, 512)

    def qkv_weight(layer):
        if not paired:
            return w_qkv[layer]
        blocks_in = 3 * features // high
        return choose(
            moved,
            w_qkv.reshape(-1, wide),
            lambda m, n, f: (layer * blocks_in + m, n),
            came_qkv[layer],
            lambda m, n, f: (m, n),
            (3 * features, wide),
            (high, wide),
        ).reshape(3, features, wide)

    def out_weight(layer, tokens):
        if not paired:
            return w_out[layer]
        return choose(
            moved,
            w_out.reshape(-1, features),
            lambda m, n, f: (layer * (wide // high) + m, n),
            came_out[layer],
            lambda m, n, f: (m, n),
            (wide, features),
            (high, features),
            tokens,
        )

    def up_weight(layer, tokens):
        if not paired:
            return w_up[layer]
        rows_in = features // high
        return choose(
            moved,
            w_up.reshape(-1, inner_width),
            lambda m, n, f: (layer * rows_in + m, n),
            came_ffn[layer],
            lambda m, n, f: (n * rows_in + m, 0),
            (features, inner_width),
            (high, features),
            tokens,
        )

    def down_weight(layer, tokens):
        if not paired:
            return w_down[layer]
        rows_in = inner_width // high
        return choose(
            moved,
            w_down.reshape(-1, features),
            lambda m, n, f: (layer * rows_in + m, n),
            came_ffn[layer],
            lambda m, n, f: (rows_in + m, n),
            (inner_width, features),
            (high, features),
            tokens,
        )

    qkv_weights, out_weights, up_weights, down_weights = [], [], [], []
    positions = lax.rem(jnp.arange(total, dtype=jnp.int32) + part * rows, total)
    ends = jnp.cumsum(lengths[0])
    segment = jnp.sum((positions[:, None] >= ends[None, :]).astype(jnp.int32), axis=1)
    own_valid = positions[:rows] < ends[-1]
    columns = segment[:, None]
    rows_of = segment.reshape(blocks, 1, size)
    firsts = positions.reshape(blocks, size)[:, :1]
    lows = jnp.max(jnp.where(ends[None, :] <= firsts, ends[None, :], 0), axis=1) // size
    lasts = firsts + (size - 1)
    highs = jnp.min(jnp.where(ends[None, :] > lasts, ends[None, :], total), axis=1)
    highs = (highs + size - 1) // size
    ranges = jnp.concatenate(
        [(part * chunk_blocks).reshape(1), jnp.stack([lows, highs], axis=1).reshape(-1)]
    ).astype(jnp.int32)
    gains = ln_gain.astype(jnp.float32)
    shifts = ln_bias.astype(jnp.float32)

    def chunk(values, k):
        return values[k * rows : (k + 1) * rows]

    saved = []
    normed = layer_norm(stream, gains[0, 0], shifts[0, 0]).astype(jnp.bfloat16)
    for layer in range(LAYERS):
        last = layer + 1 == LAYERS
        normed_all = layout.gather(normed)
        bias = jnp.stack(
            [qv_biases[layer, 0], jnp.zeros_like(qv_biases[layer, 0]), qv_biases[layer, 1]]
        )[:, None, :]
        qkv_weights.append(qkv_weight(layer))
        joined = None
        for k in range(ways):
            joined = project(normed_all[k], qkv_weights[layer], bias, k, ways, joined)
        context, lse = attend(
            joined, ranges, columns, rows_of, blocks
        )
        chunks = context.reshape(ways, rows, -1)
        if paired:
            came_ffn.append(layout.exchanged(packs[layer]))
        out_weights.append(out_weight(layer, (context,)))
        up_weights.append(up_weight(layer, (context,)))
        down_weights.append(down_weight(layer, (context,)))
        weight = out_weights[layer]
        received = layout.scatter(
            lambda k: times(chunks, (k,), weight, NN, tokens=(up_weights[layer],))
        )
        middle, normed_ffn = join(
            chunks,
            (0,),
            weight,
            stream,
            b_out[layer].astype(jnp.float32),
            gains[layer, 1],
            shifts[layer, 1],
            received,
        )
        ffn_all = layout.gather(normed_ffn)
        hidden, slopes = [], []
        for k in range(ways):
            one, other = gelu_up(ffn_all[k], up_weights[layer], up_biases[layer][None, :])
            hidden.append(one)
            slopes.append(other)
        if paired and not last:
            packs.append(take(w_up, w_down, layer + 1, (hidden[-1],)))
        weight = down_weights[layer]
        received = layout.scatter(lambda k: times(hidden[k], (), weight, NN))
        saved.append(
            (stream, middle, normed_all, joined, context, lse, ffn_all, hidden, slopes)
        )
        following = (layer + 1) % LAYERS
        ended = join(
            hidden[0],
            (),
            weight,
            middle,
            b_down[layer].astype(jnp.float32),
            gains[following, 0],
            shifts[following, 0],
            received,
            last,
        )
        if last:
            final_low = ended[0]
        else:
            stream, normed = ended

    logits = swap((matmul(final_low, head_all) + b_head.astype(jnp.float32)))
    grad_logits = jnp.where(own_valid[:, None], logit_grad, 0.0).astype(jnp.bfloat16)
    head_grad = inner_rows(final_low, grad_logits)
    head_bias_grad = column_sums(grad_logits)
    grad_stream = outer_cols(grad_logits, head_all)

    tiles = features // wide
    inner_tiles = inner_width // wide
    ffn_shape = (2, features * inner_tiles + FFN_SMALL, wide)
    attn_shape = (2, 2 * features + ATTN_SMALL, wide)

    def shares(vectors):
        matrix = jnp.stack(vectors)

        def share(k):
            return lax.dynamic_slice_in_dim(matrix, lax.rem(part + k, ways) * wide, wide, 1)

        received = layout.scatter(lambda k: share(k).astype(jnp.bfloat16))
        return share(0) + sum(values.astype(jnp.float32) for values in received)

    def with_small(buffer, lines):
        lines = jnp.pad(lines, ((0, -lines.shape[0] % 16), (0, 0))).astype(jnp.bfloat16)
        first = buffer.shape[1] // features * features
        return lax.dynamic_update_slice(buffer, lines[None], (0, first, 0))

    head_lines = [
        head_grad.T,
        jnp.pad(head_bias_grad.reshape(ways, -1), ((0, 0), (0, wide - b_head.shape[0] // ways))).reshape(
            1, features
        ),
    ]
    low = grad_stream.astype(jnp.bfloat16)
    bias_down = column_sums(low)
    outputs = [None] * 4
    smalls = {}
    joined_rows = 3 * features
    every = range(ways)

    def unpack_ffn(layer, one, two, flag):
        smalls["ffn", layer] = (one, two, flag)
        outputs[0] = unpack(
            one, two, flag, 0, features, inner_tiles, layer, outputs[0], features, 0
        )
        outputs[1] = unpack(
            two, one, flag, 0, inner_width, tiles, layer, outputs[1], inner_width, 0
        )

    def unpack_attn(layer, one, two, flag):
        smalls["attn", layer] = (one, two, flag)
        outputs[2] = unpack(
            one, two, flag, 0, 2 * features, 1, layer, outputs[2], joined_rows, 0
        )
        outputs[2] = unpack(
            two, one, flag, 0, features, 1, layer, outputs[2], joined_rows, 2 * features
        )
        outputs[3] = unpack(
            two, one, flag, features, wide, tiles, layer, outputs[3], wide, 0
        )

    buffers = {}
    mines = {}
    for layer in reversed(range(LAYERS)):
        above = layer + 1
        top = above == LAYERS
        stream_in, middle, normed_all, joined, context, lse, ffn_all, hidden, slopes = saved[
            layer
        ]
        low_all = layout.gather(low)
        inner, inner_sums = [], []
        for k in every:
            tokens = ()
            if paired and not top:
                tokens = (mines["ffn", above],)
            one, other = inner_grad(low_all[k], down_weights[layer], slopes[k], tokens)
            inner.append(one)
            inner_sums.append(other)
        weight = up_weights[layer]
        received = layout.scatter(lambda k: times(inner[k], (), weight, NT))
        grad_middle, middle_low, norm_sums = norm_back(
            [(inner[0], ())], weight, middle, grad_stream, gains[layer, 1], received
        )
        bias_up = sum(inner_sums)
        bias_out = norm_sums[2]
        lines = [bias_down, norm_sums[0], norm_sums[1]]
        if top:
            lines += list(head_lines[0]) + list(head_lines[1])
        lines = jnp.concatenate([bias_up.reshape(inner_tiles, wide), shares(lines)])
        tokens = (lines,)
        if paired and not top:
            mines["attn", above] = layout.combine(*buffers["attn", above], (grad_middle,))
            tokens += (mines["attn", above],)
        buffer = weight_grad(
            [(hidden[k], ()) for k in every],
            [(low_all[k], ()) for k in every],
            None,
            ffn_shape,
            lambda g, n: (1, n * inner_width),
            tokens,
        )
        buffer = weight_grad(
            [(ffn_all[k], ()) for k in every],
            [(inner[k], ()) for k in every],
            buffer,
            ffn_shape,
            lambda g, n: (0, n * features),
        )
        buffer = with_small(buffer, lines)
        buffers["ffn", layer] = (buffer, layout.send_home(buffer))

        low_all = layout.gather(middle_low)
        grad_context = None
        for k in every:
            grad_context = times(
                low_all[k], (), out_weights[layer], NT, k, ways, grad_context
            )
        grads, qkv_sums = attend_back(
            joined,
            grad_context,
            context,
            lse,
            ranges,
            columns,
            rows_of,
            blocks,
            ways,
            (buffer,),
        )
        buffer = weight_grad(
            [(context.reshape(ways, rows, -1), (k,)) for k in every],
            [(low_all[k], ()) for k in every],
            None,
            attn_shape,
            lambda g, n: (1, features + n * wide),
        )
        weight = qkv_weights[layer]
        received = layout.scatter(lambda k: times_kinds(grads, k, weight))
        grad_stream, low, norm_sums = norm_back(
            [(grads, (0, kind)) for kind in range(3)],
            weight,
            stream_in,
            grad_middle,
            gains[layer, 0],
            received,
        )
        tokens = ()
        if paired and not top:
            tokens = (scattered,)
        buffer = weight_grad(
            [(normed_all[k], ()) for k in every],
            [(grads, (k, None)) for k in every],
            buffer,
            attn_shape,
            lambda g, n: (g // 2, g % 2 * features),
            tokens,
        )
        norm_sums = pick(norm_sums, 0, norm_sums.shape[0], (buffer,))
        lines = jnp.concatenate([qkv_sums[:2], shares([bias_out, norm_sums[0], norm_sums[1]])])
        bias_down = norm_sums[2]
        buffer = with_small(buffer, lines)
        buffers["attn", layer] = (buffer, layout.send_home(buffer))
        if paired:
            mines["ffn", layer] = layout.combine(*buffers["ffn", layer], (grad_stream,))
            if top:
                scattered = lax.psum_scatter(
                    mines["ffn", layer],
                    "dp",
                    scatter_dimension=0,
                    axis_index_groups=layout.groups(),
                    tiled=True,
                )

    if paired:
        whole = lax.all_gather(
            scattered, "dp", axis=0, axis_index_groups=layout.groups(), tiled=True
        )
        unpack_ffn(LAYERS - 1, *layout.finish(whole))
        for layer in range(1, LAYERS):
            unpack_attn(
                layer,
                *layout.finish(
                    lax.psum(mines["attn", layer], "dp", axis_index_groups=layout.groups())
                ),
            )
        mine = mines["ffn", 0]
        half_rows = mine.shape[0] // 2
        halves = [
            layout.chip_sum(mine[n * half_rows : (n + 1) * half_rows], n) for n in range(2)
        ]
        mine = layout.combine(*buffers["attn", 0])
        attn = layout.finish(layout.chip_sum(mine, 0, tuple(outputs)))
        unpack_ffn(0, *layout.finish(jnp.concatenate(halves)))
        unpack_attn(0, *attn)
    else:
        flag = jnp.zeros((1,), jnp.int32)
        for layer in reversed(range(LAYERS)):
            summed = lax.psum(buffers["ffn", layer][0], "dp")
            unpack_ffn(layer, summed[0], summed[1], flag)
            summed = lax.psum(buffers["attn", layer][0], "dp")
            unpack_attn(layer, summed[0], summed[1], flag)

    input_grad = swap(low).astype(jnp.float32)

    grad_qkv = outputs[2].reshape(LAYERS, 3, features, wide)

    def lines_of(kind, layer):
        one, two, flag = smalls[kind, layer]
        first = one.shape[0] // features * features
        return jnp.where(flag[0] == 0, one[first:], two[first:]).astype(jnp.float32)

    ffn_lines = [lines_of("ffn", layer) for layer in range(LAYERS)]
    attn_lines = [lines_of("attn", layer) for layer in range(LAYERS)]
    t = inner_tiles
    bias_up = jnp.stack([lines[:t].reshape(-1) for lines in ffn_lines])
    bias_down = jnp.stack([lines[t] for lines in ffn_lines])
    bias_qv = jnp.stack([lines[:2] for lines in attn_lines])
    bias_out = jnp.stack([lines[2] for lines in attn_lines])
    gain = jnp.stack(
        [jnp.stack([attn_lines[layer][3], ffn_lines[layer][t + 1]]) for layer in range(LAYERS)]
    )
    shift = jnp.stack(
        [jnp.stack([attn_lines[layer][4], ffn_lines[layer][t + 2]]) for layer in range(LAYERS)]
    )
    vocab = b_head.shape[0]
    head_weight = ffn_lines[-1][t + 3 : t + 3 + vocab].T
    head_bias = ffn_lines[-1][t + 3 + vocab, : vocab // ways]
    return (
        logits,
        input_grad,
        gain,
        shift,
        grad_qkv,
        bias_qv,
        outputs[3],
        bias_out,
        outputs[0],
        bias_up,
        outputs[1],
        bias_down,
        head_weight,
        head_bias,
    )


def solution(mesh):
    layout = Layout(mesh.shape["dp"], mesh.shape["tensor"])
    by_rows = P(("dp", "tensor"), None)
    placed = (
        by_rows,
        by_rows,
        P("dp", None),
        P(),
        P(),
        P(None, None, None, "tensor"),
        P(None, None, "tensor"),
        P(None, "tensor", None),
        P(),
        P(None, None, "tensor"),
        P(None, "tensor"),
        P(None, "tensor", None),
        P(),
        P("tensor", None),
        P(),
    )
    return jax.shard_map(
        functools.partial(per_device, layout),
        mesh=mesh,
        in_specs=placed,
        out_specs=(
            by_rows,
            by_rows,
            P(None, None, "tensor"),
            P(None, None, "tensor"),
            P(None, None, None, "tensor"),
            P(None, None, "tensor"),
            P(None, "tensor", None),
            P(None, "tensor"),
            P(None, None, "tensor"),
            P(None, "tensor"),
            P(None, "tensor", None),
            P(None, "tensor"),
            P("tensor", None),
            P("tensor"),
        ),
        check_vma=False,
    )
```

```python
import functools

import jax
import jax.numpy as jnp
from jax import lax
from jax.experimental import pallas as pl
from jax.experimental.pallas import tpu as pltpu
from jax.sharding import PartitionSpec as P

HEAD_DIM = 64
LAYERS = 2
EPSILON = 1e-05
PAIR = 2 * HEAD_DIM
NEGATIVE = -1e30
FFN_SMALL = 256
ATTN_SMALL = 128
LOG2_E = 1.4426950408889634
LN_2 = 0.6931471805599453
MIB = 1 << 20
NN = (((1,), (0,)), ((), ()))
NT = (((1,), (1,)), ((), ()))
TN = (((0,), (0,)), ((), ()))


def layer_norm(values, gain, shift):
    mean = jnp.mean(values, axis=-1, keepdims=True)
    centred = values - mean
    spread = jnp.mean(centred * centred, axis=-1, keepdims=True)
    return centred * lax.rsqrt(spread + EPSILON) * gain + shift


def matmul(left, right):
    return jnp.dot(left, right, preferred_element_type=jnp.float32)


def outer_cols(left, right):
    return lax.dot_general(left, right, NT, preferred_element_type=jnp.float32)


def inner_rows(left, right):
    return lax.dot_general(left, right, TN, preferred_element_type=jnp.float32)


def column_sums(values):
    return jnp.sum(values, axis=0, dtype=jnp.float32)


def tile(size, limit):
    return size if size <= limit else limit


LIGHT = pl.CostEstimate(flops=0, bytes_accessed=0, transcendentals=0)


def after(kernel, first, tokens):
    return lambda *refs: kernel(*refs[:first], *refs[first + len(tokens) :])


def params(mib):
    return pltpu.CompilerParams(vmem_limit_bytes=mib * MIB)


def project_kernel(x_ref, w_ref, b_ref, *rest):
    out_ref = rest[-1]
    gain = jnp.where(pl.program_id(0) == 0, HEAD_DIM ** (-0.5) * LOG2_E, 1.0)
    value = jnp.dot(x_ref[...], w_ref[...], preferred_element_type=jnp.float32)
    out_ref[...] = ((value + b_ref[...]) * gain).astype(jnp.bfloat16)


def project(x, weight, bias, chunk, ways, joined):
    rows, depth = x.shape
    kinds, unused, width = weight.shape
    wide = tile(width, 512)
    in_specs = [
        pl.BlockSpec((rows, depth), lambda k, n: (0, 0)),
        pl.BlockSpec((None, depth, wide), lambda k, n: (k, 0, n)),
        pl.BlockSpec((None, 1, wide), lambda k, n: (k, 0, n)),
    ]
    args = [x, weight, bias]
    aliases = {}
    if joined is not None:
        in_specs.append(pl.BlockSpec(memory_space=pl.ANY))
        args.append(joined)
        aliases = {3: 0}
    return pl.pallas_call(
        project_kernel,
        grid=(kinds, width // wide),
        in_specs=in_specs,
        out_specs=pl.BlockSpec((None, rows, wide), lambda k, n: (k, chunk, n)),
        out_shape=jax.ShapeDtypeStruct((kinds, rows * ways, width), jnp.bfloat16),
        input_output_aliases=aliases,
        compiler_params=params(32),
        cost_estimate=LIGHT,
    )(*args)


ERF_STEP = 0.3275911
ERF_TERMS = (0.254829592, -0.284496736, 1.421413741, -1.453152027, 1.061405429)


def gelu_kernel(sub, x_ref, w_ref, b_ref, hidden_ref, slope_ref):
    for start in range(0, x_ref.shape[0], sub):
        rows = pl.ds(start, sub)
        u = (
            jnp.dot(x_ref[rows, :], w_ref[...], preferred_element_type=jnp.float32)
            + b_ref[...]
        )
        density = jnp.exp(u * u * -0.5)
        t = 1.0 / (1.0 + (ERF_STEP * 0.5**0.5) * jnp.abs(u))
        poly = ERF_TERMS[4]
        for term in ERF_TERMS[3::-1]:
            poly = poly * t + term
        tail = (0.5 * poly) * t * density
        phi = jnp.where(u < 0.0, tail, 1.0 - tail)
        hidden_ref[rows, :] = (u * phi).astype(jnp.bfloat16)
        slope_ref[rows, :] = (phi + u * density * 0.3989422804014327).astype(jnp.bfloat16)


def gelu_up(x, weight, bias):
    rows, depth = x.shape
    width = weight.shape[1]
    wide = tile(width, 512)
    out = jax.ShapeDtypeStruct((rows, width), jnp.bfloat16)
    return pl.pallas_call(
        functools.partial(gelu_kernel, tile(rows, 256)),
        grid=(width // wide,),
        in_specs=[
            pl.BlockSpec((rows, depth), lambda n: (0, 0)),
            pl.BlockSpec((depth, wide), lambda n: (0, n)),
            pl.BlockSpec((1, wide), lambda n: (0, n)),
        ],
        out_specs=[pl.BlockSpec((rows, wide), lambda n: (0, n))] * 2,
        out_shape=[out, out],
        compiler_params=params(32),
        cost_estimate=LIGHT,
    )(x, weight, bias)


def times_kernel(dims, x_ref, w_ref, *rest):
    rest[-1][...] = lax.dot_general(
        x_ref[...], w_ref[...], dims, preferred_element_type=jnp.float32
    ).astype(jnp.bfloat16)


def row_spec(array, lead, high):
    return pl.BlockSpec(
        (None,) * len(lead) + (high, array.shape[-1]), lambda m: lead + (m, 0)
    )


def whole_spec(array):
    return pl.BlockSpec(array.shape, lambda m: (0,) * array.ndim)


def times(x, lead, weight, dims, chunk=0, chunks=1, buffer=None, tokens=()):
    rows = x.shape[-2]
    width = weight.shape[0] if dims == NT else weight.shape[1]
    high = tile(rows, 256)
    in_specs = [row_spec(x, lead, high), whole_spec(weight)]
    args = [x, weight]
    aliases = {}
    if buffer is not None:
        aliases = {2: 0}
        in_specs.append(pl.BlockSpec(memory_space=pl.ANY))
        args.append(buffer)
    in_specs += [pl.BlockSpec(memory_space=pl.ANY)] * len(tokens)
    args += tokens
    return pl.pallas_call(
        functools.partial(times_kernel, dims),
        grid=(rows // high,),
        in_specs=in_specs,
        out_specs=pl.BlockSpec((high, width), lambda m: (chunk * (rows // high) + m, 0)),
        out_shape=jax.ShapeDtypeStruct((rows * chunks, width), jnp.bfloat16),
        input_output_aliases=aliases,
        compiler_params=params(40),
        cost_estimate=LIGHT,
    )(*args)


def kinds_kernel(x_ref, w_ref, out_ref):
    total = lax.dot_general(x_ref[0], w_ref[0], NT, preferred_element_type=jnp.float32)
    for kind in range(1, w_ref.shape[0]):
        total += lax.dot_general(
            x_ref[kind], w_ref[kind], NT, preferred_element_type=jnp.float32
        )
    out_ref[...] = total.astype(jnp.bfloat16)


def times_kinds(x, chunk, weight):
    kinds, rows, width = x.shape[1:]
    features = weight.shape[1]
    high = tile(rows, 256)
    return pl.pallas_call(
        kinds_kernel,
        grid=(rows // high,),
        in_specs=[
            pl.BlockSpec((None, kinds, high, width), lambda m: (chunk, 0, m, 0)),
            whole_spec(weight),
        ],
        out_specs=pl.BlockSpec((high, features), lambda m: (m, 0)),
        out_shape=jax.ShapeDtypeStruct((rows, features), jnp.bfloat16),
        compiler_params=params(40),
        cost_estimate=LIGHT,
    )(x, weight)


def join_kernel(count, last, x_ref, w_ref, res_ref, bias_ref, gain_ref, shift_ref, *rest):
    received, outs = rest[:count], rest[count:]
    value = jnp.dot(x_ref[...], w_ref[...], preferred_element_type=jnp.float32)
    for ref in received:
        value += ref[...].astype(jnp.float32)
    value += res_ref[...] + bias_ref[...]
    if last:
        outs[0][...] = value.astype(jnp.bfloat16)
    else:
        outs[0][...] = value
        outs[1][...] = layer_norm(value, gain_ref[...], shift_ref[...]).astype(jnp.bfloat16)


def join(x, lead, weight, residual, bias, gain, shift, received, last=False):
    rows, features = residual.shape
    high = tile(rows, 256)
    block = pl.BlockSpec((high, features), lambda m: (m, 0))
    vector = pl.BlockSpec((1, features), lambda m: (0, 0))
    low = jax.ShapeDtypeStruct(residual.shape, jnp.bfloat16)
    full = jax.ShapeDtypeStruct(residual.shape, jnp.float32)
    return pl.pallas_call(
        functools.partial(join_kernel, len(received), last),
        grid=(rows // high,),
        in_specs=[row_spec(x, lead, high), whole_spec(weight), block, vector, vector, vector]
        + [block] * len(received),
        out_specs=[block] if last else [block, block],
        out_shape=[low] if last else [full, low],
        compiler_params=params(40),
        cost_estimate=LIGHT,
    )(x, weight, residual, bias[None], gain[None], shift[None], *received)


def inner_kernel(sub, d_ref, w_ref, slope_ref, out_ref, sums_ref):
    sums = jnp.zeros(sums_ref.shape, jnp.float32)
    for start in range(0, d_ref.shape[0], sub):
        rows = pl.ds(start, sub)
        value = lax.dot_general(
            d_ref[rows, :], w_ref[...], NT, preferred_element_type=jnp.float32
        )
        value = (value * slope_ref[rows, :].astype(jnp.float32)).astype(jnp.bfloat16)
        out_ref[rows, :] = value
        sums += jnp.sum(value.astype(jnp.float32), axis=0, keepdims=True)
    sums_ref[...] = sums


def inner_grad(d, weight, slope, tokens=()):
    rows, features = d.shape
    width = weight.shape[0]
    wide = tile(width, 512)
    column = pl.BlockSpec((rows, wide), lambda n: (0, n))
    return pl.pallas_call(
        after(functools.partial(inner_kernel, tile(rows, 256)), 3, tokens),
        grid=(width // wide,),
        in_specs=[
            pl.BlockSpec((rows, features), lambda n: (0, 0)),
            pl.BlockSpec((wide, features), lambda n: (n, 0)),
            column,
        ]
        + [pl.BlockSpec(memory_space=pl.ANY)] * len(tokens),
        out_specs=[column, pl.BlockSpec((1, wide), lambda n: (0, n))],
        out_shape=[
            jax.ShapeDtypeStruct((rows, width), jnp.bfloat16),
            jax.ShapeDtypeStruct((1, width), jnp.float32),
        ],
        compiler_params=params(40),
        cost_estimate=LIGHT,
    )(d, weight, slope, *tokens)


def back_kernel(kinds, count, *refs):
    xs, ws = refs[:kinds], refs[kinds]
    value_ref, grad_ref, gain_ref = refs[kinds + 1 : kinds + 4]
    received = refs[kinds + 4 : kinds + 4 + count]
    full_ref, low_ref, sums_ref = refs[kinds + 4 + count :]
    if kinds == 1:
        weights = [ws[...]]
    else:
        weights = [ws[k] for k in range(kinds)]
    given = lax.dot_general(xs[0][...], weights[0], NT, preferred_element_type=jnp.float32)
    for k in range(1, kinds):
        given += lax.dot_general(xs[k][...], weights[k], NT, preferred_element_type=jnp.float32)
    for ref in received:
        given += ref[...].astype(jnp.float32)
    values = value_ref[...]
    centred = values - jnp.mean(values, axis=-1, keepdims=True)
    scale = lax.rsqrt(jnp.mean(centred * centred, axis=-1, keepdims=True) + EPSILON)
    unit = centred * scale
    inward = given * gain_ref[...]
    mean = jnp.mean(inward, axis=-1, keepdims=True)
    along = jnp.mean(inward * unit, axis=-1, keepdims=True)
    full = grad_ref[...] + scale * (inward - mean - unit * along)
    low = full.astype(jnp.bfloat16)
    full_ref[...] = full
    low_ref[...] = low

    @pl.when(pl.program_id(0) == 0)
    def _():
        sums_ref[...] = jnp.zeros(sums_ref.shape, jnp.float32)

    sums_ref[0:1, :] += jnp.sum(given * unit, axis=0, keepdims=True)
    sums_ref[1:2, :] += jnp.sum(given, axis=0, keepdims=True)
    sums_ref[2:3, :] += jnp.sum(low.astype(jnp.float32), axis=0, keepdims=True)


def norm_back(xs, weight, values, grad, gain, received):
    rows, features = values.shape
    high = tile(rows, 256)
    block = pl.BlockSpec((high, features), lambda m: (m, 0))
    return pl.pallas_call(
        functools.partial(back_kernel, len(xs), len(received)),
        grid=(rows // high,),
        in_specs=[row_spec(x, lead, high) for x, lead in xs]
        + [whole_spec(weight), block, block, pl.BlockSpec((1, features), lambda m: (0, 0))]
        + [block] * len(received),
        out_specs=[block, block, pl.BlockSpec((8, features), lambda m: (0, 0))],
        out_shape=[
            jax.ShapeDtypeStruct(values.shape, jnp.float32),
            jax.ShapeDtypeStruct(values.shape, jnp.bfloat16),
            jax.ShapeDtypeStruct((8, features), jnp.float32),
        ],
        compiler_params=params(48),
        cost_estimate=LIGHT,
    )(*[x for x, unused in xs], weight, values, grad, gain[None], *received)


def weight_kernel(chunks, *refs):
    x_refs, d_refs = refs[:chunks], refs[chunks : 2 * chunks]
    out_ref, turned = refs[-2:]

    @pl.when((pl.program_id(1) == 0) & (pl.program_id(2) == 0))
    def _():
        for k in range(chunks):
            turned[k] = x_refs[k][...].T

    total = jnp.dot(turned[0], d_refs[0][...], preferred_element_type=jnp.float32)
    for k in range(1, chunks):
        total += jnp.dot(turned[k], d_refs[k][...], preferred_element_type=jnp.float32)
    out_ref[...] = total.astype(jnp.bfloat16)


def weight_grad(xs, ds, buffer, shape, place, tokens=()):
    chunks = len(xs)
    rows, tall = xs[0][0].shape[-2:]
    width = ds[0][0].shape[-1]
    kinds = 1
    if None in ds[0][1]:
        kinds = ds[0][0].shape[ds[0][1].index(None)]
    high, wide = tile(tall, 512), shape[2]

    def x_spec(lead):
        return pl.BlockSpec(
            (None,) * len(lead) + (rows, high), lambda m, g, n: lead + (0, m)
        )

    def d_spec(lead):
        return pl.BlockSpec(
            (None,) * len(lead) + (rows, wide),
            lambda m, g, n: tuple(g if at is None else at for at in lead) + (0, n),
        )

    def out_index(m, g, n):
        half, row = place(g, n)
        return half, row // high + m, 0

    in_specs = [x_spec(lead) for unused, lead in xs] + [d_spec(lead) for unused, lead in ds]
    args = [array for array, unused in xs] + [array for array, unused in ds]
    aliases = {}
    if buffer is not None:
        aliases = {len(args): 0}
        in_specs.append(pl.BlockSpec(memory_space=pl.ANY))
        args.append(buffer)
    in_specs += [pl.BlockSpec(memory_space=pl.ANY)] * len(tokens)
    args += tokens
    return pl.pallas_call(
        functools.partial(weight_kernel, chunks),
        grid=(tall // high, kinds, width // wide),
        in_specs=in_specs,
        out_specs=pl.BlockSpec((None, high, wide), out_index),
        out_shape=jax.ShapeDtypeStruct(shape, jnp.bfloat16),
        scratch_shapes=[pltpu.VMEM((chunks, high, rows), jnp.bfloat16)],
        input_output_aliases=aliases,
        compiler_params=params(40),
        cost_estimate=LIGHT,
    )(*args)


def choose_kernel(flag, own_ref, other_ref, out_ref):
    out_ref[...] = jnp.where(flag[0] == 0, own_ref[...], other_ref[...])


def choose(flag, own, own_place, other, other_place, shape, block, tokens=()):
    def spec(which, place):
        def index(m, n, f):
            here = jnp.where(f[0] == which, 1, 0)
            row, column = place(m, n, f)
            return here * row, here * column

        return pl.BlockSpec(block, index)

    return pl.pallas_call(
        after(choose_kernel, 3, tokens),
        grid_spec=pltpu.PrefetchScalarGridSpec(
            num_scalar_prefetch=1,
            grid=(shape[0] // block[0], shape[1] // block[1]),
            in_specs=[spec(0, own_place), spec(1, other_place)]
            + [pl.BlockSpec(memory_space=pl.ANY)] * len(tokens),
            out_specs=pl.BlockSpec(block, lambda m, n, f: (m, n)),
        ),
        out_shape=jax.ShapeDtypeStruct(shape, jnp.bfloat16),
        compiler_params=params(32),
        cost_estimate=LIGHT,
    )(flag, own, other, *tokens)


def copy_kernel(in_ref, out_ref):
    out_ref[...] = in_ref[...]


def pick(values, first, rows, tokens):
    width = values.shape[1]
    high = tile(rows, 512)
    return pl.pallas_call(
        after(copy_kernel, 1, tokens),
        grid=(rows // high,),
        in_specs=[pl.BlockSpec((high, width), lambda m: (first // high + m, 0))]
        + [pl.BlockSpec(memory_space=pl.ANY)] * len(tokens),
        out_specs=pl.BlockSpec((high, width), lambda m: (m, 0)),
        out_shape=jax.ShapeDtypeStruct((rows, width), values.dtype),
        compiler_params=params(16),
        cost_estimate=LIGHT,
    )(values, *tokens)


def take_kernel(count, up_ref, down_ref, out_ref):
    out_ref[...] = jnp.where(pl.program_id(0) < count, up_ref[...], down_ref[...])


def take(w_up, w_down, layer, tokens=()):
    features, inner = w_up.shape[1:]
    high = tile(features, 512)
    rows, down = features // high, inner // high
    ups = rows * (inner // features)

    def up_index(m):
        here = jnp.minimum(m, ups - 1)
        return layer, here % rows, here // rows

    return pl.pallas_call(
        after(functools.partial(take_kernel, ups), 2, tokens),
        grid=(ups + down,),
        in_specs=[
            pl.BlockSpec((None, high, features), up_index),
            pl.BlockSpec((None, high, features), lambda m: (layer, jnp.maximum(m - ups, 0), 0)),
        ]
        + [pl.BlockSpec(memory_space=pl.ANY)] * len(tokens),
        out_specs=pl.BlockSpec((high, features), lambda m: (m, 0)),
        out_shape=jax.ShapeDtypeStruct((2 * inner, features), jnp.bfloat16),
        compiler_params=params(32),
        cost_estimate=LIGHT,
    )(w_up, w_down, *tokens)


def fold_kernel(place, mine_ref, given_ref, out_ref):
    out_ref[...] = (
        mine_ref[...].astype(jnp.float32) + given_ref[...].astype(jnp.float32)
    ).astype(jnp.bfloat16)


def fold(mine, given, place, tokens=()):
    rows, width = given.shape
    block = (rows, width)
    return pl.pallas_call(
        after(fold_kernel, 3, tokens),
        grid_spec=pltpu.PrefetchScalarGridSpec(
            num_scalar_prefetch=1,
            grid=(1,),
            in_specs=[
                pl.BlockSpec(block, lambda m, p: (p[0], 0)),
                pl.BlockSpec(block, lambda m, p: (0, 0)),
            ]
            + [pl.BlockSpec(memory_space=pl.ANY)] * len(tokens),
            out_specs=pl.BlockSpec(block, lambda m, p: (0, 0)),
        ),
        out_shape=jax.ShapeDtypeStruct(block, jnp.bfloat16),
        compiler_params=params(32),
        cost_estimate=LIGHT,
    )(place.astype(jnp.int32).reshape(1), mine, given, *tokens)


def unpack_kernel(flag, one_ref, two_ref, *rest):
    rest[-1][...] = jnp.where(flag[0] == 0, one_ref[...], two_ref[...]).astype(jnp.float32)


def unpack(one, two, flag, first, tall, tiles, layer, output, out_rows, out_first):
    wide = one.shape[1]
    high = tile(tall, 1024)
    skip = first // high

    def spec(which):
        def index(m, n, f):
            here = jnp.where(f[0] == which, 1, 0)
            return here * (skip + n * (tall // high) + m), 0

        return pl.BlockSpec((high, wide), index)

    args = [flag, one, two]
    in_specs = [spec(0), spec(1)]
    aliases = {}
    if output is not None:
        aliases = {3: 0}
        in_specs.append(pl.BlockSpec(memory_space=pl.ANY))
        args.append(output)
    return pl.pallas_call(
        unpack_kernel,
        grid_spec=pltpu.PrefetchScalarGridSpec(
            num_scalar_prefetch=1,
            grid=(tall // high, tiles),
            in_specs=in_specs,
            out_specs=pl.BlockSpec(
                (None, high, wide), lambda m, n, f: (layer, out_first // high + m, n)
            ),
        ),
        out_shape=jax.ShapeDtypeStruct((LAYERS, out_rows, tiles * wide), jnp.float32),
        input_output_aliases=aliases,
        compiler_params=params(32),
        cost_estimate=LIGHT,
    )(*args)


def head_lanes(shape):
    return lax.broadcasted_iota(jnp.int32, shape, 1) < HEAD_DIM


def split_heads(values):
    first = head_lanes(values.shape)
    zero = jnp.zeros_like(values)
    return jnp.where(first, values, zero), jnp.where(first, zero, values)


def attend_kernel(
    blocks, ranges, q_ref, k_ref, v_ref, col_ref, row_ref, ctx_ref, lse_ref, tops, sums, totals
):
    i = pl.program_id(0)
    size, width = q_ref.shape
    heads = width // HEAD_DIM
    pairs = width // PAIR
    groups, group_heads, unused = lse_ref.shape
    shift = ranges[0]
    low, high = ranges[1 + 2 * i], ranges[2 + 2 * i]
    own = row_ref[i]
    tops[...] = jnp.full(tops.shape, NEGATIVE, jnp.float32)
    sums[...] = jnp.zeros(sums.shape, jnp.float32)
    totals[...] = jnp.zeros(totals.shape, jnp.float32)

    def scores(rows, same, p):
        lanes = slice(p * PAIR, (p + 1) * PAIR)
        keys = k_ref[rows, lanes]
        found = []
        for query in split_heads(q_ref[:, lanes]):
            s = lax.dot_general(keys, query, NT, preferred_element_type=jnp.float32)
            found.append(jnp.where(same, s, NEGATIVE))
        return found

    def place_of(j):
        place = lax.rem(j + blocks - shift, blocks)
        rows = pl.ds(pl.multiple_of(place * size, size), size)
        return rows, col_ref[rows, :] == own

    def highest(j, unused):
        rows, same = place_of(j)
        for p in range(pairs):
            for h, s in enumerate(scores(rows, same, p)):
                at = slice(2 * p + h, 2 * p + h + 1)
                tops[at, :] = jnp.maximum(tops[at, :], jnp.max(s, axis=0, keepdims=True))
        return unused

    def step(j, unused):
        rows, same = place_of(j)
        for p in range(pairs):
            lanes = slice(p * PAIR, (p + 1) * PAIR)
            shares = []
            for h, s in enumerate(scores(rows, same, p)):
                at = slice(2 * p + h, 2 * p + h + 1)
                weights = jnp.exp2(s - tops[at, :])
                sums[at, :] += jnp.sum(weights, axis=0, keepdims=True)
                shares.append(weights.astype(jnp.bfloat16))
            totals[:, lanes] += lax.dot_general(
                jnp.concatenate(shares, axis=0),
                jnp.concatenate(split_heads(v_ref[rows, lanes]), axis=0),
                TN,
                preferred_element_type=jnp.float32,
            )
        return unused

    lax.fori_loop(low, high, highest, 0)
    lax.fori_loop(low, high, step, 0)
    picks = (
        lax.broadcasted_iota(jnp.int32, (heads, width), 1) // HEAD_DIM
        == lax.broadcasted_iota(jnp.int32, (heads, width), 0)
    ).astype(jnp.float32)
    scale = lax.dot_general(
        1.0 / sums[...],
        picks,
        TN,
        preferred_element_type=jnp.float32,
        precision=lax.Precision.HIGHEST,
    )
    ctx_ref[...] = (totals[...] * scale).astype(jnp.bfloat16)
    logs = tops[...] + jnp.log(sums[...]) * LOG2_E
    for group in range(groups):
        lse_ref[group] = logs[group * group_heads : (group + 1) * group_heads, :]


def group_width(width):
    return tile(width, 2 * PAIR)


def attend(joined, ranges, columns, rows_of, blocks, tokens=()):
    unused, total, width = joined.shape
    size = total // blocks
    heads = width // HEAD_DIM
    group_heads = group_width(width) // HEAD_DIM
    groups = heads // group_heads
    grid_spec = pltpu.PrefetchScalarGridSpec(
        num_scalar_prefetch=1,
        grid=(blocks,),
        in_specs=[
            pl.BlockSpec((None, size, width), lambda i, r: (0, i, 0)),
            pl.BlockSpec((None, total, width), lambda i, r: (1, 0, 0)),
            pl.BlockSpec((None, total, width), lambda i, r: (2, 0, 0)),
            pl.BlockSpec((total, 1), lambda i, r: (0, 0)),
            pl.BlockSpec((blocks, 1, size), lambda i, r: (0, 0, 0)),
        ]
        + [pl.BlockSpec(memory_space=pl.ANY)] * len(tokens),
        out_specs=[
            pl.BlockSpec((size, width), lambda i, r: (i, 0)),
            pl.BlockSpec((groups, None, group_heads, size), lambda i, r: (0, i, 0, 0)),
        ],
        scratch_shapes=[
            pltpu.VMEM((heads, size), jnp.float32),
            pltpu.VMEM((heads, size), jnp.float32),
            pltpu.VMEM((size, width), jnp.float32),
        ],
    )
    return pl.pallas_call(
        after(functools.partial(attend_kernel, blocks), 6, tokens),
        grid_spec=grid_spec,
        out_shape=[
            jax.ShapeDtypeStruct((total, width), jnp.bfloat16),
            jax.ShapeDtypeStruct((groups, blocks, group_heads, size), jnp.float32),
        ],
        compiler_params=params(40),
        cost_estimate=LIGHT,
    )(ranges, joined, joined, joined, columns, rows_of, *tokens)


def attend_back_kernel(
    blocks,
    ranges,
    q_ref,
    k_ref,
    v_ref,
    g_ref,
    ctx_ref,
    lse_ref,
    col_ref,
    row_ref,
    out_ref,
    sums_ref,
    dq_ref,
    dk_ref,
    dv_ref,
    delta_ref,
):
    total, width = q_ref.shape
    size = total // blocks
    pairs = width // PAIR
    chunks, unused, own_rows, unused = out_ref.shape
    shift = ranges[0]
    picks = (
        lax.broadcasted_iota(jnp.int32, (8, width), 1) // HEAD_DIM
        == lax.broadcasted_iota(jnp.int32, (8, width), 0)
    ).astype(jnp.float32)

    def prepare(i, unused):
        rows = pl.ds(pl.multiple_of(i * size, size), size)
        product = g_ref[rows, :].astype(jnp.float32) * ctx_ref[rows, :].astype(jnp.float32)
        delta_ref[i] = lax.dot_general(
            picks,
            product,
            NT,
            preferred_element_type=jnp.float32,
            precision=lax.Precision.HIGHEST,
        )
        dq_ref[rows, :] = jnp.zeros((size, width), jnp.float32)
        return unused

    sums_ref[...] = jnp.zeros(sums_ref.shape, jnp.float32)
    lax.fori_loop(0, blocks, prepare, 0)

    def key_block(i, unused):
        rows = pl.ds(pl.multiple_of(i * size, size), size)
        own = col_ref[rows, :]
        dk_ref[...] = jnp.zeros((size, width), jnp.float32)
        dv_ref[...] = jnp.zeros((size, width), jnp.float32)

        def step(j, unused):
            place = lax.rem(j + blocks - shift, blocks)
            there = pl.ds(pl.multiple_of(place * size, size), size)
            same = own == row_ref[place]
            for pair in range(pairs):
                lanes = slice(pair * PAIR, (pair + 1) * PAIR)
                query = q_ref[there, lanes]
                grad = g_ref[there, lanes]
                keys = split_heads(k_ref[rows, lanes])
                values = split_heads(v_ref[rows, lanes])
                shares, slopes = [], []
                for h in range(2):
                    at = 2 * pair + h
                    s = lax.dot_general(
                        keys[h], query, NT, preferred_element_type=jnp.float32
                    )
                    s = jnp.where(same, s, NEGATIVE)
                    p = jnp.exp2(s - lse_ref[place, at : at + 1, :])
                    dp = lax.dot_general(
                        values[h], grad, NT, preferred_element_type=jnp.float32
                    )
                    shares.append(p.astype(jnp.bfloat16))
                    slopes.append(
                        (p * (dp - delta_ref[place, at : at + 1, :])).astype(jnp.bfloat16)
                    )
                dv_ref[:, lanes] += jnp.dot(
                    jnp.concatenate(shares, axis=1),
                    jnp.concatenate(split_heads(grad), axis=0),
                    preferred_element_type=jnp.float32,
                )
                dk_ref[:, lanes] += jnp.dot(
                    jnp.concatenate(slopes, axis=1),
                    jnp.concatenate(split_heads(query), axis=0),
                    preferred_element_type=jnp.float32,
                )
                dq_ref[there, lanes] += lax.dot_general(
                    jnp.concatenate(slopes, axis=0),
                    jnp.concatenate(keys, axis=0),
                    TN,
                    preferred_element_type=jnp.float32,
                )
            return unused

        lax.fori_loop(ranges[1 + 2 * i], ranges[2 + 2 * i], step, 0)
        per_chunk = own_rows // size
        chunk = lax.div(i, per_chunk)
        spot = pl.ds(pl.multiple_of(lax.rem(i, per_chunk) * size, size), size)
        out_ref[chunk, 1, spot, :] = (dk_ref[...] * LN_2).astype(jnp.bfloat16)
        out_ref[chunk, 2, spot, :] = dv_ref[...].astype(jnp.bfloat16)
        sums_ref[1:2, :] += jnp.sum(dv_ref[...], axis=0, keepdims=True)
        return unused

    lax.fori_loop(0, blocks, key_block, 0)
    for chunk in range(chunks):
        dq = dq_ref[pl.ds(chunk * own_rows, own_rows), :] * HEAD_DIM ** (-0.5)
        sums_ref[0:1, :] += jnp.sum(dq, axis=0, keepdims=True)
        out_ref[chunk, 0] = dq.astype(jnp.bfloat16)


def attend_back(
    joined, grad, context, lse, ranges, columns, rows_of, blocks, ways, tokens=()
):
    unused, total, width = joined.shape
    size = total // blocks
    wide = group_width(width)
    rows = total // ways
    whole = pl.BlockSpec((total, wide), lambda p, r: (0, p))
    grid_spec = pltpu.PrefetchScalarGridSpec(
        num_scalar_prefetch=1,
        grid=(width // wide,),
        in_specs=[
            pl.BlockSpec((None, total, wide), lambda p, r: (0, 0, p)),
            pl.BlockSpec((None, total, wide), lambda p, r: (1, 0, p)),
            pl.BlockSpec((None, total, wide), lambda p, r: (2, 0, p)),
            whole,
            whole,
            pl.BlockSpec((None,) + lse.shape[1:], lambda p, r: (p, 0, 0, 0)),
            pl.BlockSpec((total, 1), lambda p, r: (0, 0)),
            pl.BlockSpec((blocks, 1, size), lambda p, r: (0, 0, 0)),
        ]
        + [pl.BlockSpec(memory_space=pl.ANY)] * len(tokens),
        out_specs=[
            pl.BlockSpec((ways, 3, rows, wide), lambda p, r: (0, 0, 0, p)),
            pl.BlockSpec((8, wide), lambda p, r: (0, p)),
        ],
        scratch_shapes=[
            pltpu.VMEM((total, wide), jnp.float32),
            pltpu.VMEM((size, wide), jnp.float32),
            pltpu.VMEM((size, wide), jnp.float32),
            pltpu.VMEM((blocks, 8, size), jnp.float32),
        ],
    )
    return pl.pallas_call(
        after(functools.partial(attend_back_kernel, blocks), 9, tokens),
        grid_spec=grid_spec,
        out_shape=[
            jax.ShapeDtypeStruct((ways, 3, rows, width), jnp.bfloat16),
            jax.ShapeDtypeStruct((8, width), jnp.float32),
        ],
        compiler_params=params(48),
        cost_estimate=LIGHT,
    )(ranges, joined, joined, joined, grad, context, lse, columns, rows_of, *tokens)


class Layout:
    def __init__(self, dp, tensor):
        self.dp, self.tensor = dp, tensor
        self.paired = tensor == 2 and dp % 2 == 0 and LAYERS == 2
        self.ways = tensor

    def index(self):
        if self.paired:
            return lax.rem(lax.axis_index("dp"), 2)
        return lax.axis_index("tensor")

    def permute(self, values, target):
        pairs = []
        for place in range(self.dp * self.tensor):
            there = target(*divmod(place, self.tensor))
            if there != place:
                pairs.append((place, there))
        return lax.ppermute(values, ("dp", "tensor"), pairs)

    def stays(self):
        return lax.rem(lax.axis_index("dp"), 2) == lax.axis_index("tensor")

    def exchanged(self, values):
        return self.permute(values, lambda dp, tensor: (dp // 2 * 2 + tensor) * 2 + dp % 2)

    def swap(self, values):
        if not self.paired:
            return values
        return jnp.where(self.stays(), values, self.exchanged(values))

    def moved(self):
        return jnp.where(self.stays(), 0, 1).astype(jnp.int32).reshape(1)

    def across(self, values, bit):
        return self.permute(values, lambda dp, tensor: (dp ^ 2 * bit) * 2 + tensor)

    def chip_sum(self, mine, turn, tokens=()):
        chips = self.dp // 2
        bits = [1 << n for n in range(chips.bit_length() - 1)]
        if 1 << len(bits) != chips:
            return lax.psum(mine, "dp", axis_index_groups=self.groups())
        bits = bits[turn:] + bits[:turn]
        chip = lax.axis_index("dp") // 2
        for bit in bits:
            place = chip // bit % 2
            half = mine.shape[0] // 2
            given = self.across(
                lax.dynamic_slice_in_dim(mine, (1 - place) * half, half, 0), bit
            )
            mine = fold(mine, given, place, tokens if bit == bits[-1] else ())
        for bit in reversed(bits):
            given = self.across(mine, bit)
            mine = jnp.where(
                chip // bit % 2 == 0,
                jnp.concatenate([mine, given]),
                jnp.concatenate([given, mine]),
            )
        return mine

    def shift(self, values, step):
        if self.paired:
            return self.permute(values, lambda dp, tensor: (dp // 2 * 2 + (dp + step) % 2) * 2 + tensor)
        return self.permute(
            values, lambda dp, tensor: dp * self.tensor + (tensor + step) % self.tensor
        )

    def gather(self, values):
        return [values] + [self.shift(values, -step) for step in range(1, self.ways)]

    def send_home(self, buffer):
        return self.exchanged(buffer) if self.paired else None

    def combine(self, buffer, other, tokens=()):
        core = self.index()
        halves, rows, width = buffer.shape
        high = rows // 8
        moved = self.moved()

        def half(which, tokens):
            def place(m, n, f):
                return f[1] * 8 + m, n

            return choose(
                jnp.concatenate([moved, which.reshape(1)]),
                buffer.reshape(-1, width),
                place,
                other.reshape(-1, width),
                place,
                (rows, width),
                (high, width),
                tokens,
            )

        given = self.shift(half(1 - core, tokens), 1)
        return fold(half(core, tokens), given, core * 0)

    def groups(self):
        return [[2 * chip + at for chip in range(self.dp // 2)] for at in range(2)]

    def chip_scatter(self, mine):
        return lax.psum_scatter(
            mine, "dp", scatter_dimension=0, axis_index_groups=self.groups(), tiled=True
        )

    def chip_gather(self, part):
        return lax.all_gather(part, "dp", axis=0, axis_index_groups=self.groups(), tiled=True)

    def finish(self, mine):
        return mine, self.shift(mine, 1), self.index().reshape(1)

    def scatter(self, part):
        return [self.shift(part(k), k) for k in range(1, self.ways)]


def per_device(
    layout,
    frames,
    logit_grad,
    lengths,
    ln_gain,
    ln_bias,
    w_qkv,
    b_qv,
    w_out,
    b_out,
    w_up,
    b_up,
    w_down,
    b_down,
    w_head,
    b_head,
):
    ways = layout.ways
    rows, features = frames.shape
    total = rows * ways
    size = min(256, rows)
    blocks = total // size
    chunk_blocks = rows // size
    part = layout.index()
    swap = layout.swap

    low = frames.astype(jnp.bfloat16)
    came_frames = layout.exchanged(low) if layout.paired else low
    if layout.paired:
        low = jnp.where(layout.stays(), low, came_frames)
    stream = low.astype(jnp.float32)
    small = jnp.concatenate(
        [
            b_qv.reshape(-1),
            b_up.reshape(-1),
            w_head.reshape(-1),
            logit_grad.astype(jnp.bfloat16).reshape(-1),
        ]
    ).reshape(-1, 128)
    if layout.paired:
        came_small = layout.exchanged(small)
        small = jnp.where(layout.stays(), small, came_small)
    small = small.reshape(-1)
    came_lengths = layout.exchanged(lengths) if layout.paired else lengths
    if layout.paired:
        lengths = jnp.where(layout.stays(), lengths, came_lengths)
    at = [b_qv.size, b_up.size, w_head.size, logit_grad.size]
    at = [sum(at[:n]) for n in range(5)]
    qv_biases = small[at[0] : at[1]].reshape(b_qv.shape).astype(jnp.float32)
    up_biases = small[at[1] : at[2]].reshape(b_up.shape).astype(jnp.float32)
    head_part = small[at[2] : at[3]].reshape(w_head.shape)
    logit_grad = small[at[3] : at[4]].reshape(logit_grad.shape)
    head_parts = layout.gather(head_part)
    head_all = jnp.roll(jnp.concatenate(head_parts), part * w_head.shape[0], axis=0)

    wide = w_qkv.shape[3]
    inner_width = w_up.shape[2]
    paired = layout.paired
    moved = layout.moved() if paired else None
    came_ffn = []
    if paired:
        own_qkv, own_out = w_qkv.reshape(-1, wide), w_out.reshape(-1, features)
        qkv_rows = 3 * features
        came_qkv = [layout.exchanged(w_qkv[0]).reshape(-1, wide)]
        came_out = [layout.exchanged(pick(own_out, 0, wide, (came_frames,)))]
        packs = [take(w_up, w_down, 0, (came_qkv[0], came_frames, came_small, came_lengths))]
        picked = packs[0]
        for layer in range(1, LAYERS):
            picked = pick(own_qkv, layer * qkv_rows, qkv_rows, (picked,))
            came_qkv.append(layout.exchanged(picked))
            picked = pick(own_out, layer * wide, wide, (picked,))
            came_out.append(layout.exchanged(picked))
    high = tile(wide, 512)

    def qkv_weight(layer):
        if not paired:
            return w_qkv[layer]
        blocks_in = 3 * features // high
        return choose(
            moved,
            w_qkv.reshape(-1, wide),
            lambda m, n, f: (layer * blocks_in + m, n),
            came_qkv[layer],
            lambda m, n, f: (m, n),
            (3 * features, wide),
            (high, wide),
        ).reshape(3, features, wide)

    def out_weight(layer, tokens):
        if not paired:
            return w_out[layer]
        return choose(
            moved,
            w_out.reshape(-1, features),
            lambda m, n, f: (layer * (wide // high) + m, n),
            came_out[layer],
            lambda m, n, f: (m, n),
            (wide, features),
            (high, features),
            tokens,
        )

    def up_weight(layer, tokens):
        if not paired:
            return w_up[layer]
        rows_in = features // high
        return choose(
            moved,
            w_up.reshape(-1, inner_width),
            lambda m, n, f: (layer * rows_in + m, n),
            came_ffn[layer],
            lambda m, n, f: (n * rows_in + m, 0),
            (features, inner_width),
            (high, features),
            tokens,
        )

    def down_weight(layer, tokens):
        if not paired:
            return w_down[layer]
        rows_in = inner_width // high
        return choose(
            moved,
            w_down.reshape(-1, features),
            lambda m, n, f: (layer * rows_in + m, n),
            came_ffn[layer],
            lambda m, n, f: (rows_in + m, n),
            (inner_width, features),
            (high, features),
            tokens,
        )

    qkv_weights, out_weights, up_weights, down_weights = [], [], [], []
    positions = lax.rem(jnp.arange(total, dtype=jnp.int32) + part * rows, total)
    ends = jnp.cumsum(lengths[0])
    segment = jnp.sum((positions[:, None] >= ends[None, :]).astype(jnp.int32), axis=1)
    own_valid = positions[:rows] < ends[-1]
    columns = segment[:, None]
    rows_of = segment.reshape(blocks, 1, size)
    firsts = positions.reshape(blocks, size)[:, :1]
    lows = jnp.max(jnp.where(ends[None, :] <= firsts, ends[None, :], 0), axis=1) // size
    lasts = firsts + (size - 1)
    highs = jnp.min(jnp.where(ends[None, :] > lasts, ends[None, :], total), axis=1)
    highs = (highs + size - 1) // size
    ranges = jnp.concatenate(
        [(part * chunk_blocks).reshape(1), jnp.stack([lows, highs], axis=1).reshape(-1)]
    ).astype(jnp.int32)
    gains = ln_gain.astype(jnp.float32)
    shifts = ln_bias.astype(jnp.float32)

    def chunk(values, k):
        return values[k * rows : (k + 1) * rows]

    saved = []
    normed = layer_norm(stream, gains[0, 0], shifts[0, 0]).astype(jnp.bfloat16)
    for layer in range(LAYERS):
        last = layer + 1 == LAYERS
        normed_all = layout.gather(normed)
        bias = jnp.stack(
            [qv_biases[layer, 0], jnp.zeros_like(qv_biases[layer, 0]), qv_biases[layer, 1]]
        )[:, None, :]
        qkv_weights.append(qkv_weight(layer))
        joined = None
        for k in range(ways):
            joined = project(normed_all[k], qkv_weights[layer], bias, k, ways, joined)
        context, lse = attend(
            joined, ranges, columns, rows_of, blocks
        )
        chunks = context.reshape(ways, rows, -1)
        if paired:
            came_ffn.append(layout.exchanged(packs[layer]))
        out_weights.append(out_weight(layer, (context,)))
        up_weights.append(up_weight(layer, (context,)))
        down_weights.append(down_weight(layer, (context,)))
        weight = out_weights[layer]
        received = layout.scatter(
            lambda k: times(chunks, (k,), weight, NN, tokens=(up_weights[layer],))
        )
        middle, normed_ffn = join(
            chunks,
            (0,),
            weight,
            stream,
            b_out[layer].astype(jnp.float32),
            gains[layer, 1],
            shifts[layer, 1],
            received,
        )
        ffn_all = layout.gather(normed_ffn)
        hidden, slopes = [], []
        for k in range(ways):
            one, other = gelu_up(ffn_all[k], up_weights[layer], up_biases[layer][None, :])
            hidden.append(one)
            slopes.append(other)
        if paired and not last:
            packs.append(take(w_up, w_down, layer + 1, (came_qkv[layer + 1],)))
        weight = down_weights[layer]
        received = layout.scatter(lambda k: times(hidden[k], (), weight, NN))
        saved.append(
            (stream, middle, normed_all, joined, context, lse, ffn_all, hidden, slopes)
        )
        following = (layer + 1) % LAYERS
        ended = join(
            hidden[0],
            (),
            weight,
            middle,
            b_down[layer].astype(jnp.float32),
            gains[following, 0],
            shifts[following, 0],
            received,
            last,
        )
        if last:
            final_low = ended[0]
        else:
            stream, normed = ended

    logits = swap((matmul(final_low, head_all) + b_head.astype(jnp.float32)))
    grad_logits = jnp.where(own_valid[:, None], logit_grad, 0.0).astype(jnp.bfloat16)
    head_grad = inner_rows(final_low, grad_logits)
    head_bias_grad = column_sums(grad_logits)
    grad_stream = outer_cols(grad_logits, head_all)

    tiles = features // wide
    inner_tiles = inner_width // wide
    ffn_shape = (2, features * inner_tiles + FFN_SMALL, wide)
    attn_shape = (2, 2 * features + ATTN_SMALL, wide)

    def shares(vectors):
        matrix = jnp.stack(vectors)

        def share(k):
            return lax.dynamic_slice_in_dim(matrix, lax.rem(part + k, ways) * wide, wide, 1)

        received = layout.scatter(lambda k: share(k).astype(jnp.bfloat16))
        return share(0) + sum(values.astype(jnp.float32) for values in received)

    def with_small(buffer, lines):
        lines = jnp.pad(lines, ((0, -lines.shape[0] % 16), (0, 0))).astype(jnp.bfloat16)
        first = buffer.shape[1] // features * features
        return lax.dynamic_update_slice(buffer, lines[None], (0, first, 0))

    head_lines = [
        head_grad.T,
        jnp.pad(head_bias_grad.reshape(ways, -1), ((0, 0), (0, wide - b_head.shape[0] // ways))).reshape(
            1, features
        ),
    ]
    low = grad_stream.astype(jnp.bfloat16)
    bias_down = column_sums(low)
    outputs = [None] * 4
    smalls = {}
    joined_rows = 3 * features
    every = range(ways)

    def unpack_ffn(layer, one, two, flag):
        smalls["ffn", layer] = (one, two, flag)
        outputs[0] = unpack(
            one, two, flag, 0, features, inner_tiles, layer, outputs[0], features, 0
        )
        outputs[1] = unpack(
            two, one, flag, 0, inner_width, tiles, layer, outputs[1], inner_width, 0
        )

    def unpack_attn(layer, one, two, flag):
        smalls["attn", layer] = (one, two, flag)
        outputs[2] = unpack(
            one, two, flag, 0, 2 * features, 1, layer, outputs[2], joined_rows, 0
        )
        outputs[2] = unpack(
            two, one, flag, 0, features, 1, layer, outputs[2], joined_rows, 2 * features
        )
        outputs[3] = unpack(
            two, one, flag, features, wide, tiles, layer, outputs[3], wide, 0
        )

    buffers = {}
    mines = {}
    for layer in reversed(range(LAYERS)):
        above = layer + 1
        top = above == LAYERS
        stream_in, middle, normed_all, joined, context, lse, ffn_all, hidden, slopes = saved[
            layer
        ]
        low_all = layout.gather(low)
        inner, inner_sums = [], []
        for k in every:
            tokens = ()
            if paired and not top:
                tokens = (mines["ffn", above],)
            one, other = inner_grad(low_all[k], down_weights[layer], slopes[k], tokens)
            inner.append(one)
            inner_sums.append(other)
        weight = up_weights[layer]
        received = layout.scatter(lambda k: times(inner[k], (), weight, NT))
        grad_middle, middle_low, norm_sums = norm_back(
            [(inner[0], ())], weight, middle, grad_stream, gains[layer, 1], received
        )
        bias_up = sum(inner_sums)
        bias_out = norm_sums[2]
        lines = [bias_down, norm_sums[0], norm_sums[1]]
        if top:
            lines += list(head_lines[0]) + list(head_lines[1])
        lines = jnp.concatenate([bias_up.reshape(inner_tiles, wide), shares(lines)])
        tokens = (lines,)
        if paired and not top:
            mines["attn", above] = layout.combine(*buffers["attn", above], (grad_middle,))
            scattered.append(layout.chip_scatter(mines["attn", above]))
            tokens += (mines["attn", above],)
        buffer = weight_grad(
            [(hidden[k], ()) for k in every],
            [(low_all[k], ()) for k in every],
            None,
            ffn_shape,
            lambda g, n: (1, n * inner_width),
            tokens,
        )
        buffer = weight_grad(
            [(ffn_all[k], ()) for k in every],
            [(inner[k], ()) for k in every],
            buffer,
            ffn_shape,
            lambda g, n: (0, n * features),
        )
        buffer = with_small(buffer, lines)
        buffers["ffn", layer] = (buffer, layout.send_home(buffer))

        low_all = layout.gather(middle_low)
        grad_context = None
        for k in every:
            grad_context = times(
                low_all[k], (), out_weights[layer], NT, k, ways, grad_context
            )
        grads, qkv_sums = attend_back(
            joined,
            grad_context,
            context,
            lse,
            ranges,
            columns,
            rows_of,
            blocks,
            ways,
            (buffer,),
        )
        buffer = weight_grad(
            [(context.reshape(ways, rows, -1), (k,)) for k in every],
            [(low_all[k], ()) for k in every],
            None,
            attn_shape,
            lambda g, n: (1, features + n * wide),
        )
        weight = qkv_weights[layer]
        received = layout.scatter(lambda k: times_kinds(grads, k, weight))
        grad_stream, low, norm_sums = norm_back(
            [(grads, (0, kind)) for kind in range(3)],
            weight,
            stream_in,
            grad_middle,
            gains[layer, 0],
            received,
        )
        tokens = ()
        if paired:
            mines["ffn", layer] = layout.combine(*buffers["ffn", layer], (grad_stream,))
            if top:
                scattered = [layout.chip_scatter(mines["ffn", layer])]
            else:
                tokens = (mines["ffn", layer], scattered[0])
        buffer = weight_grad(
            [(normed_all[k], ()) for k in every],
            [(grads, (k, None)) for k in every],
            buffer,
            attn_shape,
            lambda g, n: (g // 2, g % 2 * features),
            tokens,
        )
        norm_sums = pick(norm_sums, 0, norm_sums.shape[0], (buffer,))
        lines = jnp.concatenate([qkv_sums[:2], shares([bias_out, norm_sums[0], norm_sums[1]])])
        bias_down = norm_sums[2]
        buffer = with_small(buffer, lines)
        buffers["attn", layer] = (buffer, layout.send_home(buffer))

    if paired:
        unpack_ffn(LAYERS - 1, *layout.finish(layout.chip_gather(scattered[0])))
        ready = (outputs[0], outputs[1])
        unpack_attn(LAYERS - 1, *layout.finish(layout.chip_gather(scattered[1])))
        mine = mines["ffn", 0]
        half_rows = mine.shape[0] // 2
        halves = [
            layout.chip_sum(mine[n * half_rows : (n + 1) * half_rows], n, ready)
            for n in range(2)
        ]
        ready = (outputs[2], outputs[3])
        attn = layout.finish(
            layout.chip_sum(
                layout.combine(*buffers["attn", 0], (scattered[1],)), 0, ready
            )
        )
        unpack_ffn(0, *layout.finish(jnp.concatenate(halves)))
        unpack_attn(0, *attn)
    else:
        flag = jnp.zeros((1,), jnp.int32)
        for layer in reversed(range(LAYERS)):
            summed = lax.psum(buffers["ffn", layer][0], "dp")
            unpack_ffn(layer, summed[0], summed[1], flag)
            summed = lax.psum(buffers["attn", layer][0], "dp")
            unpack_attn(layer, summed[0], summed[1], flag)

    input_grad = swap(low).astype(jnp.float32)

    grad_qkv = outputs[2].reshape(LAYERS, 3, features, wide)

    def lines_of(kind, layer):
        one, two, flag = smalls[kind, layer]
        first = one.shape[0] // features * features
        return jnp.where(flag[0] == 0, one[first:], two[first:]).astype(jnp.float32)

    ffn_lines = [lines_of("ffn", layer) for layer in range(LAYERS)]
    attn_lines = [lines_of("attn", layer) for layer in range(LAYERS)]
    t = inner_tiles
    bias_up = jnp.stack([lines[:t].reshape(-1) for lines in ffn_lines])
    bias_down = jnp.stack([lines[t] for lines in ffn_lines])
    bias_qv = jnp.stack([lines[:2] for lines in attn_lines])
    bias_out = jnp.stack([lines[2] for lines in attn_lines])
    gain = jnp.stack(
        [jnp.stack([attn_lines[layer][3], ffn_lines[layer][t + 1]]) for layer in range(LAYERS)]
    )
    shift = jnp.stack(
        [jnp.stack([attn_lines[layer][4], ffn_lines[layer][t + 2]]) for layer in range(LAYERS)]
    )
    vocab = b_head.shape[0]
    head_weight = ffn_lines[-1][t + 3 : t + 3 + vocab].T
    head_bias = ffn_lines[-1][t + 3 + vocab, : vocab // ways]
    return (
        logits,
        input_grad,
        gain,
        shift,
        grad_qkv,
        bias_qv,
        outputs[3],
        bias_out,
        outputs[0],
        bias_up,
        outputs[1],
        bias_down,
        head_weight,
        head_bias,
    )


def solution(mesh):
    layout = Layout(mesh.shape["dp"], mesh.shape["tensor"])
    by_rows = P(("dp", "tensor"), None)
    placed = (
        by_rows,
        by_rows,
        P("dp", None),
        P(),
        P(),
        P(None, None, None, "tensor"),
        P(None, None, "tensor"),
        P(None, "tensor", None),
        P(),
        P(None, None, "tensor"),
        P(None, "tensor"),
        P(None, "tensor", None),
        P(),
        P("tensor", None),
        P(),
    )
    return jax.shard_map(
        functools.partial(per_device, layout),
        mesh=mesh,
        in_specs=placed,
        out_specs=(
            by_rows,
            by_rows,
            P(None, None, "tensor"),
            P(None, None, "tensor"),
            P(None, None, None, "tensor"),
            P(None, None, "tensor"),
            P(None, "tensor", None),
            P(None, "tensor"),
            P(None, None, "tensor"),
            P(None, "tensor"),
            P(None, "tensor", None),
            P(None, "tensor"),
            P("tensor", None),
            P("tensor"),
        ),
        check_vma=False,
    )
```

```python
import functools

import jax
import jax.numpy as jnp
from jax import lax
from jax.experimental import pallas as pl
from jax.experimental.pallas import tpu as pltpu
from jax.sharding import PartitionSpec as P

HEAD_DIM = 64
LAYERS = 2
EPSILON = 1e-05
PAIR = 2 * HEAD_DIM
NEGATIVE = -1e30
FFN_SMALL = 256
ATTN_SMALL = 128
LOG2_E = 1.4426950408889634
LN_2 = 0.6931471805599453
MIB = 1 << 20
NN = (((1,), (0,)), ((), ()))
NT = (((1,), (1,)), ((), ()))
TN = (((0,), (0,)), ((), ()))


def layer_norm(values, gain, shift):
    mean = jnp.mean(values, axis=-1, keepdims=True)
    centred = values - mean
    spread = jnp.mean(centred * centred, axis=-1, keepdims=True)
    return centred * lax.rsqrt(spread + EPSILON) * gain + shift


def matmul(left, right):
    return jnp.dot(left, right, preferred_element_type=jnp.float32)


def outer_cols(left, right):
    return lax.dot_general(left, right, NT, preferred_element_type=jnp.float32)


def inner_rows(left, right):
    return lax.dot_general(left, right, TN, preferred_element_type=jnp.float32)


def column_sums(values):
    return jnp.sum(values, axis=0, dtype=jnp.float32)


def tile(size, limit):
    return size if size <= limit else limit


LIGHT = pl.CostEstimate(flops=0, bytes_accessed=0, transcendentals=0)


def after(kernel, first, tokens):
    return lambda *refs: kernel(*refs[:first], *refs[first + len(tokens) :])


def params(mib):
    return pltpu.CompilerParams(vmem_limit_bytes=mib * MIB)


def project_kernel(x_ref, w_ref, b_ref, *rest):
    out_ref = rest[-1]
    gain = jnp.where(pl.program_id(0) == 0, HEAD_DIM ** (-0.5) * LOG2_E, 1.0)
    value = jnp.dot(x_ref[...], w_ref[...], preferred_element_type=jnp.float32)
    out_ref[...] = ((value + b_ref[...]) * gain).astype(jnp.bfloat16)


def project(x, weight, bias, chunk, ways, joined):
    rows, depth = x.shape
    kinds, unused, width = weight.shape
    wide = tile(width, 512)
    in_specs = [
        pl.BlockSpec((rows, depth), lambda k, n: (0, 0)),
        pl.BlockSpec((None, depth, wide), lambda k, n: (k, 0, n)),
        pl.BlockSpec((None, 1, wide), lambda k, n: (k, 0, n)),
    ]
    args = [x, weight, bias]
    aliases = {}
    if joined is not None:
        in_specs.append(pl.BlockSpec(memory_space=pl.ANY))
        args.append(joined)
        aliases = {3: 0}
    return pl.pallas_call(
        project_kernel,
        grid=(kinds, width // wide),
        in_specs=in_specs,
        out_specs=pl.BlockSpec((None, rows, wide), lambda k, n: (k, chunk, n)),
        out_shape=jax.ShapeDtypeStruct((kinds, rows * ways, width), jnp.bfloat16),
        input_output_aliases=aliases,
        compiler_params=params(32),
        cost_estimate=LIGHT,
    )(*args)


ERF_STEP = 0.3275911
ERF_TERMS = (0.254829592, -0.284496736, 1.421413741, -1.453152027, 1.061405429)


def gelu_kernel(sub, x_ref, w_ref, b_ref, hidden_ref, slope_ref):
    for start in range(0, x_ref.shape[0], sub):
        rows = pl.ds(start, sub)
        u = (
            jnp.dot(x_ref[rows, :], w_ref[...], preferred_element_type=jnp.float32)
            + b_ref[...]
        )
        density = jnp.exp(u * u * -0.5)
        t = 1.0 / (1.0 + (ERF_STEP * 0.5**0.5) * jnp.abs(u))
        poly = ERF_TERMS[4]
        for term in ERF_TERMS[3::-1]:
            poly = poly * t + term
        tail = (0.5 * poly) * t * density
        phi = jnp.where(u < 0.0, tail, 1.0 - tail)
        hidden_ref[rows, :] = (u * phi).astype(jnp.bfloat16)
        slope_ref[rows, :] = (phi + u * density * 0.3989422804014327).astype(jnp.bfloat16)


def gelu_up(x, weight, bias):
    rows, depth = x.shape
    width = weight.shape[1]
    wide = tile(width, 512)
    out = jax.ShapeDtypeStruct((rows, width), jnp.bfloat16)
    return pl.pallas_call(
        functools.partial(gelu_kernel, tile(rows, 256)),
        grid=(width // wide,),
        in_specs=[
            pl.BlockSpec((rows, depth), lambda n: (0, 0)),
            pl.BlockSpec((depth, wide), lambda n: (0, n)),
            pl.BlockSpec((1, wide), lambda n: (0, n)),
        ],
        out_specs=[pl.BlockSpec((rows, wide), lambda n: (0, n))] * 2,
        out_shape=[out, out],
        compiler_params=params(32),
        cost_estimate=LIGHT,
    )(x, weight, bias)


def times_kernel(dims, x_ref, w_ref, *rest):
    rest[-1][...] = lax.dot_general(
        x_ref[...], w_ref[...], dims, preferred_element_type=jnp.float32
    ).astype(jnp.bfloat16)


def row_spec(array, lead, high):
    return pl.BlockSpec(
        (None,) * len(lead) + (high, array.shape[-1]), lambda m: lead + (m, 0)
    )


def whole_spec(array):
    return pl.BlockSpec(array.shape, lambda m: (0,) * array.ndim)


def times(x, lead, weight, dims, chunk=0, chunks=1, buffer=None, tokens=()):
    rows = x.shape[-2]
    width = weight.shape[0] if dims == NT else weight.shape[1]
    high = tile(rows, 256)
    in_specs = [row_spec(x, lead, high), whole_spec(weight)]
    args = [x, weight]
    aliases = {}
    if buffer is not None:
        aliases = {2: 0}
        in_specs.append(pl.BlockSpec(memory_space=pl.ANY))
        args.append(buffer)
    in_specs += [pl.BlockSpec(memory_space=pl.ANY)] * len(tokens)
    args += tokens
    return pl.pallas_call(
        functools.partial(times_kernel, dims),
        grid=(rows // high,),
        in_specs=in_specs,
        out_specs=pl.BlockSpec((high, width), lambda m: (chunk * (rows // high) + m, 0)),
        out_shape=jax.ShapeDtypeStruct((rows * chunks, width), jnp.bfloat16),
        input_output_aliases=aliases,
        compiler_params=params(40),
        cost_estimate=LIGHT,
    )(*args)


def kinds_kernel(x_ref, w_ref, out_ref):
    total = lax.dot_general(x_ref[0], w_ref[0], NT, preferred_element_type=jnp.float32)
    for kind in range(1, w_ref.shape[0]):
        total += lax.dot_general(
            x_ref[kind], w_ref[kind], NT, preferred_element_type=jnp.float32
        )
    out_ref[...] = total.astype(jnp.bfloat16)


def times_kinds(x, chunk, weight):
    kinds, rows, width = x.shape[1:]
    features = weight.shape[1]
    high = tile(rows, 256)
    return pl.pallas_call(
        kinds_kernel,
        grid=(rows // high,),
        in_specs=[
            pl.BlockSpec((None, kinds, high, width), lambda m: (chunk, 0, m, 0)),
            whole_spec(weight),
        ],
        out_specs=pl.BlockSpec((high, features), lambda m: (m, 0)),
        out_shape=jax.ShapeDtypeStruct((rows, features), jnp.bfloat16),
        compiler_params=params(40),
        cost_estimate=LIGHT,
    )(x, weight)


def join_kernel(count, last, x_ref, w_ref, res_ref, bias_ref, gain_ref, shift_ref, *rest):
    received, outs = rest[:count], rest[count:]
    value = jnp.dot(x_ref[...], w_ref[...], preferred_element_type=jnp.float32)
    for ref in received:
        value += ref[...].astype(jnp.float32)
    value += res_ref[...] + bias_ref[...]
    if last:
        outs[0][...] = value.astype(jnp.bfloat16)
    else:
        outs[0][...] = value
        outs[1][...] = layer_norm(value, gain_ref[...], shift_ref[...]).astype(jnp.bfloat16)


def join(x, lead, weight, residual, bias, gain, shift, received, last=False):
    rows, features = residual.shape
    high = tile(rows, 256)
    block = pl.BlockSpec((high, features), lambda m: (m, 0))
    vector = pl.BlockSpec((1, features), lambda m: (0, 0))
    low = jax.ShapeDtypeStruct(residual.shape, jnp.bfloat16)
    full = jax.ShapeDtypeStruct(residual.shape, jnp.float32)
    return pl.pallas_call(
        functools.partial(join_kernel, len(received), last),
        grid=(rows // high,),
        in_specs=[row_spec(x, lead, high), whole_spec(weight), block, vector, vector, vector]
        + [block] * len(received),
        out_specs=[block] if last else [block, block],
        out_shape=[low] if last else [full, low],
        compiler_params=params(40),
        cost_estimate=LIGHT,
    )(x, weight, residual, bias[None], gain[None], shift[None], *received)


def inner_kernel(sub, d_ref, w_ref, slope_ref, out_ref, sums_ref):
    sums = jnp.zeros(sums_ref.shape, jnp.float32)
    for start in range(0, d_ref.shape[0], sub):
        rows = pl.ds(start, sub)
        value = lax.dot_general(
            d_ref[rows, :], w_ref[...], NT, preferred_element_type=jnp.float32
        )
        value = (value * slope_ref[rows, :].astype(jnp.float32)).astype(jnp.bfloat16)
        out_ref[rows, :] = value
        sums += jnp.sum(value.astype(jnp.float32), axis=0, keepdims=True)
    sums_ref[...] = sums


def inner_grad(d, weight, slope, tokens=()):
    rows, features = d.shape
    width = weight.shape[0]
    wide = tile(width, 512)
    column = pl.BlockSpec((rows, wide), lambda n: (0, n))
    return pl.pallas_call(
        after(functools.partial(inner_kernel, tile(rows, 256)), 3, tokens),
        grid=(width // wide,),
        in_specs=[
            pl.BlockSpec((rows, features), lambda n: (0, 0)),
            pl.BlockSpec((wide, features), lambda n: (n, 0)),
            column,
        ]
        + [pl.BlockSpec(memory_space=pl.ANY)] * len(tokens),
        out_specs=[column, pl.BlockSpec((1, wide), lambda n: (0, n))],
        out_shape=[
            jax.ShapeDtypeStruct((rows, width), jnp.bfloat16),
            jax.ShapeDtypeStruct((1, width), jnp.float32),
        ],
        compiler_params=params(40),
        cost_estimate=LIGHT,
    )(d, weight, slope, *tokens)


def back_kernel(kinds, count, *refs):
    xs, ws = refs[:kinds], refs[kinds]
    value_ref, grad_ref, gain_ref = refs[kinds + 1 : kinds + 4]
    received = refs[kinds + 4 : kinds + 4 + count]
    full_ref, low_ref, sums_ref = refs[kinds + 4 + count :]
    if kinds == 1:
        weights = [ws[...]]
    else:
        weights = [ws[k] for k in range(kinds)]
    given = lax.dot_general(xs[0][...], weights[0], NT, preferred_element_type=jnp.float32)
    for k in range(1, kinds):
        given += lax.dot_general(xs[k][...], weights[k], NT, preferred_element_type=jnp.float32)
    for ref in received:
        given += ref[...].astype(jnp.float32)
    values = value_ref[...]
    centred = values - jnp.mean(values, axis=-1, keepdims=True)
    scale = lax.rsqrt(jnp.mean(centred * centred, axis=-1, keepdims=True) + EPSILON)
    unit = centred * scale
    inward = given * gain_ref[...]
    mean = jnp.mean(inward, axis=-1, keepdims=True)
    along = jnp.mean(inward * unit, axis=-1, keepdims=True)
    full = grad_ref[...] + scale * (inward - mean - unit * along)
    low = full.astype(jnp.bfloat16)
    full_ref[...] = full
    low_ref[...] = low

    @pl.when(pl.program_id(0) == 0)
    def _():
        sums_ref[...] = jnp.zeros(sums_ref.shape, jnp.float32)

    sums_ref[0:1, :] += jnp.sum(given * unit, axis=0, keepdims=True)
    sums_ref[1:2, :] += jnp.sum(given, axis=0, keepdims=True)
    sums_ref[2:3, :] += jnp.sum(low.astype(jnp.float32), axis=0, keepdims=True)


def norm_back(xs, weight, values, grad, gain, received):
    rows, features = values.shape
    high = tile(rows, 256)
    block = pl.BlockSpec((high, features), lambda m: (m, 0))
    return pl.pallas_call(
        functools.partial(back_kernel, len(xs), len(received)),
        grid=(rows // high,),
        in_specs=[row_spec(x, lead, high) for x, lead in xs]
        + [whole_spec(weight), block, block, pl.BlockSpec((1, features), lambda m: (0, 0))]
        + [block] * len(received),
        out_specs=[block, block, pl.BlockSpec((8, features), lambda m: (0, 0))],
        out_shape=[
            jax.ShapeDtypeStruct(values.shape, jnp.float32),
            jax.ShapeDtypeStruct(values.shape, jnp.bfloat16),
            jax.ShapeDtypeStruct((8, features), jnp.float32),
        ],
        compiler_params=params(48),
        cost_estimate=LIGHT,
    )(*[x for x, unused in xs], weight, values, grad, gain[None], *received)


def weight_kernel(chunks, *refs):
    x_refs, d_refs = refs[:chunks], refs[chunks : 2 * chunks]
    out_ref, turned = refs[-2:]

    @pl.when((pl.program_id(1) == 0) & (pl.program_id(2) == 0))
    def _():
        for k in range(chunks):
            turned[k] = x_refs[k][...].T

    total = jnp.dot(turned[0], d_refs[0][...], preferred_element_type=jnp.float32)
    for k in range(1, chunks):
        total += jnp.dot(turned[k], d_refs[k][...], preferred_element_type=jnp.float32)
    out_ref[...] = total.astype(jnp.bfloat16)


def weight_grad(xs, ds, buffer, shape, place, tokens=()):
    chunks = len(xs)
    rows, tall = xs[0][0].shape[-2:]
    width = ds[0][0].shape[-1]
    kinds = 1
    if None in ds[0][1]:
        kinds = ds[0][0].shape[ds[0][1].index(None)]
    high, wide = tile(tall, 512), shape[2]

    def x_spec(lead):
        return pl.BlockSpec(
            (None,) * len(lead) + (rows, high), lambda m, g, n: lead + (0, m)
        )

    def d_spec(lead):
        return pl.BlockSpec(
            (None,) * len(lead) + (rows, wide),
            lambda m, g, n: tuple(g if at is None else at for at in lead) + (0, n),
        )

    def out_index(m, g, n):
        half, row = place(g, n)
        return half, row // high + m, 0

    in_specs = [x_spec(lead) for unused, lead in xs] + [d_spec(lead) for unused, lead in ds]
    args = [array for array, unused in xs] + [array for array, unused in ds]
    aliases = {}
    if buffer is not None:
        aliases = {len(args): 0}
        in_specs.append(pl.BlockSpec(memory_space=pl.ANY))
        args.append(buffer)
    in_specs += [pl.BlockSpec(memory_space=pl.ANY)] * len(tokens)
    args += tokens
    return pl.pallas_call(
        functools.partial(weight_kernel, chunks),
        grid=(tall // high, kinds, width // wide),
        in_specs=in_specs,
        out_specs=pl.BlockSpec((None, high, wide), out_index),
        out_shape=jax.ShapeDtypeStruct(shape, jnp.bfloat16),
        scratch_shapes=[pltpu.VMEM((chunks, high, rows), jnp.bfloat16)],
        input_output_aliases=aliases,
        compiler_params=params(40),
        cost_estimate=LIGHT,
    )(*args)


def choose_kernel(flag, own_ref, other_ref, out_ref):
    out_ref[...] = jnp.where(flag[0] == 0, own_ref[...], other_ref[...])


def choose(flag, own, own_place, other, other_place, shape, block, tokens=()):
    def spec(which, place):
        def index(m, n, f):
            here = jnp.where(f[0] == which, 1, 0)
            row, column = place(m, n, f)
            return here * row, here * column

        return pl.BlockSpec(block, index)

    return pl.pallas_call(
        after(choose_kernel, 3, tokens),
        grid_spec=pltpu.PrefetchScalarGridSpec(
            num_scalar_prefetch=1,
            grid=(shape[0] // block[0], shape[1] // block[1]),
            in_specs=[spec(0, own_place), spec(1, other_place)]
            + [pl.BlockSpec(memory_space=pl.ANY)] * len(tokens),
            out_specs=pl.BlockSpec(block, lambda m, n, f: (m, n)),
        ),
        out_shape=jax.ShapeDtypeStruct(shape, jnp.bfloat16),
        compiler_params=params(32),
        cost_estimate=LIGHT,
    )(flag, own, other, *tokens)


def copy_kernel(in_ref, out_ref):
    out_ref[...] = in_ref[...]


def pick(values, first, rows, tokens):
    width = values.shape[1]
    high = rows if rows % 512 else 512
    return pl.pallas_call(
        after(copy_kernel, 1, tokens),
        grid=(rows // high,),
        in_specs=[pl.BlockSpec((high, width), lambda m: (first // high + m, 0))]
        + [pl.BlockSpec(memory_space=pl.ANY)] * len(tokens),
        out_specs=pl.BlockSpec((high, width), lambda m: (m, 0)),
        out_shape=jax.ShapeDtypeStruct((rows, width), values.dtype),
        compiler_params=params(16),
        cost_estimate=LIGHT,
    )(values, *tokens)


def take_kernel(count, up_ref, down_ref, out_ref):
    out_ref[...] = jnp.where(pl.program_id(0) < count, up_ref[...], down_ref[...])


def take(w_up, w_down, layer, tokens=()):
    features, inner = w_up.shape[1:]
    high = tile(features, 512)
    rows, down = features // high, inner // high
    ups = rows * (inner // features)

    def up_index(m):
        here = jnp.minimum(m, ups - 1)
        return layer, here % rows, here // rows

    return pl.pallas_call(
        after(functools.partial(take_kernel, ups), 2, tokens),
        grid=(ups + down,),
        in_specs=[
            pl.BlockSpec((None, high, features), up_index),
            pl.BlockSpec((None, high, features), lambda m: (layer, jnp.maximum(m - ups, 0), 0)),
        ]
        + [pl.BlockSpec(memory_space=pl.ANY)] * len(tokens),
        out_specs=pl.BlockSpec((high, features), lambda m: (m, 0)),
        out_shape=jax.ShapeDtypeStruct((2 * inner, features), jnp.bfloat16),
        compiler_params=params(32),
        cost_estimate=LIGHT,
    )(w_up, w_down, *tokens)


def fold_kernel(place, mine_ref, given_ref, out_ref):
    out_ref[...] = (
        mine_ref[...].astype(jnp.float32) + given_ref[...].astype(jnp.float32)
    ).astype(jnp.bfloat16)


def fold(mine, given, place, tokens=()):
    block = given.shape
    return pl.pallas_call(
        after(fold_kernel, 3, tokens),
        grid_spec=pltpu.PrefetchScalarGridSpec(
            num_scalar_prefetch=1,
            grid=(1,),
            in_specs=[
                pl.BlockSpec(block, lambda m, p: (p[0], 0)),
                pl.BlockSpec(block, lambda m, p: (0, 0)),
            ]
            + [pl.BlockSpec(memory_space=pl.ANY)] * len(tokens),
            out_specs=pl.BlockSpec(block, lambda m, p: (0, 0)),
        ),
        out_shape=jax.ShapeDtypeStruct(block, jnp.bfloat16),
        compiler_params=params(32),
        cost_estimate=LIGHT,
    )(place.astype(jnp.int32).reshape(1), mine, given, *tokens)


def unpack_kernel(flag, one_ref, two_ref, *rest):
    rest[-1][...] = jnp.where(flag[0] == 0, one_ref[...], two_ref[...]).astype(jnp.float32)


def unpack(one, two, flag, first, tall, tiles, layer, output, out_rows, out_first):
    wide = one.shape[1]
    high = tile(tall, 1024)
    skip = first // high

    def spec(which):
        def index(m, n, f):
            here = jnp.where(f[0] == which, 1, 0)
            return here * (skip + n * (tall // high) + m), 0

        return pl.BlockSpec((high, wide), index)

    args = [flag, one, two]
    in_specs = [spec(0), spec(1)]
    aliases = {}
    if output is not None:
        aliases = {3: 0}
        in_specs.append(pl.BlockSpec(memory_space=pl.ANY))
        args.append(output)
    return pl.pallas_call(
        unpack_kernel,
        grid_spec=pltpu.PrefetchScalarGridSpec(
            num_scalar_prefetch=1,
            grid=(tall // high, tiles),
            in_specs=in_specs,
            out_specs=pl.BlockSpec(
                (None, high, wide), lambda m, n, f: (layer, out_first // high + m, n)
            ),
        ),
        out_shape=jax.ShapeDtypeStruct((LAYERS, out_rows, tiles * wide), jnp.float32),
        input_output_aliases=aliases,
        compiler_params=params(32),
        cost_estimate=LIGHT,
    )(*args)


def head_lanes(shape):
    return lax.broadcasted_iota(jnp.int32, shape, 1) < HEAD_DIM


def split_heads(values):
    first = head_lanes(values.shape)
    zero = jnp.zeros_like(values)
    return jnp.where(first, values, zero), jnp.where(first, zero, values)


def attend_kernel(
    blocks, ranges, q_ref, k_ref, v_ref, col_ref, row_ref, ctx_ref, lse_ref, tops, sums, totals
):
    i = pl.program_id(0)
    size, width = q_ref.shape
    heads = width // HEAD_DIM
    pairs = width // PAIR
    groups, group_heads, unused = lse_ref.shape
    shift = ranges[0]
    low, high = ranges[1 + 2 * i], ranges[2 + 2 * i]
    own = row_ref[i]
    tops[...] = jnp.full(tops.shape, NEGATIVE, jnp.float32)
    sums[...] = jnp.zeros(sums.shape, jnp.float32)
    totals[...] = jnp.zeros(totals.shape, jnp.float32)

    def scores(rows, same, p):
        lanes = slice(p * PAIR, (p + 1) * PAIR)
        keys = k_ref[rows, lanes]
        found = []
        for query in split_heads(q_ref[:, lanes]):
            s = lax.dot_general(keys, query, NT, preferred_element_type=jnp.float32)
            found.append(jnp.where(same, s, NEGATIVE))
        return found

    def place_of(j):
        place = lax.rem(j + blocks - shift, blocks)
        rows = pl.ds(pl.multiple_of(place * size, size), size)
        return rows, col_ref[rows, :] == own

    def highest(j, unused):
        rows, same = place_of(j)
        for p in range(pairs):
            for h, s in enumerate(scores(rows, same, p)):
                at = slice(2 * p + h, 2 * p + h + 1)
                tops[at, :] = jnp.maximum(tops[at, :], jnp.max(s, axis=0, keepdims=True))
        return unused

    def step(j, unused):
        rows, same = place_of(j)
        for p in range(pairs):
            lanes = slice(p * PAIR, (p + 1) * PAIR)
            shares = []
            for h, s in enumerate(scores(rows, same, p)):
                at = slice(2 * p + h, 2 * p + h + 1)
                weights = jnp.exp2(s - tops[at, :])
                sums[at, :] += jnp.sum(weights, axis=0, keepdims=True)
                shares.append(weights.astype(jnp.bfloat16))
            totals[:, lanes] += lax.dot_general(
                jnp.concatenate(shares, axis=0),
                jnp.concatenate(split_heads(v_ref[rows, lanes]), axis=0),
                TN,
                preferred_element_type=jnp.float32,
            )
        return unused

    lax.fori_loop(low, high, highest, 0)
    lax.fori_loop(low, high, step, 0)
    picks = (
        lax.broadcasted_iota(jnp.int32, (heads, width), 1) // HEAD_DIM
        == lax.broadcasted_iota(jnp.int32, (heads, width), 0)
    ).astype(jnp.float32)
    scale = lax.dot_general(
        1.0 / sums[...],
        picks,
        TN,
        preferred_element_type=jnp.float32,
        precision=lax.Precision.HIGHEST,
    )
    ctx_ref[...] = (totals[...] * scale).astype(jnp.bfloat16)
    logs = tops[...] + jnp.log(sums[...]) * LOG2_E
    for group in range(groups):
        lse_ref[group] = logs[group * group_heads : (group + 1) * group_heads, :]


def group_width(width):
    return tile(width, 2 * PAIR)


def attend(joined, ranges, columns, rows_of, blocks, tokens=()):
    unused, total, width = joined.shape
    size = total // blocks
    heads = width // HEAD_DIM
    group_heads = group_width(width) // HEAD_DIM
    groups = heads // group_heads
    grid_spec = pltpu.PrefetchScalarGridSpec(
        num_scalar_prefetch=1,
        grid=(blocks,),
        in_specs=[
            pl.BlockSpec((None, size, width), lambda i, r: (0, i, 0)),
            pl.BlockSpec((None, total, width), lambda i, r: (1, 0, 0)),
            pl.BlockSpec((None, total, width), lambda i, r: (2, 0, 0)),
            pl.BlockSpec((total, 1), lambda i, r: (0, 0)),
            pl.BlockSpec((blocks, 1, size), lambda i, r: (0, 0, 0)),
        ]
        + [pl.BlockSpec(memory_space=pl.ANY)] * len(tokens),
        out_specs=[
            pl.BlockSpec((size, width), lambda i, r: (i, 0)),
            pl.BlockSpec((groups, None, group_heads, size), lambda i, r: (0, i, 0, 0)),
        ],
        scratch_shapes=[
            pltpu.VMEM((heads, size), jnp.float32),
            pltpu.VMEM((heads, size), jnp.float32),
            pltpu.VMEM((size, width), jnp.float32),
        ],
    )
    return pl.pallas_call(
        after(functools.partial(attend_kernel, blocks), 6, tokens),
        grid_spec=grid_spec,
        out_shape=[
            jax.ShapeDtypeStruct((total, width), jnp.bfloat16),
            jax.ShapeDtypeStruct((groups, blocks, group_heads, size), jnp.float32),
        ],
        compiler_params=params(40),
        cost_estimate=LIGHT,
    )(ranges, joined, joined, joined, columns, rows_of, *tokens)


def attend_back_kernel(
    blocks,
    ranges,
    q_ref,
    k_ref,
    v_ref,
    g_ref,
    ctx_ref,
    lse_ref,
    col_ref,
    row_ref,
    out_ref,
    sums_ref,
    dq_ref,
    dk_ref,
    dv_ref,
    delta_ref,
):
    total, width = q_ref.shape
    size = total // blocks
    pairs = width // PAIR
    chunks, unused, own_rows, unused = out_ref.shape
    shift = ranges[0]
    picks = (
        lax.broadcasted_iota(jnp.int32, (8, width), 1) // HEAD_DIM
        == lax.broadcasted_iota(jnp.int32, (8, width), 0)
    ).astype(jnp.float32)

    def prepare(i, unused):
        rows = pl.ds(pl.multiple_of(i * size, size), size)
        product = g_ref[rows, :].astype(jnp.float32) * ctx_ref[rows, :].astype(jnp.float32)
        delta_ref[i] = lax.dot_general(
            picks,
            product,
            NT,
            preferred_element_type=jnp.float32,
            precision=lax.Precision.HIGHEST,
        )
        dq_ref[rows, :] = jnp.zeros((size, width), jnp.float32)
        return unused

    sums_ref[...] = jnp.zeros(sums_ref.shape, jnp.float32)
    lax.fori_loop(0, blocks, prepare, 0)

    def key_block(i, unused):
        rows = pl.ds(pl.multiple_of(i * size, size), size)
        own = col_ref[rows, :]
        dk_ref[...] = jnp.zeros((size, width), jnp.float32)
        dv_ref[...] = jnp.zeros((size, width), jnp.float32)

        def step(j, unused):
            place = lax.rem(j + blocks - shift, blocks)
            there = pl.ds(pl.multiple_of(place * size, size), size)
            same = own == row_ref[place]
            for pair in range(pairs):
                lanes = slice(pair * PAIR, (pair + 1) * PAIR)
                query = q_ref[there, lanes]
                grad = g_ref[there, lanes]
                keys = split_heads(k_ref[rows, lanes])
                values = split_heads(v_ref[rows, lanes])
                shares, slopes = [], []
                for h in range(2):
                    at = 2 * pair + h
                    s = lax.dot_general(
                        keys[h], query, NT, preferred_element_type=jnp.float32
                    )
                    s = jnp.where(same, s, NEGATIVE)
                    p = jnp.exp2(s - lse_ref[place, at : at + 1, :])
                    dp = lax.dot_general(
                        values[h], grad, NT, preferred_element_type=jnp.float32
                    )
                    shares.append(p.astype(jnp.bfloat16))
                    slopes.append(
                        (p * (dp - delta_ref[place, at : at + 1, :])).astype(jnp.bfloat16)
                    )
                dv_ref[:, lanes] += jnp.dot(
                    jnp.concatenate(shares, axis=1),
                    jnp.concatenate(split_heads(grad), axis=0),
                    preferred_element_type=jnp.float32,
                )
                dk_ref[:, lanes] += jnp.dot(
                    jnp.concatenate(slopes, axis=1),
                    jnp.concatenate(split_heads(query), axis=0),
                    preferred_element_type=jnp.float32,
                )
                dq_ref[there, lanes] += lax.dot_general(
                    jnp.concatenate(slopes, axis=0),
                    jnp.concatenate(keys, axis=0),
                    TN,
                    preferred_element_type=jnp.float32,
                )
            return unused

        lax.fori_loop(ranges[1 + 2 * i], ranges[2 + 2 * i], step, 0)
        per_chunk = own_rows // size
        chunk = lax.div(i, per_chunk)
        spot = pl.ds(pl.multiple_of(lax.rem(i, per_chunk) * size, size), size)
        out_ref[chunk, 1, spot, :] = (dk_ref[...] * LN_2).astype(jnp.bfloat16)
        out_ref[chunk, 2, spot, :] = dv_ref[...].astype(jnp.bfloat16)
        sums_ref[1:2, :] += jnp.sum(dv_ref[...], axis=0, keepdims=True)
        return unused

    lax.fori_loop(0, blocks, key_block, 0)
    for chunk in range(chunks):
        dq = dq_ref[pl.ds(chunk * own_rows, own_rows), :] * HEAD_DIM ** (-0.5)
        sums_ref[0:1, :] += jnp.sum(dq, axis=0, keepdims=True)
        out_ref[chunk, 0] = dq.astype(jnp.bfloat16)


def attend_back(
    joined, grad, context, lse, ranges, columns, rows_of, blocks, ways, tokens=()
):
    unused, total, width = joined.shape
    size = total // blocks
    wide = group_width(width)
    rows = total // ways
    whole = pl.BlockSpec((total, wide), lambda p, r: (0, p))
    grid_spec = pltpu.PrefetchScalarGridSpec(
        num_scalar_prefetch=1,
        grid=(width // wide,),
        in_specs=[
            pl.BlockSpec((None, total, wide), lambda p, r: (0, 0, p)),
            pl.BlockSpec((None, total, wide), lambda p, r: (1, 0, p)),
            pl.BlockSpec((None, total, wide), lambda p, r: (2, 0, p)),
            whole,
            whole,
            pl.BlockSpec((None,) + lse.shape[1:], lambda p, r: (p, 0, 0, 0)),
            pl.BlockSpec((total, 1), lambda p, r: (0, 0)),
            pl.BlockSpec((blocks, 1, size), lambda p, r: (0, 0, 0)),
        ]
        + [pl.BlockSpec(memory_space=pl.ANY)] * len(tokens),
        out_specs=[
            pl.BlockSpec((ways, 3, rows, wide), lambda p, r: (0, 0, 0, p)),
            pl.BlockSpec((8, wide), lambda p, r: (0, p)),
        ],
        scratch_shapes=[
            pltpu.VMEM((total, wide), jnp.float32),
            pltpu.VMEM((size, wide), jnp.float32),
            pltpu.VMEM((size, wide), jnp.float32),
            pltpu.VMEM((blocks, 8, size), jnp.float32),
        ],
    )
    return pl.pallas_call(
        after(functools.partial(attend_back_kernel, blocks), 9, tokens),
        grid_spec=grid_spec,
        out_shape=[
            jax.ShapeDtypeStruct((ways, 3, rows, width), jnp.bfloat16),
            jax.ShapeDtypeStruct((8, width), jnp.float32),
        ],
        compiler_params=params(48),
        cost_estimate=LIGHT,
    )(ranges, joined, joined, joined, grad, context, lse, columns, rows_of, *tokens)


class Layout:
    def __init__(self, dp, tensor):
        self.dp, self.tensor = dp, tensor
        self.paired = tensor == 2 and dp % 2 == 0 and LAYERS == 2
        self.ways = tensor

    def index(self):
        if self.paired:
            return lax.rem(lax.axis_index("dp"), 2)
        return lax.axis_index("tensor")

    def permute(self, values, target):
        pairs = []
        for place in range(self.dp * self.tensor):
            there = target(*divmod(place, self.tensor))
            if there != place:
                pairs.append((place, there))
        return lax.ppermute(values, ("dp", "tensor"), pairs)

    def stays(self):
        return lax.rem(lax.axis_index("dp"), 2) == lax.axis_index("tensor")

    def exchanged(self, values):
        return self.permute(values, lambda dp, tensor: (dp // 2 * 2 + tensor) * 2 + dp % 2)

    def swap(self, values):
        if not self.paired:
            return values
        return jnp.where(self.stays(), values, self.exchanged(values))

    def moved(self):
        return jnp.where(self.stays(), 0, 1).astype(jnp.int32).reshape(1)

    def across(self, values, bit):
        return self.permute(values, lambda dp, tensor: (dp ^ 2 * bit) * 2 + tensor)

    def chip_sum(self, mine, turn, pins):
        chips = self.dp // 2
        bits = [1 << n for n in range(chips.bit_length() - 1)]
        if 1 << len(bits) != chips:
            mine = lax.psum(mine, "dp", axis_index_groups=self.groups())
            return mine, [mine] * 3
        folds = []
        bits = bits[turn:] + bits[:turn]
        chip = lax.axis_index("dp") // 2
        for bit in bits:
            place = chip // bit % 2
            half = mine.shape[0] // 2
            given = self.across(
                lax.dynamic_slice_in_dim(mine, (1 - place) * half, half, 0), bit
            )
            mine = fold(mine, given, place, pins[len(folds)] if len(folds) < len(pins) else ())
            folds.append(mine)
        for bit in reversed(bits):
            given = self.across(mine, bit)
            mine = jnp.where(
                chip // bit % 2 == 0,
                jnp.concatenate([mine, given]),
                jnp.concatenate([given, mine]),
            )
        return mine, folds

    def shift(self, values, step):
        if self.paired:
            return self.permute(values, lambda dp, tensor: (dp // 2 * 2 + (dp + step) % 2) * 2 + tensor)
        return self.permute(
            values, lambda dp, tensor: dp * self.tensor + (tensor + step) % self.tensor
        )

    def gather(self, values):
        return [values] + [self.shift(values, -step) for step in range(1, self.ways)]

    def send_home(self, buffer):
        return self.exchanged(buffer) if self.paired else None

    def combine(self, buffer, other, tokens=()):
        core = self.index()
        halves, rows, width = buffer.shape
        high = rows // 8
        moved = self.moved()

        def half(which, tokens):
            def place(m, n, f):
                return f[1] * 8 + m, n

            return choose(
                jnp.concatenate([moved, which.reshape(1)]),
                buffer.reshape(-1, width),
                place,
                other.reshape(-1, width),
                place,
                (rows, width),
                (high, width),
                tokens,
            )

        given = self.shift(half(1 - core, tokens), 1)
        return fold(half(core, tokens), given, core * 0)

    def groups(self):
        return [[2 * chip + at for chip in range(self.dp // 2)] for at in range(2)]

    def chip_scatter(self, mine):
        return lax.psum_scatter(
            mine, "dp", scatter_dimension=0, axis_index_groups=self.groups(), tiled=True
        )

    def chip_gather(self, part):
        return lax.all_gather(part, "dp", axis=0, axis_index_groups=self.groups(), tiled=True)

    def finish(self, mine):
        return mine, self.shift(mine, 1), self.index().reshape(1)

    def scatter(self, part):
        return [self.shift(part(k), k) for k in range(1, self.ways)]


def per_device(
    layout,
    frames,
    logit_grad,
    lengths,
    ln_gain,
    ln_bias,
    w_qkv,
    b_qv,
    w_out,
    b_out,
    w_up,
    b_up,
    w_down,
    b_down,
    w_head,
    b_head,
):
    ways = layout.ways
    rows, features = frames.shape
    total = rows * ways
    size = min(256, rows)
    blocks = total // size
    chunk_blocks = rows // size
    part = layout.index()
    swap = layout.swap

    low = frames.astype(jnp.bfloat16)
    came_frames = layout.exchanged(low) if layout.paired else low
    if layout.paired:
        low = jnp.where(layout.stays(), low, came_frames)
    stream = low.astype(jnp.float32)
    small = jnp.concatenate(
        [
            b_qv.reshape(-1),
            b_up.reshape(-1),
            w_head.reshape(-1),
            logit_grad.astype(jnp.bfloat16).reshape(-1),
        ]
    ).reshape(-1, 128)
    if layout.paired:
        came_small = layout.exchanged(small)
        small = jnp.where(layout.stays(), small, came_small)
    small = small.reshape(-1)
    came_lengths = layout.exchanged(lengths) if layout.paired else lengths
    if layout.paired:
        lengths = jnp.where(layout.stays(), lengths, came_lengths)
    at = [b_qv.size, b_up.size, w_head.size, logit_grad.size]
    at = [sum(at[:n]) for n in range(5)]
    qv_biases = small[at[0] : at[1]].reshape(b_qv.shape).astype(jnp.float32)
    up_biases = small[at[1] : at[2]].reshape(b_up.shape).astype(jnp.float32)
    head_part = small[at[2] : at[3]].reshape(w_head.shape)
    logit_grad = small[at[3] : at[4]].reshape(logit_grad.shape)
    head_parts = layout.gather(head_part)
    head_all = jnp.roll(jnp.concatenate(head_parts), part * w_head.shape[0], axis=0)

    wide = w_qkv.shape[3]
    inner_width = w_up.shape[2]
    paired = layout.paired
    moved = layout.moved() if paired else None
    came_ffn = []
    if paired:
        own_qkv, own_out = w_qkv.reshape(-1, wide), w_out.reshape(-1, features)
        qkv_rows = 3 * features
        came_qkv = [layout.exchanged(w_qkv[0]).reshape(-1, wide)]
        came_out = [layout.exchanged(pick(own_out, 0, wide, (came_frames,)))]
        packs = [take(w_up, w_down, 0, (came_out[0], came_qkv[0], came_small, came_lengths))]
        picked = packs[0]
        for layer in range(1, LAYERS):
            picked = pick(own_qkv, layer * qkv_rows, qkv_rows, (picked,))
            came_qkv.append(layout.exchanged(picked))
            picked = pick(own_out, layer * wide, wide, (picked,))
            came_out.append(layout.exchanged(picked))
    high = tile(wide, 512)

    def qkv_weight(layer):
        if not paired:
            return w_qkv[layer]
        blocks_in = 3 * features // high
        return choose(
            moved,
            w_qkv.reshape(-1, wide),
            lambda m, n, f: (layer * blocks_in + m, n),
            came_qkv[layer],
            lambda m, n, f: (m, n),
            (3 * features, wide),
            (high, wide),
        ).reshape(3, features, wide)

    def out_weight(layer, tokens):
        if not paired:
            return w_out[layer]
        return choose(
            moved,
            w_out.reshape(-1, features),
            lambda m, n, f: (layer * (wide // high) + m, n),
            came_out[layer],
            lambda m, n, f: (m, n),
            (wide, features),
            (high, features),
            tokens,
        )

    def up_weight(layer, tokens):
        if not paired:
            return w_up[layer]
        rows_in = features // high
        return choose(
            moved,
            w_up.reshape(-1, inner_width),
            lambda m, n, f: (layer * rows_in + m, n),
            came_ffn[layer],
            lambda m, n, f: (n * rows_in + m, 0),
            (features, inner_width),
            (high, features),
            tokens,
        )

    def down_weight(layer, tokens):
        if not paired:
            return w_down[layer]
        rows_in = inner_width // high
        return choose(
            moved,
            w_down.reshape(-1, features),
            lambda m, n, f: (layer * rows_in + m, n),
            came_ffn[layer],
            lambda m, n, f: (rows_in + m, n),
            (inner_width, features),
            (high, features),
            tokens,
        )

    qkv_weights, out_weights, up_weights, down_weights = [], [], [], []
    positions = lax.rem(jnp.arange(total, dtype=jnp.int32) + part * rows, total)
    ends = jnp.cumsum(lengths[0])
    segment = jnp.sum((positions[:, None] >= ends[None, :]).astype(jnp.int32), axis=1)
    own_valid = positions[:rows] < ends[-1]
    columns = segment[:, None]
    rows_of = segment.reshape(blocks, 1, size)
    firsts = positions.reshape(blocks, size)[:, :1]
    lows = jnp.max(jnp.where(ends[None, :] <= firsts, ends[None, :], 0), axis=1) // size
    lasts = firsts + (size - 1)
    highs = jnp.min(jnp.where(ends[None, :] > lasts, ends[None, :], total), axis=1)
    highs = (highs + size - 1) // size
    ranges = jnp.concatenate(
        [(part * chunk_blocks).reshape(1), jnp.stack([lows, highs], axis=1).reshape(-1)]
    ).astype(jnp.int32)
    gains = ln_gain.astype(jnp.float32)
    shifts = ln_bias.astype(jnp.float32)

    def chunk(values, k):
        return values[k * rows : (k + 1) * rows]

    saved = []
    normed = layer_norm(stream, gains[0, 0], shifts[0, 0]).astype(jnp.bfloat16)
    for layer in range(LAYERS):
        last = layer + 1 == LAYERS
        normed_all = layout.gather(normed)
        bias = jnp.stack(
            [qv_biases[layer, 0], jnp.zeros_like(qv_biases[layer, 0]), qv_biases[layer, 1]]
        )[:, None, :]
        qkv_weights.append(qkv_weight(layer))
        joined = None
        for k in range(ways):
            joined = project(normed_all[k], qkv_weights[layer], bias, k, ways, joined)
        context, lse = attend(
            joined, ranges, columns, rows_of, blocks
        )
        chunks = context.reshape(ways, rows, -1)
        if paired:
            came_ffn.append(layout.exchanged(packs[layer]))
        out_weights.append(out_weight(layer, (context,)))
        up_weights.append(up_weight(layer, (context,)))
        down_weights.append(down_weight(layer, (context,)))
        weight = out_weights[layer]
        received = layout.scatter(
            lambda k: times(chunks, (k,), weight, NN, tokens=(up_weights[layer],))
        )
        middle, normed_ffn = join(
            chunks,
            (0,),
            weight,
            stream,
            b_out[layer].astype(jnp.float32),
            gains[layer, 1],
            shifts[layer, 1],
            received,
        )
        ffn_all = layout.gather(normed_ffn)
        hidden, slopes = [], []
        for k in range(ways):
            one, other = gelu_up(ffn_all[k], up_weights[layer], up_biases[layer][None, :])
            hidden.append(one)
            slopes.append(other)
        if paired and not last:
            packs.append(take(w_up, w_down, layer + 1, (came_qkv[layer + 1],)))
        weight = down_weights[layer]
        received = layout.scatter(lambda k: times(hidden[k], (), weight, NN))
        saved.append(
            (stream, middle, normed_all, joined, context, lse, ffn_all, hidden, slopes)
        )
        following = (layer + 1) % LAYERS
        ended = join(
            hidden[0],
            (),
            weight,
            middle,
            b_down[layer].astype(jnp.float32),
            gains[following, 0],
            shifts[following, 0],
            received,
            last,
        )
        if last:
            final_low = ended[0]
        else:
            stream, normed = ended

    logits = swap((matmul(final_low, head_all) + b_head.astype(jnp.float32)))
    grad_logits = jnp.where(own_valid[:, None], logit_grad, 0.0).astype(jnp.bfloat16)
    head_grad = inner_rows(final_low, grad_logits)
    head_bias_grad = column_sums(grad_logits)
    grad_stream = outer_cols(grad_logits, head_all)

    tiles = features // wide
    inner_tiles = inner_width // wide
    ffn_shape = (2, features * inner_tiles + FFN_SMALL, wide)
    attn_shape = (2, 2 * features + ATTN_SMALL, wide)

    def shares(vectors):
        matrix = jnp.stack(vectors)

        def share(k):
            return lax.dynamic_slice_in_dim(matrix, lax.rem(part + k, ways) * wide, wide, 1)

        received = layout.scatter(lambda k: share(k).astype(jnp.bfloat16))
        return share(0) + sum(values.astype(jnp.float32) for values in received)

    def with_small(buffer, lines):
        lines = jnp.pad(lines, ((0, -lines.shape[0] % 16), (0, 0))).astype(jnp.bfloat16)
        first = buffer.shape[1] // features * features
        return lax.dynamic_update_slice(buffer, lines[None], (0, first, 0))

    head_lines = [
        head_grad.T,
        jnp.pad(head_bias_grad.reshape(ways, -1), ((0, 0), (0, wide - b_head.shape[0] // ways))).reshape(
            1, features
        ),
    ]
    low = grad_stream.astype(jnp.bfloat16)
    bias_down = column_sums(low)
    outputs = [None] * 4
    smalls = {}
    joined_rows = 3 * features
    every = range(ways)

    def unpack_ffn(layer, one, two, flag):
        smalls["ffn", layer] = (one, two, flag)
        outputs[0] = unpack(
            one, two, flag, 0, features, inner_tiles, layer, outputs[0], features, 0
        )
        outputs[1] = unpack(
            two, one, flag, 0, inner_width, tiles, layer, outputs[1], inner_width, 0
        )

    def unpack_attn(layer, one, two, flag):
        smalls["attn", layer] = (one, two, flag)
        outputs[2] = unpack(
            one, two, flag, 0, 2 * features, 1, layer, outputs[2], joined_rows, 0
        )
        outputs[2] = unpack(
            two, one, flag, 0, features, 1, layer, outputs[2], joined_rows, 2 * features
        )
        outputs[3] = unpack(
            two, one, flag, features, wide, tiles, layer, outputs[3], wide, 0
        )

    buffers = {}
    mines = {}
    for layer in reversed(range(LAYERS)):
        above = layer + 1
        top = above == LAYERS
        stream_in, middle, normed_all, joined, context, lse, ffn_all, hidden, slopes = saved[
            layer
        ]
        low_all = layout.gather(low)
        inner, inner_sums = [], []
        for k in every:
            tokens = ()
            if paired and not top:
                tokens = (mines["ffn", above],)
            one, other = inner_grad(low_all[k], down_weights[layer], slopes[k], tokens)
            inner.append(one)
            inner_sums.append(other)
        weight = up_weights[layer]
        received = layout.scatter(lambda k: times(inner[k], (), weight, NT))
        grad_middle, middle_low, norm_sums = norm_back(
            [(inner[0], ())], weight, middle, grad_stream, gains[layer, 1], received
        )
        bias_up = sum(inner_sums)
        bias_out = norm_sums[2]
        lines = [bias_down, norm_sums[0], norm_sums[1]]
        if top:
            lines += list(head_lines[0]) + list(head_lines[1])
        lines = jnp.concatenate([bias_up.reshape(inner_tiles, wide), shares(lines)])
        tokens = (lines,)
        if paired and not top:
            mines["attn", above] = layout.combine(*buffers["attn", above], (grad_middle,))
            scattered.append(layout.chip_scatter(mines["attn", above]))
            tokens += (mines["attn", above],)
        buffer = weight_grad(
            [(hidden[k], ()) for k in every],
            [(low_all[k], ()) for k in every],
            None,
            ffn_shape,
            lambda g, n: (1, n * inner_width),
            tokens,
        )
        buffer = weight_grad(
            [(ffn_all[k], ()) for k in every],
            [(inner[k], ()) for k in every],
            buffer,
            ffn_shape,
            lambda g, n: (0, n * features),
        )
        buffer = with_small(buffer, lines)
        buffers["ffn", layer] = (buffer, layout.send_home(buffer))

        low_all = layout.gather(middle_low)
        grad_context = None
        for k in every:
            grad_context = times(
                low_all[k], (), out_weights[layer], NT, k, ways, grad_context
            )
        grads, qkv_sums = attend_back(
            joined,
            grad_context,
            context,
            lse,
            ranges,
            columns,
            rows_of,
            blocks,
            ways,
            (buffer, scattered[0]) if paired and not top else (buffer,),
        )
        buffer = weight_grad(
            [(context.reshape(ways, rows, -1), (k,)) for k in every],
            [(low_all[k], ()) for k in every],
            None,
            attn_shape,
            lambda g, n: (1, features + n * wide),
        )
        weight = qkv_weights[layer]
        received = layout.scatter(lambda k: times_kinds(grads, k, weight))
        grad_stream, low, norm_sums = norm_back(
            [(grads, (0, kind)) for kind in range(3)],
            weight,
            stream_in,
            grad_middle,
            gains[layer, 0],
            received,
        )
        tokens = ()
        if paired:
            mines["ffn", layer] = layout.combine(*buffers["ffn", layer], (grad_stream,))
            if top:
                scattered = [layout.chip_scatter(mines["ffn", layer])]
            else:
                gathered = layout.chip_gather(scattered[0])
                tokens = (mines["ffn", layer], gathered)
        buffer = weight_grad(
            [(normed_all[k], ()) for k in every],
            [(grads, (k, None)) for k in every],
            buffer,
            attn_shape,
            lambda g, n: (g // 2, g % 2 * features),
            tokens,
        )
        norm_sums = pick(norm_sums, 0, norm_sums.shape[0], (buffer,))
        lines = jnp.concatenate([qkv_sums[:2], shares([bias_out, norm_sums[0], norm_sums[1]])])
        bias_down = norm_sums[2]
        buffer = with_small(buffer, lines)
        buffers["attn", layer] = (buffer, layout.send_home(buffer))

    if paired:
        unpack_ffn(LAYERS - 1, *layout.finish(gathered))
        ready = (outputs[0], outputs[1])
        unpack_attn(LAYERS - 1, *layout.finish(layout.chip_gather(scattered[1])))
        mine = layout.combine(*buffers["attn", 0])
        attn, folds = layout.chip_sum(mine, 0, ())
        folds = folds + folds
        pins = ((mine, scattered[1]), (folds[0],), (folds[1],) + ready)
        mine = mines["ffn", 0]
        half_rows = mine.shape[0] // 2
        halves = [
            layout.chip_sum(mine[n * half_rows : (n + 1) * half_rows], n, pins)[0]
            for n in range(2)
        ]
        unpack_ffn(0, *layout.finish(jnp.concatenate(halves)))
        unpack_attn(0, *layout.finish(attn))
    else:
        flag = jnp.zeros((1,), jnp.int32)
        for layer in reversed(range(LAYERS)):
            summed = lax.psum(buffers["ffn", layer][0], "dp")
            unpack_ffn(layer, summed[0], summed[1], flag)
            summed = lax.psum(buffers["attn", layer][0], "dp")
            unpack_attn(layer, summed[0], summed[1], flag)

    input_grad = swap(low).astype(jnp.float32)

    grad_qkv = outputs[2].reshape(LAYERS, 3, features, wide)

    def lines_of(kind, layer):
        one, two, flag = smalls[kind, layer]
        first = one.shape[0] // features * features
        return jnp.where(flag[0] == 0, one[first:], two[first:]).astype(jnp.float32)

    ffn_lines = [lines_of("ffn", layer) for layer in range(LAYERS)]
    attn_lines = [lines_of("attn", layer) for layer in range(LAYERS)]
    t = inner_tiles
    bias_up = jnp.stack([lines[:t].reshape(-1) for lines in ffn_lines])
    bias_down = jnp.stack([lines[t] for lines in ffn_lines])
    bias_qv = jnp.stack([lines[:2] for lines in attn_lines])
    bias_out = jnp.stack([lines[2] for lines in attn_lines])
    gain = jnp.stack(
        [jnp.stack([attn_lines[layer][3], ffn_lines[layer][t + 1]]) for layer in range(LAYERS)]
    )
    shift = jnp.stack(
        [jnp.stack([attn_lines[layer][4], ffn_lines[layer][t + 2]]) for layer in range(LAYERS)]
    )
    vocab = b_head.shape[0]
    head_weight = ffn_lines[-1][t + 3 : t + 3 + vocab].T
    head_bias = ffn_lines[-1][t + 3 + vocab, : vocab // ways]
    return (
        logits,
        input_grad,
        gain,
        shift,
        grad_qkv,
        bias_qv,
        outputs[3],
        bias_out,
        outputs[0],
        bias_up,
        outputs[1],
        bias_down,
        head_weight,
        head_bias,
    )


def solution(mesh):
    layout = Layout(mesh.shape["dp"], mesh.shape["tensor"])
    by_rows = P(("dp", "tensor"), None)
    placed = (
        by_rows,
        by_rows,
        P("dp", None),
        P(),
        P(),
        P(None, None, None, "tensor"),
        P(None, None, "tensor"),
        P(None, "tensor", None),
        P(),
        P(None, None, "tensor"),
        P(None, "tensor"),
        P(None, "tensor", None),
        P(),
        P("tensor", None),
        P(),
    )
    return jax.shard_map(
        functools.partial(per_device, layout),
        mesh=mesh,
        in_specs=placed,
        out_specs=(
            by_rows,
            by_rows,
            P(None, None, "tensor"),
            P(None, None, "tensor"),
            P(None, None, None, "tensor"),
            P(None, None, "tensor"),
            P(None, "tensor", None),
            P(None, "tensor"),
            P(None, None, "tensor"),
            P(None, "tensor"),
            P(None, "tensor", None),
            P(None, "tensor"),
            P("tensor", None),
            P("tensor"),
        ),
        check_vma=False,
    )
```
